128 devices in a mesh: lat: 4 (over y_hi, core), lon: 32 (over z, y_lo, x).
Axes of the slice: x: 4, y: 4 (y_hi: 2, y_lo: 2; y = y_hi * 2 + y_lo), z: 4, core: 2. Of those that a mesh axis runs over, the one named last changes fastest.
Arguments:
- tokens: bfloat16 [4, 24, 384, 512], P(None, 'lat', 'lon'), may hold values from -9 to 9
- region_ids: int32 [24, 384], P('lat', 'lon'), may hold values from 0 to 3
- shift_lat: int32 [4], replicated, may hold values from 1 to 5
- shift_lon: int32 [4], replicated, may hold values from 1 to 11
- gain_attn: float32 [512], replicated, may hold values from 0.25 to 1.75
- w_qkv: bfloat16 [512, 1536], replicated, may hold values from -1 to 1
- w_out: bfloat16 [512, 512], replicated, may hold values from -0.25 to 0.25
- gain_mlp: float32 [512], replicated, may hold values from 0.25 to 1.75
- w_up: bfloat16 [512, 2048], replicated, may hold values from -0.25 to 0.25
- w_down: bfloat16 [2048, 512], replicated, may hold values from -0.125 to 0.125
- cotangent: bfloat16 [4, 24, 384, 512], P(None, 'lat', 'lon'), may hold values from -6 to 6
Outputs:
- block_out: bfloat16 [4, 24, 384, 512], P(None, 'lat', 'lon')
- grad_tokens: bfloat16 [4, 24, 384, 512], P(None, 'lat', 'lon')
- grad_gain_attn: float32 [512], replicated
- grad_qkv: float32 [512, 1536], replicated
- grad_out: float32 [512, 512], replicated
- grad_gain_mlp: float32 [512], replicated
- grad_up: float32 [512, 2048], replicated
- grad_down: float32 [2048, 512], replicated
The draws below stay inside these ranges and needn't reach their ends.
Inputs may be any that keep to these rules, and one draw needn't show every extreme that they name: `region_ids`: a query attends only to keys of its window whose region number is equal to its own.
All inputs are finite; a program needn't handle non-finite values.
Results may differ from the reference program's by a relative error of at most 0.014.
The reference program's roundings to bfloat16 on the way count: a program that leaves them out, or rounds other values in their place, can miss the bound.
Values may be sent and summed in bfloat16 or wider, within the bound.
A program may use at most 192 MiB of HBM per device.

```python
import jax
import jax.numpy as jnp
from jax import lax

D = 512
HEADS = 8
FF = 2048
LEV = 4
WV = 2
WH = 6
WW = 12
NLAT = 24
NLON = 384


def draw_tokens(key, part):
    key = jax.random.fold_in(key, 3)
    jitter_key = jax.random.fold_in(key, 0)
    jitter = jax.random.truncated_normal(jitter_key, -6.0, 6.0, (LEV, NLAT, NLON, D), jnp.float32)
    return jitter.astype(jnp.bfloat16)


def draw_w_qkv(key, part):
    key = jax.random.fold_in(key, 5)
    base_key = jax.random.fold_in(key, 0)
    weights = jax.random.truncated_normal(base_key, -6.0, 6.0, (D, 3 * D), jnp.float32) * D ** (-0.5)
    return weights.astype(jnp.bfloat16)


def set_ends(entries, key, smallest, largest):
    dims = entries.shape
    index_at = [jax.random.randint(jax.random.fold_in(key, axis), (), 0, dims[axis]) for axis in range(len(dims))]
    entries = entries.at[tuple(index_at)].set(smallest)
    longest = dims.index(max(dims))
    index_at[longest] = (index_at[longest] + 1) % dims[longest]
    return entries.at[tuple(index_at)].set(largest)


def shard_levels(key, dims, pieces, low, largest):
    level, own = 1.0, jax.random.fold_in(key, 6)
    for position, parts in pieces:
        steps = jnp.exp(jax.random.uniform(jax.random.fold_in(own, position), (parts,), jnp.float32, low / len(pieces), largest / len(pieces)))
        level = level * jnp.repeat(steps, dims[position] // parts).reshape([-1 if axis == position else 1 for axis in range(len(dims))])
    return level


def bell_draw(stream_key, shape, deviation, most, pieces=(), dtype=jnp.bfloat16):
    factor_of = shard_levels(stream_key, shape, pieces, -0.22, 0.18) if pieces else 1.0
    result = jax.random.normal(stream_key, shape, jnp.float32) * deviation * factor_of
    return jnp.minimum(jnp.maximum(result, -most), most).astype(dtype)


def setup_inputs(seed: int = 0) -> dict:
    splits = jax.random.split(jax.random.key(seed), 12)
    tokens = draw_tokens(jax.random.fold_in(splits[11], 71), 0)
    region_ids = set_ends(jax.random.randint(splits[1], (NLAT, NLON), 0, 4), jax.random.fold_in(splits[1], 1), 0, 3).astype(jnp.int32)
    shift_lat = set_ends(jax.random.randint(splits[2], (LEV,), 1, WH), jax.random.fold_in(splits[2], 1), 1, WH - 1).astype(jnp.int32)
    shift_lon = set_ends(jax.random.randint(splits[3], (LEV,), 1, WW), jax.random.fold_in(splits[3], 1), 1, WW - 1).astype(jnp.int32)
    gain_attn = jnp.clip(1.0 + 0.15 * jax.random.normal(splits[4], (D,), jnp.float32), 0.25, 1.75)
    w_qkv = draw_w_qkv(jax.random.fold_in(splits[11], 71), 0)
    w_out = bell_draw(splits[6], (D, D), D ** -0.5, 0.25)
    gain_mlp = jnp.clip(1.0 + 0.15 * jax.random.normal(splits[7], (D,), jnp.float32), 0.25, 1.75)
    w_up = bell_draw(splits[8], (D, FF), D ** -0.5, 0.25)
    w_down = bell_draw(splits[9], (FF, D), FF ** -0.5, 0.125)
    cotangent = bell_draw(splits[10], (LEV, NLAT, NLON, D), 1.0, 6.0, ((1, 4), (2, 32)))
    return {"tokens": tokens, "region_ids": region_ids, "shift_lat": shift_lat, "shift_lon": shift_lon, "gain_attn": gain_attn, "w_qkv": w_qkv, "w_out": w_out, "gain_mlp": gain_mlp, "w_up": w_up, "w_down": w_down, "cotangent": cotangent}


EPS = 1e-05

def norm_stats(values):
    center = values - lax.optimization_barrier(jnp.mean(values, axis=-1, keepdims=True))
    inv_scale = lax.rsqrt(lax.optimization_barrier(jnp.mean(center * center, axis=-1, keepdims=True)) + EPS)
    return (center * inv_scale, inv_scale)

def norm_back(grad, normed, inv_scale, gain):
    gain_grad = lax.optimization_barrier(jnp.sum((grad * normed).reshape(-1, grad.shape[-1]), axis=0))
    graded = grad * gain
    term = inv_scale * (graded - lax.optimization_barrier(jnp.mean(graded, axis=-1, keepdims=True)) - normed * lax.optimization_barrier(jnp.mean(graded * normed, axis=-1, keepdims=True)))
    return (term, gain_grad)

def gelu_value(inner):
    return 0.5 * inner * (1.0 + lax.erf(inner * 0.7071067811865476))

def gelu_slope(inner):
    return 0.5 * (1.0 + lax.erf(inner * 0.7071067811865476)) + inner * jnp.exp(-0.5 * inner * inner) * 0.3989422804014327

def roll_levels(field, rows, cols):
    return jax.vmap(lambda plane, down, across: jnp.roll(plane, (down, across), axis=(0, 1)))(field, rows, cols)

def to_windows(field):
    levels, lat_rows, lon_cols, feats = field.shape
    field = field.reshape(levels // WV, WV, lat_rows // WH, WH, lon_cols // WW, WW, feats)
    return field.transpose(0, 2, 4, 1, 3, 5, 6).reshape(-1, WV * WH * WW, feats)

def from_windows(field, levels, lat_rows, lon_cols):
    feats = field.shape[-1]
    field = field.reshape(levels // WV, lat_rows // WH, lon_cols // WW, WV, WH, WW, feats)
    return field.transpose(0, 3, 1, 4, 2, 5, 6).reshape(levels, lat_rows, lon_cols, feats)

def split_heads(packed):
    count, win_tokens, triple = packed.shape
    model_width = triple // 3
    head_size = model_width // HEADS
    query = packed[..., :model_width].reshape(count, win_tokens, HEADS, head_size).astype(jnp.float32)
    keyset = packed[..., model_width:2 * model_width].reshape(count, win_tokens, HEADS, head_size).astype(jnp.float32)
    values = packed[..., 2 * model_width:].reshape(count, win_tokens, HEADS, head_size).astype(jnp.float32)
    return (query, keyset, values, head_size ** (-0.5))

def attend(packed, labels):
    query, keyset, values, factor = split_heads(packed)
    scores = jnp.einsum('wqhe,wkhe->whqk', query, keyset) * factor
    allowed = labels[:, None, :, None] == labels[:, None, None, :]
    scores = jnp.where(allowed, scores, -jnp.inf)
    peak = lax.optimization_barrier(jnp.max(scores, axis=-1, keepdims=True))
    expo = jnp.exp(scores - peak)
    probs = expo / lax.optimization_barrier(jnp.sum(expo, axis=-1, keepdims=True))
    weights = probs.astype(jnp.bfloat16)
    mixed = jnp.einsum('whqk,wkhe->wqhe', weights.astype(jnp.float32), values).astype(jnp.bfloat16)
    return (mixed.reshape(packed.shape[0], packed.shape[1], -1), probs, weights)

def attend_back(grad_mixed, packed, labels):
    query, keyset, values, factor = split_heads(packed)
    _, probs, weights = attend(packed, labels)
    count, win_tokens, model_width = grad_mixed.shape
    dgrad = grad_mixed.reshape(count, win_tokens, HEADS, -1).astype(jnp.float32)
    grad_probs = jnp.einsum('wqhe,wkhe->whqk', dgrad, values)
    grad_values = jnp.einsum('whqk,wqhe->wkhe', weights.astype(jnp.float32), dgrad)
    grad_scores = (probs * (grad_probs - lax.optimization_barrier(jnp.sum(grad_probs * probs, axis=-1, keepdims=True))) * factor).astype(jnp.bfloat16)
    grad_scores = grad_scores.astype(jnp.float32)
    grad_query = jnp.einsum('whqk,wkhe->wqhe', grad_scores, keyset)
    grad_keys = jnp.einsum('whqk,wqhe->wkhe', grad_scores, query)
    joined = jnp.concatenate([grad_query.reshape(count, win_tokens, model_width), grad_keys.reshape(count, win_tokens, model_width), grad_values.reshape(count, win_tokens, model_width)], axis=-1)
    return joined.astype(jnp.bfloat16)

def reference(tokens, region_ids, shift_lat, shift_lon, gain_attn, w_qkv, w_out, gain_mlp, w_up, w_down, cotangent):
    row_shift = shift_lat.astype(jnp.int32)
    col_shift = shift_lon.astype(jnp.int32)
    blocks = LEV // WV * (NLAT // WH)
    start_state = tokens.astype(jnp.float32)
    normed_a, scale_a = norm_stats(start_state)
    h_attn = (normed_a * gain_attn).astype(jnp.bfloat16)
    frame_h = roll_levels(h_attn, row_shift, col_shift)
    frame_ids = roll_levels(jnp.broadcast_to(region_ids[None, :, :], (LEV, NLAT, NLON)), row_shift, col_shift)
    labels = to_windows(frame_ids[..., None])[..., 0]
    flat_h = frame_h.reshape(-1, D)
    qkv = jnp.dot(flat_h, w_qkv, preferred_element_type=jnp.float32).astype(jnp.bfloat16)
    packed = to_windows(qkv.reshape(LEV, NLAT, NLON, 3 * D))
    packed_blocks = packed.reshape(blocks, -1, WV * WH * WW, 3 * D)
    label_blocks = labels.reshape(blocks, -1, WV * WH * WW)
    mixed_w = lax.map(lambda pair: attend(pair[0], pair[1])[0], (packed_blocks, label_blocks))
    mixed = from_windows(mixed_w.reshape(-1, WV * WH * WW, D), LEV, NLAT, NLON).reshape(-1, D)
    attn = jnp.dot(mixed, w_out, preferred_element_type=jnp.float32).astype(jnp.bfloat16)
    attn_back = roll_levels(attn.reshape(LEV, NLAT, NLON, D), -row_shift, -col_shift)
    resid = start_state + attn_back.astype(jnp.float32)
    normed_m, scale_m = norm_stats(resid)
    h_mlp = (normed_m * gain_mlp).astype(jnp.bfloat16)
    flat_m = h_mlp.reshape(-1, D)
    pre = jnp.dot(flat_m, w_up, preferred_element_type=jnp.float32)
    act = gelu_value(pre).astype(jnp.bfloat16)
    block_out = (resid + jnp.dot(act, w_down, preferred_element_type=jnp.float32).reshape(LEV, NLAT, NLON, D)).astype(jnp.bfloat16)
    cot_flat = cotangent.reshape(-1, D)
    grad_down = jnp.dot(act.T, cot_flat, preferred_element_type=jnp.float32)
    grad_act = jnp.dot(cot_flat, w_down.T, preferred_element_type=jnp.float32)
    grad_pre = (grad_act * gelu_slope(pre)).astype(jnp.bfloat16)
    grad_up = jnp.dot(flat_m.T, grad_pre, preferred_element_type=jnp.float32)
    dh_mlp = jnp.dot(grad_pre, w_up.T, preferred_element_type=jnp.float32).reshape(LEV, NLAT, NLON, D)
    term_m, grad_gain_mlp = norm_back(dh_mlp, normed_m, scale_m, gain_mlp)
    grad_resid = cotangent.astype(jnp.float32) + term_m
    grad_attn = roll_levels(grad_resid.astype(jnp.bfloat16), row_shift, col_shift).reshape(-1, D)
    grad_out = jnp.dot(mixed.T, grad_attn, preferred_element_type=jnp.float32)
    grad_mixed = jnp.dot(grad_attn, w_out.T, preferred_element_type=jnp.float32).astype(jnp.bfloat16)
    grad_mixed_w = to_windows(grad_mixed.reshape(LEV, NLAT, NLON, D)).reshape(blocks, -1, WV * WH * WW, D)
    grad_cells_w = lax.map(lambda trio: attend_back(trio[0], trio[1], trio[2]), (grad_mixed_w, packed_blocks, label_blocks))
    grad_cells = from_windows(grad_cells_w.reshape(-1, WV * WH * WW, 3 * D), LEV, NLAT, NLON).reshape(-1, 3 * D)
    grad_qkv = jnp.dot(flat_h.T, grad_cells, preferred_element_type=jnp.float32)
    grad_frame = jnp.dot(grad_cells, w_qkv.T, preferred_element_type=jnp.float32).astype(jnp.bfloat16)
    grad_h = roll_levels(grad_frame.reshape(LEV, NLAT, NLON, D), -row_shift, -col_shift).astype(jnp.float32)
    term_a, grad_gain_attn = norm_back(grad_h, normed_a, scale_a, gain_attn)
    grad_tokens = (grad_resid + term_a).astype(jnp.bfloat16)
    return (block_out, grad_tokens, grad_gain_attn, grad_qkv, grad_out, grad_gain_mlp, grad_up, grad_down)
```

```python
import functools

import jax
import jax.numpy as jnp
from jax import lax
from jax.experimental import pallas as pl
from jax.experimental.pallas import tpu as pltpu
from jax.sharding import PartitionSpec as P

HEADS = 8
WV = 2
WH = 6
WW = 12
WIN = WV * WH * WW
PLANE = WH * WW
LABEL_ROWS = 80
LABELS = 128
EPS = 1e-05
MESH = pl.DeviceIdType.MESH
F32 = jnp.float32
BF16 = jnp.bfloat16
CUBE = 6
PART = 1024
WIDTH = 256
HALF = CUBE * PART
VMEM_BYTES = 60 * 1024 * 1024
DIMS_ZERO = (((0,), (0,)), ((), ()))
DIMS_LAST = (((1,), (1,)), ((), ()))


def mm(a, b):
    return jnp.dot(a, b, preferred_element_type=F32)


def mm_tn(a, b):
    return lax.dot_general(a, b, DIMS_ZERO, preferred_element_type=F32)


def mm_nt(a, b):
    return lax.dot_general(a, b, DIMS_LAST, preferred_element_type=F32)


def norm_stats(values):
    center = values - jnp.mean(values, axis=-1, keepdims=True)
    inv_scale = lax.rsqrt(jnp.mean(center * center, axis=-1, keepdims=True) + EPS)
    return (center * inv_scale, inv_scale)


def norm_back(grad, normed, inv_scale, gain):
    gain_grad = jnp.sum(grad * normed, axis=0, keepdims=True)
    graded = grad * gain
    term = inv_scale * (
        graded
        - jnp.mean(graded, axis=-1, keepdims=True)
        - normed * jnp.mean(graded * normed, axis=-1, keepdims=True)
    )
    return (term, gain_grad)


def wrap(value, count):
    return lax.rem(value + count, count)


def neighbours(step):
    lat, lon = lax.axis_index("lat"), lax.axis_index("lon")
    lats, lons = lax.axis_size("lat"), lax.axis_size("lon")
    lat_to, lon_to = wrap(lat + step, lats), wrap(lon + step, lons)
    return [(lat_to, lon), (lat, lon_to), (lat_to, lon_to)]


def cube_peers():
    lat, lon = lax.axis_index("lat"), lax.axis_index("lon")
    core, y_hi = lax.rem(lat, 2), lat // 2
    x, y_lo, z = lax.rem(lon, 4), lax.rem(lon // 4, 2), lon // 8
    y = y_hi * 2 + y_lo

    def device(x, y, z):
        return ((y // 2) * 2 + core, z * 8 + lax.rem(y, 2) * 4 + x)

    def flip(p):
        return p + 1 - 2 * lax.rem(p, 2)

    def first(p):
        return lax.rem(p + p // 2, 2)

    peers = [
        device(flip(x), y, z),
        device(3 - x, y, z),
        device(x, flip(y), z),
        device(x, 3 - y, z),
        device(x, y, flip(z)),
        device(x, y, 3 - z),
    ]
    bits = [first(x), x // 2, first(y), y // 2, first(z), z // 2]
    return (y_hi * 2 + 1 - core, lon), core, peers, bits


def greet(devices):
    barrier = pltpu.get_barrier_semaphore()
    for device in devices:
        pl.semaphore_signal(barrier, inc=1, device_id=device, device_id_type=MESH)
    pl.semaphore_wait(barrier, len(devices))


def remote(src, dst, send, recv, device):
    return pltpu.make_async_remote_copy(
        src_ref=src, dst_ref=dst, send_sem=send, recv_sem=recv, device_id=device, device_id_type=MESH
    )


def targets(window, row_ref, col_ref, sign):
    cell = lax.broadcasted_iota(jnp.int32, (WIN, 1), 0)
    level = (cell >= PLANE).astype(jnp.int32)
    inner = cell - PLANE * level
    row = jnp.floor((inner.astype(F32) + 0.5) * (1.0 / WW)).astype(jnp.int32)
    col = inner - WW * row
    down = jnp.where(level == 0, row_ref[2 * window], row_ref[2 * window + 1])
    across = jnp.where(level == 0, col_ref[2 * window], col_ref[2 * window + 1])
    row = row + sign * down
    col = col + sign * across
    if sign < 0:
        row_out, col_out = (row < 0).astype(jnp.int32), (col < 0).astype(jnp.int32)
    else:
        row_out, col_out = (row >= WH).astype(jnp.int32), (col >= WW).astype(jnp.int32)
    row = row - sign * WH * row_out
    col = col - sign * WW * col_out
    return row_out + 2 * col_out, row * WW + col, level


def one_hot(quadrant, index, which, width):
    lanes = lax.broadcasted_iota(jnp.int32, (index.shape[0], width), 1)
    return jnp.where((lanes == index) & (quadrant == which), 1.0, 0.0).astype(BF16)


def select(quadrant, index, sources):
    total = None
    for which, source in enumerate(sources):
        term = mm(one_hot(quadrant, index, which, source.shape[0]), source)
        total = term if total is None else total + term
    return total


def halo_in_kernel(tok, cot, lab, tok_x, cot_x, lab_x, send, recv):
    ahead = neighbours(1)
    greet(ahead + neighbours(-1))
    copies = []
    for a, (own, ext) in enumerate(((tok, tok_x), (lab, lab_x), (cot, cot_x))):
        for q in range(3):
            copies.append(remote(own, ext.at[q], send.at[a, q], recv.at[a, q], ahead[q]))
            copies[-1].start()
    for copy in copies:
        copy.wait()


def compute_kernel(
    rows, cols, tok, tok_x, cot, cot_x, lab, lab_x, gain_a, w_qkv, w_out, gain_m, w_up, w_down,
    grads, gains, out, grad_tok,
    tokf, cotf, labf, norm_a, h_a, qkv, probs, mixed, resid, norm_m, h_m, dh, dqkv,
):
    width = tok.shape[1]
    for w in range(2):
        here = pl.ds(w * WIN, WIN)
        quadrant, index, level = targets(w, rows, cols, -1)
        spread = index + PLANE * level
        tokf[here, :] = select(quadrant, spread, [tok[here, :]] + [tok_x[q, here, :] for q in range(3)])
        cotf[here, :] = select(
            quadrant, spread, [cot[here, :]] + [cot_x[q, here, :] for q in range(3)]
        ).astype(BF16)
        labf[here, :] = select(quadrant, index, [lab[...]] + [lab_x[q] for q in range(3)]).astype(BF16)
    normed, scale_a = norm_stats(tokf[...])
    norm_a[...] = normed
    h_a[...] = (normed * gain_a[...]).astype(BF16)
    for c in range(3):
        part = pl.ds(c * width, width)
        qkv[:, part] = mm(h_a[...], w_qkv[:, part]).astype(BF16)

    low = lax.broadcasted_iota(jnp.int32, (1, 128), 1) < 64

    def pair_stack(block):
        zero = jnp.zeros_like(block)
        return jnp.concatenate([jnp.where(low, block, zero), jnp.where(low, zero, block)], axis=0)

    def pair_join(stack):
        return jnp.where(low, stack[:WIN], stack[WIN:])

    for w in range(2):
        here = pl.ds(w * WIN, WIN)
        allowed = mm_nt(labf[here, :], labf[here, :]) > 0.5
        allowed = jnp.concatenate([allowed, allowed], axis=0)
        for p in range(HEADS // 2):
            lanes = [pl.ds(part * width + p * 128, 128) for part in range(3)]
            query = pair_stack(qkv[here, lanes[0]])
            scores = mm_nt(query, qkv[here, lanes[1]]) * 0.125
            scores = jnp.where(allowed, scores, -jnp.inf)
            expo = jnp.exp(scores - jnp.max(scores, axis=-1, keepdims=True))
            prob = expo * (1.0 / jnp.sum(expo, axis=-1, keepdims=True))
            probs[w * 4 + p] = prob
            mixed[here, pl.ds(p * 128, 128)] = pair_join(
                mm(prob.astype(BF16), qkv[here, lanes[2]])
            ).astype(BF16)

    attn = mm(mixed[...], w_out[...]).astype(BF16).astype(F32)
    resid[...] = tokf[...] + attn
    normed, scale_m = norm_stats(resid[...])
    norm_m[...] = normed
    h_m[...] = (normed * gain_m[...]).astype(BF16)
    dh[...] = jnp.zeros_like(dh)

    def ff_step(c, carry):
        part = pl.ds(pl.multiple_of(c * 512, 512), 512)
        pre = mm(h_m[...], w_up[:, part])
        cdf = 0.5 * (1.0 + lax.erf(pre * 0.7071067811865476))
        act = (pre * cdf).astype(BF16)
        slope = cdf + pre * jnp.exp(-0.5 * pre * pre) * 0.3989422804014327
        resid[...] += mm(act, w_down[part, :])
        grad_pre = (mm_nt(cotf[...], w_down[part, :]) * slope).astype(BF16)
        dh[...] += mm_nt(grad_pre, w_up[:, part])
        down = mm_tn(act, cotf[...]).astype(BF16)
        up = mm_tn(h_m[...], grad_pre).astype(BF16)
        for b in range(2):
            cut = slice(b * WIDTH, (b + 1) * WIDTH)
            grads[pl.ds(pl.multiple_of(b * 2048 + c * 512, 512), 512), :] = down[:, cut]
            grads[pl.ds(pl.multiple_of(4096 + (2 * c + b) * 512, 512), 512), :] = up[:, cut]
        return carry

    lax.fori_loop(0, 4, ff_step, 0)
    out[...] = resid[...].astype(BF16)
    term, gain_grad_m = norm_back(dh[...], norm_m[...], scale_m, gain_m[...])
    resid[...] = cotf[...].astype(F32) + term
    grad_attn = resid[...].astype(BF16)
    grad_out = mm_tn(mixed[...], grad_attn).astype(BF16)
    for b in range(2):
        grads[pl.ds(8192 + b * 512, 512), :] = grad_out[:, b * WIDTH : (b + 1) * WIDTH]
    mixed[...] = mm_nt(grad_attn, w_out[...]).astype(BF16)

    for w in range(2):
        here = pl.ds(w * WIN, WIN)
        for p in range(HEADS // 2):
            lanes = [pl.ds(part * width + p * 128, 128) for part in range(3)]
            prob = probs[w * 4 + p]
            dmix = pair_stack(mixed[here, pl.ds(p * 128, 128)])
            query = pair_stack(qkv[here, lanes[0]])
            dprob = mm_nt(dmix, qkv[here, lanes[2]])
            dqkv[here, lanes[2]] = mm_tn(prob.astype(BF16), dmix).astype(BF16)
            dscore = prob * (dprob - jnp.sum(dprob * prob, axis=-1, keepdims=True)) * 0.125
            dscore = dscore.astype(BF16)
            dqkv[here, lanes[0]] = pair_join(mm(dscore, qkv[here, lanes[1]])).astype(BF16)
            dqkv[here, lanes[1]] = mm_tn(dscore, query).astype(BF16)

    dframe = None
    for c in range(3):
        part = pl.ds(c * width, width)
        grad_qkv = mm_tn(h_a[...], dqkv[:, part]).astype(BF16)
        for b in range(2):
            grads[pl.ds(9216 + (2 * c + b) * 512, 512), :] = grad_qkv[:, b * WIDTH : (b + 1) * WIDTH]
        term = mm_nt(dqkv[:, part], w_qkv[:, part])
        dframe = term if dframe is None else dframe + term
    dframe = dframe.astype(BF16).astype(F32)
    term, gain_grad_a = norm_back(dframe, norm_a[...], scale_a, gain_a[...])
    grad_tok[...] = (resid[...] + term).astype(BF16)
    for r in range(4):
        gains[r : r + 1, :] = gain_grad_a[:, r * 128 : (r + 1) * 128]
        gains[r + 4 : r + 5, :] = gain_grad_m[:, r * 128 : (r + 1) * 128]


def reduce_kernel(
    grads, gains, out, grad_tok,
    total, gains_sum, out_x, grad_tok_x,
    mine, core_in, cube_in, gains_acc, gains_in,
    halo_send, halo_recv, core_send, core_recv, rs_send, rs_recv, ag_send, ag_recv, end_send, end_recv,
    gain_send, gain_recv,
):
    core_peer, core, peers, bits = cube_peers()
    back = neighbours(-1)
    greet([core_peer] + peers + back + neighbours(1))
    started = []

    def go(*args):
        copy = remote(*args)
        copy.start()
        started.append(copy)
        return copy

    def rows_of(half, p, offset, count):
        return pl.ds(pl.multiple_of(half * HALF + p * PART + offset, 16), count)

    core_copies = [
        go(grads.at[rows_of(1 - core, p, 0, PART)], core_in.at[p], core_send.at[p], core_recv.at[p], core_peer)
        for p in range(CUBE)
    ]
    gain_peers = [core_peer] + peers

    def gain_go(step):
        return go(
            gains_acc.at[step], gains_in.at[step], gain_send.at[step], gain_recv.at[step], gain_peers[step]
        )

    gains_acc[0] = gains[...]
    gain_copies = [gain_go(0)]

    def gain_next():
        step = len(gain_copies)
        gain_copies[-1].wait_recv()
        summed = gains_acc[step - 1] + gains_in[step - 1]
        if step < 7:
            gains_acc[step] = summed
            gain_copies.append(gain_go(step))
        else:
            gains_sum[...] = summed

    offsets = [0] * CUBE
    rs_copies = {}

    def rs_go(p, s):
        dim, count = (p + s) % CUBE, PART >> (s + 1)
        rs_copies[p, s] = go(
            mine.at[p, pl.ds(pl.multiple_of(offsets[p] + (1 - bits[dim]) * count, 16), count)],
            cube_in.at[p, pl.ds(PART - (PART >> s), count)],
            rs_send.at[p, s],
            rs_recv.at[p, s],
            peers[dim],
        )
        offsets[p] = offsets[p] + bits[dim] * count

    for p in range(CUBE):
        core_copies[p].wait_recv()
        mine[p] = (grads[rows_of(core, p, 0, PART), :].astype(F32) + core_in[p].astype(F32)).astype(BF16)
        rs_go(p, 0)
    gain_next()
    halo_copies = []
    for a, (own, ext) in enumerate(((out, out_x), (grad_tok, grad_tok_x))):
        for q in range(3):
            halo_copies.append(go(own, ext.at[q], halo_send.at[a, q], halo_recv.at[a, q], back[q]))

    ag_copies = {}

    def ag_go(p, s):
        dim, count = (p + s) % CUBE, PART >> (s + 1)
        place = total.at[rows_of(core, p, offsets[p], count)]
        ag_copies[p, s] = go(place, place, ag_send.at[p, s], ag_recv.at[p, s], peers[dim])
        offsets[p] = offsets[p] - bits[dim] * count

    for s in range(CUBE):
        count = PART >> (s + 1)
        for p in range(CUBE):
            rs_copies[p, s].wait_recv()
            here = pl.ds(pl.multiple_of(offsets[p], 16), count)
            arrived = cube_in[p, pl.ds(PART - (PART >> s), count), :].astype(F32)
            summed = (mine[p, here, :].astype(F32) + arrived).astype(BF16)
            if s < CUBE - 1:
                mine[p, here, :] = summed
                rs_go(p, s + 1)
            else:
                total[rows_of(core, p, offsets[p], count), :] = summed
                ag_go(p, s)
        gain_next()

    end_copies = []
    for s in reversed(range(CUBE)):
        for p in range(CUBE):
            ag_copies[p, s].wait_recv()
            if s > 0:
                ag_go(p, s - 1)
            else:
                place = total.at[rows_of(core, p, 0, PART)]
                end_copies.append(go(place, place, end_send.at[p], end_recv.at[p], core_peer))
    for copy in end_copies + halo_copies:
        copy.wait_recv()
    for copy in started:
        copy.wait_send()


def finish_kernel(
    rows, cols, total, gains, out, out_x, grad_tok, grad_tok_x,
    block_out, grad_tokens, gain_a, gain_m, grad_qkv, grad_out, grad_up, grad_down,
    stage, sems,
):
    moves = []

    def put(start, count, target):
        stage[pl.ds(start, count), :] = total[pl.ds(start, count), :].astype(F32)
        move = pltpu.make_async_copy(stage.at[pl.ds(start, count)], target, sems.at[len(moves)])
        move.start()
        moves.append(move)

    for b in range(2):
        for r in range(4):
            put(b * 2048 + r * 512, 512, grad_down.at[pl.ds(r * 512, 512), pl.ds(b * WIDTH, WIDTH)])
    for b in range(8):
        put(4096 + b * 512, 512, grad_up.at[:, pl.ds(b * WIDTH, WIDTH)])
    for b in range(2):
        put(8192 + b * 512, 512, grad_out.at[:, pl.ds(b * WIDTH, WIDTH)])
    for b in range(6):
        put(9216 + b * 512, 512, grad_qkv.at[:, pl.ds(b * WIDTH, WIDTH)])
    for w in range(2):
        here = pl.ds(w * WIN, WIN)
        quadrant, index, level = targets(w, rows, cols, 1)
        spread = index + PLANE * level
        for own, ext, result in ((out, out_x, block_out), (grad_tok, grad_tok_x, grad_tokens)):
            result[here, :] = select(
                quadrant, spread, [own[here, :]] + [ext[q, here, :] for q in range(3)]
            ).astype(BF16)
    for r in range(4):
        gain_a[:, r * 128 : (r + 1) * 128] = gains[r : r + 1, :]
        gain_m[:, r * 128 : (r + 1) * 128] = gains[r + 4 : r + 5, :]
    for move in moves:
        move.wait()


VMEM = pl.BlockSpec(memory_space=pltpu.VMEM)
SMEM = pl.BlockSpec(memory_space=pltpu.SMEM)
ANY = pl.BlockSpec(memory_space=pl.ANY)
DMA = pltpu.SemaphoreType.DMA


def call(kernel, outs, in_specs, out_specs, scratch, name, collective_id=None):
    params = {"vmem_limit_bytes": VMEM_BYTES}
    if collective_id is not None:
        params.update(collective_id=collective_id, has_side_effects=True)
    return pl.pallas_call(
        kernel,
        out_shape=[jax.ShapeDtypeStruct(shape, dtype) for shape, dtype in outs],
        in_specs=in_specs,
        out_specs=out_specs,
        scratch_shapes=scratch,
        compiler_params=pltpu.CompilerParams(**params),
        name=name,
    )


def on_device(
    tokens,
    region_ids,
    shift_lat,
    shift_lon,
    gain_attn,
    w_qkv,
    w_out,
    gain_mlp,
    w_up,
    w_down,
    cotangent,
):
    levels, lat_rows, lon_cols, width = tokens.shape
    cells = levels * lat_rows * lon_cols
    ff = w_up.shape[1]
    tok = tokens.reshape(cells, width)
    cot = cotangent.reshape(cells, width)
    lab = (region_ids.reshape(-1, 1) == jnp.arange(LABELS)[None, :]).astype(BF16)
    lab = jnp.pad(lab, ((0, LABEL_ROWS - PLANE), (0, 0)))
    gain_a, gain_m = gain_attn.reshape(1, width), gain_mlp.reshape(1, width)

    tile = ((cells, width), BF16)
    halo = ((3, cells, width), BF16)
    tok_x, cot_x, lab_x = call(
        halo_in_kernel,
        [halo, halo, ((3, LABEL_ROWS, LABELS), BF16)],
        [VMEM] * 3,
        [VMEM] * 3,
        [DMA((3, 3)), DMA((3, 3))],
        "halo_in",
        0,
    )(tok, cot, lab)

    grads, gains, out, grad_tok = call(
        compute_kernel,
        [((2 * HALF, WIDTH), BF16), ((8, 128), F32), tile, tile],
        [SMEM, SMEM] + [VMEM] * 12,
        [VMEM] * 4,
        [
            pltpu.VMEM((cells, width), F32),
            pltpu.VMEM((cells, width), BF16),
            pltpu.VMEM((cells, LABELS), BF16),
            pltpu.VMEM((cells, width), F32),
            pltpu.VMEM((cells, width), BF16),
            pltpu.VMEM((cells, 3 * width), BF16),
            pltpu.VMEM((8, 2 * WIN, WIN), F32),
            pltpu.VMEM((cells, width), BF16),
            pltpu.VMEM((cells, width), F32),
            pltpu.VMEM((cells, width), F32),
            pltpu.VMEM((cells, width), BF16),
            pltpu.VMEM((cells, width), F32),
            pltpu.VMEM((cells, 3 * width), BF16),
        ],
        "block",
    )(shift_lat, shift_lon, tok, tok_x, cot, cot_x, lab, lab_x, gain_a, w_qkv, w_out, gain_m, w_up, w_down)

    total, gains_sum, out_x, grad_tok_x = call(
        reduce_kernel,
        [((2 * HALF, WIDTH), BF16), ((8, 128), F32), halo, halo],
        [VMEM] * 4,
        [VMEM] * 4,
        [
            pltpu.VMEM((CUBE, PART, WIDTH), BF16),
            pltpu.VMEM((CUBE, PART, WIDTH), BF16),
            pltpu.VMEM((CUBE, PART, WIDTH), BF16),
            pltpu.VMEM((7, 8, 128), F32),
            pltpu.VMEM((7, 8, 128), F32),
            DMA((2, 3)),
            DMA((2, 3)),
            DMA((CUBE,)),
            DMA((CUBE,)),
            DMA((CUBE, CUBE)),
            DMA((CUBE, CUBE)),
            DMA((CUBE, CUBE)),
            DMA((CUBE, CUBE)),
            DMA((CUBE,)),
            DMA((CUBE,)),
            DMA((7,)),
            DMA((7,)),
        ],
        "reduce",
        1,
    )(grads, gains, out, grad_tok)

    results = call(
        finish_kernel,
        [
            tile,
            tile,
            ((1, width), F32),
            ((1, width), F32),
            ((width, 3 * width), F32),
            ((width, width), F32),
            ((width, ff), F32),
            ((ff, width), F32),
        ],
        [SMEM, SMEM] + [VMEM] * 6,
        [VMEM] * 4 + [ANY] * 4,
        [pltpu.VMEM((2 * HALF, WIDTH), F32), DMA((24,))],
        "finish",
    )(shift_lat, shift_lon, total, gains_sum, out, out_x, grad_tok, grad_tok_x)
    block_out, grad_tokens, grad_gain_attn, grad_gain_mlp, grad_qkv, grad_out, grad_up, grad_down = results
    return (
        block_out.reshape(tokens.shape),
        grad_tokens.reshape(tokens.shape),
        grad_gain_attn.reshape(width),
        grad_qkv,
        grad_out,
        grad_gain_mlp.reshape(width),
        grad_up,
        grad_down,
    )


def solution(mesh):
    placed = (
        P(None, "lat", "lon", None),
        P("lat", "lon"),
        P(),
        P(),
        P(),
        P(),
        P(),
        P(),
        P(),
        P(),
        P(None, "lat", "lon", None),
    )
    return jax.shard_map(
        on_device,
        mesh=mesh,
        in_specs=placed,
        out_specs=(
            P(None, "lat", "lon", None),
            P(None, "lat", "lon", None),
            P(),
            P(),
            P(),
            P(),
            P(),
            P(),
        ),
        check_vma=False,
    )
```

```python
import functools

import jax
import jax.numpy as jnp
from jax import lax
from jax.experimental import pallas as pl
from jax.experimental.pallas import tpu as pltpu
from jax.sharding import PartitionSpec as P

HEADS = 8
WV = 2
WH = 6
WW = 12
WIN = WV * WH * WW
PLANE = WH * WW
LANES = 128
PAD = 16
SIDE = 4
EPS = 1e-05
MESH = pl.DeviceIdType.MESH
F32 = jnp.float32
BF16 = jnp.bfloat16
CHUNKS = 4
PART = 1024
ROUNDS = (256, 64, 16)
SEMS = 20
VMEM_BYTES = 60 * 1024 * 1024
DIMS_ZERO = (((0,), (0,)), ((), ()))
DIMS_LAST = (((1,), (1,)), ((), ()))


def mm(a, b):
    return jnp.dot(a, b, preferred_element_type=F32)


def mm_tn(a, b):
    return lax.dot_general(a, b, DIMS_ZERO, preferred_element_type=F32)


def mm_nt(a, b):
    return lax.dot_general(a, b, DIMS_LAST, preferred_element_type=F32)


def norm_stats(values):
    center = values - jnp.mean(values, axis=-1, keepdims=True)
    inv_scale = lax.rsqrt(jnp.mean(center * center, axis=-1, keepdims=True) + EPS)
    return (center * inv_scale, inv_scale)


def norm_back(grad, normed, inv_scale, gain):
    gain_grad = jnp.sum(grad * normed, axis=0, keepdims=True)
    graded = grad * gain
    term = inv_scale * (
        graded
        - jnp.mean(graded, axis=-1, keepdims=True)
        - normed * jnp.mean(graded * normed, axis=-1, keepdims=True)
    )
    return (term, gain_grad)


def places():
    lat, lon = lax.axis_index("lat"), lax.axis_index("lon")
    lats, lons = lax.axis_size("lat"), lax.axis_size("lon")
    core, y_hi = lax.rem(lat, 2), lat // 2
    x, y_lo, z = lax.rem(lon, SIDE), lax.rem(lon // SIDE, 2), lon // (2 * SIDE)
    y = y_hi * 2 + y_lo

    def device(x, y, z):
        x, y, z = lax.rem(x, SIDE), lax.rem(y, SIDE), lax.rem(z, SIDE)
        return ((y // 2) * 2 + core, z * 2 * SIDE + lax.rem(y, 2) * SIDE + x)

    steps = range(1, SIDE)
    peers = [
        [device(x + j, y, z) for j in steps],
        [device(x, y + j, z) for j in steps],
        [device(x, y, z + j) for j in steps],
    ]
    grid = {
        "below": (lax.rem(lat + 1, lats), lon),
        "above": (lax.rem(lat + lats - 1, lats), lon),
        "right": (lat, lax.rem(lon + 1, lons)),
        "left": (lat, lax.rem(lon + lons - 1, lons)),
    }
    return grid, core, (y_hi * 2 + 1 - core, lon), peers, (x, y, z)


def remote(src, dst, send, recv, device):
    return pltpu.make_async_remote_copy(
        src_ref=src, dst_ref=dst, send_sem=send, recv_sem=recv, device_id=device, device_id_type=MESH
    )


def cell_places(count, pad):
    cell = lax.broadcasted_iota(jnp.int32, (count, 1), 0)
    plane = WH * pad
    level = (cell >= plane).astype(jnp.int32)
    inner = cell - plane * level
    row = jnp.floor((inner.astype(F32) + 0.5) * (1.0 / pad)).astype(jnp.int32)
    return level, row, inner - pad * row


def per_level(level, ref, window):
    return jnp.where(level == 0, ref[2 * window], ref[2 * window + 1])


def fold(value, limit):
    out = ((value < 0) | (value >= limit)).astype(jnp.int32)
    return jnp.where(value < 0, value + limit, jnp.where(value >= limit, value - limit, value)), out


def one_hot(hit, index, width):
    lanes = lax.broadcasted_iota(jnp.int32, (index.shape[0], width), 1)
    return jnp.where((lanes == index) & hit, 1.0, 0.0).astype(BF16)


def roll_pair(level, row, col, out):
    index = level * PLANE + row * WW + col
    return one_hot(out == 0, index, WIN), one_hot(out == 1, index, WIN)


def row_roll(window, ref, sign, pad=WW):
    level, row, col = cell_places(WV * WH * pad, pad)
    row, out = fold(row + sign * per_level(level, ref, window), WH)
    return roll_pair(level, row, col, jnp.where(col < WW, out, 2))


def col_roll(window, ref, sign):
    level, row, col = cell_places(WIN, WW)
    col, out = fold(col + sign * per_level(level, ref, window), WW)
    return roll_pair(level, row, col, out)


def pack_matrix():
    level, row, col = cell_places(WIN, WW)
    return one_hot(level >= 0, (level * WH + row) * PAD + col, WV * WH * PAD)


def apply_roll(pair, here, there):
    return (mm(pair[0], here) + mm(pair[1], there)).astype(BF16)


def block_kernel(
    rows, cols, tok_in, cot_in, ids_in, gain_a, gain_m, w_qkv_hbm, w_out_hbm, w_up_hbm, w_down_hbm,
    total_a_hbm, total_b_hbm, gains_sum, out_t, out_tx, tok_t, tok_tx,
    w_qkv, w_out, w_up, w_down, padded,
    tok, tok_above, tok_rows, tok_left, cot, cot_above, cot_rows, cot_left, ids, ids_x,
    cotf, tokf, labf, norm_a, h_a, qkv, probs, mixed, resid, norm_m, h_m, dh, dqkv,
    out_f, out_right, tok_f, tok_right, gains_acc, gains_in,
    ga, core_a, mine_a, r1_a, m1_a, r2_a, m2_a, r3_a, total_a,
    gb, core_b, mine_b, r1_b, m1_b, r2_b, m2_b, r3_b, total_b,
    load_sem, halo_send, halo_recv, sum_send, sum_recv, gain_send, gain_recv, store_sem,
):
    width = gain_a.shape[1]
    grid, core, core_peer, peers, position = places()
    loads = [
        pltpu.make_async_copy(src, dst, load_sem.at[k])
        for k, (src, dst) in enumerate(
            ((w_qkv_hbm, w_qkv), (w_out_hbm, w_out), (w_up_hbm, w_up), (w_down_hbm, w_down))
        )
    ]
    for load in loads:
        load.start()
    greeted = [core_peer] + [p for axis in peers for p in axis] + list(grid.values())
    barrier = pltpu.get_barrier_semaphore()
    for device in greeted:
        pl.semaphore_signal(barrier, inc=1, device_id=device, device_id_type=MESH)

    started = []
    stores = []

    def go(*args):
        copy = remote(*args)
        copy.start()
        started.append(copy)
        return copy

    halos = []

    def halo_go(src, dst, device):
        k = len(halos)
        halos.append(go(src, dst, halo_send.at[k], halo_recv.at[k], device))
        return halos[-1]

    def window(w):
        return pl.ds(w * WIN, WIN)

    padded[...] = jnp.zeros_like(padded)
    packer = pack_matrix()
    for source, packed in ((tok_in, tok), (cot_in, cot)):
        for g in range(source.shape[0]):
            padded[pl.ds(g * PAD, WW), :] = source[g]
        for w in range(2):
            span = WV * WH * PAD
            packed[window(w), :] = mm(packer, padded[pl.ds(w * span, span), :]).astype(BF16)
    ids[0:8, :] = jnp.zeros((8, LANES), jnp.int32)
    ids[0:WH, 0:WW] = ids_in[...]
    pl.semaphore_wait(barrier, len(greeted))
    lat_tok = [halo_go(tok.at[window(w)], tok_above.at[window(w)], grid["below"]) for w in range(2)]
    lat_ids = halo_go(ids.at[pl.ds(0, 8)], ids.at[pl.ds(8, 8)], grid["below"])
    lat_cot = [halo_go(cot.at[window(w)], cot_above.at[window(w)], grid["below"]) for w in range(2)]
    row_pairs = [row_roll(w, rows, -1) for w in range(2)]
    col_pairs = [col_roll(w, cols, -1) for w in range(2)]
    lon_tok, lon_cot = [], []
    for w in range(2):
        lat_tok[w].wait_recv()
        tok_rows[window(w), :] = apply_roll(row_pairs[w], tok[window(w), :], tok_above[window(w), :])
        lon_tok.append(halo_go(tok_rows.at[window(w)], tok_left.at[window(w)], grid["right"]))
        if w == 0:
            lat_ids.wait_recv()
            lon_ids = halo_go(ids, ids_x, grid["right"])
    for w in range(2):
        lat_cot[w].wait_recv()
        cot_rows[window(w), :] = apply_roll(row_pairs[w], cot[window(w), :], cot_above[window(w), :])
        lon_cot.append(halo_go(cot_rows.at[window(w)], cot_left.at[window(w)], grid["right"]))

    lon_ids.wait_recv()
    ids_all = jnp.concatenate([ids[...], ids_x[...]], axis=0).astype(F32).astype(BF16)
    for load in loads:
        load.wait()
    for w in range(2):
        level, row, col = cell_places(WIN, WW)
        row, row_out = fold(row - per_level(level, rows, w), WH)
        col, col_out = fold(col - per_level(level, cols, w), WW)
        picked = mm(one_hot(level >= 0, (row_out + 2 * col_out) * 8 + row, 32), ids_all)
        lanes = lax.broadcasted_iota(jnp.int32, (WIN, LANES), 1)
        label = jnp.sum(jnp.where(lanes == col, picked, 0.0), axis=-1, keepdims=True)
        labf[window(w), :] = jnp.where(lanes.astype(F32) == label, 1.0, 0.0).astype(BF16)
    for w in range(2):
        lon_tok[w].wait_recv()
        tokf[window(w), :] = apply_roll(
            col_pairs[w], tok_rows[window(w), :], tok_left[window(w), :]
        ).astype(F32)
    normed, scale_a = norm_stats(tokf[...])
    norm_a[...] = normed
    h_a[...] = (normed * gain_a[...]).astype(BF16)
    for c in range(3):
        part = pl.ds(c * width, width)
        qkv[:, part] = mm(h_a[...], w_qkv[:, part]).astype(BF16)

    low = lax.broadcasted_iota(jnp.int32, (1, LANES), 1) < LANES // 2

    def pair_stack(block):
        zero = jnp.zeros_like(block)
        return jnp.concatenate([jnp.where(low, block, zero), jnp.where(low, zero, block)], axis=0)

    def pair_join(stack):
        return jnp.where(low, stack[:WIN], stack[WIN:])

    def pair_lanes(p):
        return [pl.ds(part * width + p * LANES, LANES) for part in range(3)]

    for w in range(2):
        here = window(w)
        allowed = mm_nt(labf[here, :], labf[here, :]) > 0.5
        allowed = jnp.concatenate([allowed, allowed], axis=0)
        for p in range(HEADS // 2):
            lanes = pair_lanes(p)
            query = pair_stack(qkv[here, lanes[0]])
            scores = mm_nt(query, qkv[here, lanes[1]]) * 0.125
            scores = jnp.where(allowed, scores, -jnp.inf)
            expo = jnp.exp(scores - jnp.max(scores, axis=-1, keepdims=True))
            prob = expo * (1.0 / jnp.sum(expo, axis=-1, keepdims=True))
            probs[w * 4 + p] = prob
            mixed[here, pl.ds(p * LANES, LANES)] = pair_join(
                mm(prob.astype(BF16), qkv[here, lanes[2]])
            ).astype(BF16)

    attn = mm(mixed[...], w_out[...]).astype(BF16).astype(F32)
    resid[...] = tokf[...] + attn
    normed, scale_m = norm_stats(resid[...])
    norm_m[...] = normed
    h_m[...] = (normed * gain_m[...]).astype(BF16)
    dh[...] = jnp.zeros_like(dh)
    for w in range(2):
        lon_cot[w].wait_recv()
        cotf[window(w), :] = apply_roll(col_pairs[w], cot_rows[window(w), :], cot_left[window(w), :])

    set_a = (ga, core_a, mine_a, (r1_a, r2_a, r3_a), (mine_a, m1_a, m2_a), total_a, total_a_hbm)
    set_b = (gb, core_b, mine_b, (r1_b, r2_b, r3_b), (mine_b, m1_b, m2_b), total_b, total_b_hbm)

    def block(offset, count):
        return pl.ds(pl.multiple_of(offset, 16), count)

    def store(src, dst):
        copy = pltpu.make_async_copy(src, dst, store_sem.at[len(stores)])
        copy.start()
        stores.append(copy)

    def chain(refs, i, k):
        partial, core_in, mine, arrivals, sums, total, total_hbm = refs
        order = [(k + r) % 3 for r in range(3)]
        used = [0]

        def send(src, dst, device):
            n = used[0]
            used[0] += 1
            return go(src, dst, sum_send.at[k, n], sum_recv.at[k, n], device)

        first = send(partial.at[1 - core, i], core_in.at[i], core_peer)
        yield
        first.wait_recv()
        mine[i] = (partial[core, i].astype(F32) + core_in[i].astype(F32)).astype(BF16)
        offset, offsets = 0, []
        for r, count in enumerate(ROUNDS):
            at = position[order[r]]
            copies = [
                send(
                    sums[r].at[i, block(lax.rem(at + j, SIDE) * count, count)],
                    arrivals[r].at[i, j - 1],
                    peers[order[r]][j - 1],
                )
                for j in range(1, SIDE)
            ]
            yield
            for copy in copies:
                copy.wait_recv()
            summed = sums[r][i, block(at * count, count), :].astype(F32)
            for j in range(SIDE - 1):
                summed = summed + arrivals[r][i, j].astype(F32)
            offset = offset + at * count
            offsets.append(offset)
            if r < 2:
                sums[r + 1][i] = summed.astype(BF16)
            else:
                total[core, i, block(offset, count), :] = summed.astype(BF16)
        for r in reversed(range(3)):
            place = total.at[core, i, block(offsets[r], ROUNDS[r])]
            copies = [send(place, place, peers[order[r]][j]) for j in range(SIDE - 1)]
            yield
            for copy in copies:
                copy.wait_recv()
        last = send(total.at[core, i], total.at[core, i], core_peer)
        store(total.at[core, i], total_hbm.at[core, i])
        yield
        last.wait_recv()
        store(total.at[1 - core, i], total_hbm.at[1 - core, i])

    def gain_chain():
        used = [0]

        def send(src, device):
            n = used[0]
            used[0] += 1
            return go(src, gains_in.at[n], gain_send.at[n], gain_recv.at[n], device)

        copy = send(gains_acc.at[0], core_peer)
        yield
        copy.wait_recv()
        gains_acc[1] = gains_acc[0] + gains_in[0]
        for axis in range(3):
            copies = [send(gains_acc.at[axis + 1], peer) for peer in peers[axis]]
            yield
            for copy in copies:
                copy.wait_recv()
            base = 1 + 3 * axis
            summed = (gains_acc[axis + 1] + gains_in[base + 1]) + (gains_in[base] + gains_in[base + 2])
            if axis < 2:
                gains_acc[axis + 2] = summed
            else:
                gains_sum[...] = summed

    def advance(*chains):
        for link in chains:
            next(link, None)

    chains = [chain(set_a, i, i) for i in range(CHUNKS)] + [chain(set_b, i, CHUNKS + i) for i in range(CHUNKS)]

    for c in range(CHUNKS):
        part = pl.ds(c * 512, 512)
        pre = mm(h_m[...], w_up[:, part])
        cdf = 0.5 * (1.0 + lax.erf(pre * 0.7071067811865476))
        act = (pre * cdf).astype(BF16)
        slope = cdf + pre * jnp.exp(-0.5 * pre * pre) * 0.3989422804014327
        resid[...] += mm(act, w_down[part, :])
        grad_pre = (mm_nt(cotf[...], w_down[part, :]) * slope).astype(BF16)
        dh[...] += mm_nt(grad_pre, w_up[:, part])
        down = mm_tn(act, cotf[...]).astype(BF16)
        up = mm_tn(h_m[...], grad_pre).astype(BF16)
        for b in range(2):
            cut = slice(b * 256, (b + 1) * 256)
            ga[0, c, b * 512 : (b + 1) * 512, :] = down[:, cut]
            ga[1, c, b * 512 : (b + 1) * 512, :] = up[:, cut]
        advance(chains[c])
        if c > 0:
            advance(chains[c - 1])
    out_f[...] = resid[...].astype(BF16)
    out_lon = halo_go(out_f, out_right, grid["left"])
    term, gain_grad_m = norm_back(dh[...], norm_m[...], scale_m, gain_m[...])
    resid[...] = cotf[...].astype(F32) + term
    grad_attn = resid[...].astype(BF16)

    def put(half, i, b, value):
        for j in range(2):
            gb[half, i, j * 512 : (j + 1) * 512, :] = value[:, b + j * LANES : b + (j + 1) * LANES]

    grad_out = mm_tn(mixed[...], grad_attn).astype(BF16)
    put(0, 0, 0, grad_out)
    put(1, 0, 256, grad_out)
    advance(chains[4], chains[3])
    mixed[...] = mm_nt(grad_attn, w_out[...]).astype(BF16)

    homes = {(0, 0): (0, 1), (1, 0): (1, 1), (2, 0): (0, 2), (0, 1): (1, 2), (1, 1): (0, 3), (2, 1): (1, 3)}
    pump = [[0, 1, 4], [2, 3], [0, 1, 4, 2], [3, 0, 1]]
    for p in range(HEADS // 2):
        lanes = pair_lanes(p)
        for w in range(2):
            here = window(w)
            prob = probs[w * 4 + p]
            dmix = pair_stack(mixed[here, pl.ds(p * LANES, LANES)])
            query = pair_stack(qkv[here, lanes[0]])
            dprob = mm_nt(dmix, qkv[here, lanes[2]])
            dqkv[here, lanes[2]] = mm_tn(prob.astype(BF16), dmix).astype(BF16)
            dscore = prob * (dprob - jnp.sum(dprob * prob, axis=-1, keepdims=True)) * 0.125
            dscore = dscore.astype(BF16)
            dqkv[here, lanes[0]] = pair_join(mm(dscore, qkv[here, lanes[1]])).astype(BF16)
            dqkv[here, lanes[1]] = mm_tn(dscore, query).astype(BF16)
        if p % 2 == 1:
            for c in range(3):
                half, i = homes[c, p // 2]
                cut = pl.ds(c * width + (p // 2) * 256, 256)
                put(half, i, 0, mm_tn(h_a[...], dqkv[:, cut]).astype(BF16))
            if p == 1:
                advance(chains[5])
            else:
                advance(chains[6], chains[7])
        advance(*[chains[k] for k in pump[p]])

    dframe = None
    for c in range(3):
        part = pl.ds(c * width, width)
        term = mm_nt(dqkv[:, part], w_qkv[:, part])
        dframe = term if dframe is None else dframe + term
    dframe = dframe.astype(BF16).astype(F32)
    advance(chains[5], chains[6], chains[7])
    term, gain_grad_a = norm_back(dframe, norm_a[...], scale_a, gain_a[...])
    for r in range(4):
        cut = slice(r * LANES, (r + 1) * LANES)
        gains_acc[0, r : r + 1, :] = gain_grad_a[:, cut]
        gains_acc[0, r + 4 : r + 5, :] = gain_grad_m[:, cut]
    gains_link = gain_chain()
    advance(gains_link)
    tok_f[...] = (resid[...] + term).astype(BF16)
    tok_lon = halo_go(tok_f, tok_right, grid["left"])
    back_pairs = [col_roll(w, cols, 1) for w in range(2)]

    def turn(arrived, own, other, rolled, rolled_x):
        arrived.wait_recv()
        for w in range(2):
            here = window(w)
            rolled[here, :] = apply_roll(back_pairs[w], own[here, :], other[here, :])
        return halo_go(rolled, rolled_x, grid["above"])

    out_lat = turn(out_lon, out_f, out_right, out_t, out_tx)
    chains.append(gains_link)
    tok_lat = None
    for step in range(9):
        advance(*chains)
        if step == 1:
            tok_lat = turn(tok_lon, tok_f, tok_right, tok_t, tok_tx)
    for copy in (out_lat, tok_lat):
        copy.wait_recv()
    for copy in started:
        copy.wait_send()
    for copy in stores:
        copy.wait()


def finish_kernel(
    rows, cols, total_a_hbm, total_b_hbm, gains, out_t, out_tx, tok_t, tok_tx,
    block_out, grad_tokens, gain_a, gain_m, grad_qkv, grad_out, grad_up, grad_down,
    total_a, total_b, stage_a, stage_b, in_sems, out_sems,
):
    loads, moves = {}, []
    for i in range(CHUNKS):
        for half in range(2):
            for kind, (src, dst) in enumerate(((total_a_hbm, total_a), (total_b_hbm, total_b))):
                load = pltpu.make_async_copy(src.at[half, i], dst.at[half, i], in_sems.at[kind, half, i])
                load.start()
                loads[kind, half, i] = load

    def put(stage, total, half, i, b, target):
        stage[half, i, b * 512 : (b + 1) * 512, :] = total[half, i, b * 512 : (b + 1) * 512, :].astype(F32)
        move = pltpu.make_async_copy(
            stage.at[half, i, pl.ds(b * 512, 512)], target, out_sems.at[len(moves)]
        )
        move.start()
        moves.append(move)

    homes = {(0, 0): None, (1, 0): None, (0, 1): (0, 0), (1, 1): (1, 0), (0, 2): (2, 0), (1, 2): (0, 1), (0, 3): (1, 1), (1, 3): (2, 1)}
    for i in range(CHUNKS):
        for half in range(2):
            loads[0, half, i].wait()
            for b in range(2):
                if half == 0:
                    target = grad_down.at[pl.ds(i * 512, 512), pl.ds(b * 256, 256)]
                else:
                    target = grad_up.at[:, pl.ds(i * 512 + b * 256, 256)]
                put(stage_a, total_a, half, i, b, target)
            loads[1, half, i].wait()
            for b in range(2):
                if i == 0:
                    target = grad_out.at[:, pl.ds(half * 256 + b * LANES, LANES)]
                else:
                    c, second = homes[half, i]
                    target = grad_qkv.at[:, pl.ds(c * 512 + second * 256 + b * LANES, LANES)]
                put(stage_b, total_b, half, i, b, target)
    for w in range(2):
        here = pl.ds(w * WIN, WIN)
        pair = row_roll(w, rows, 1, PAD)
        for own, other, result in ((out_t, out_tx, block_out), (tok_t, tok_tx, grad_tokens)):
            rolled = apply_roll(pair, own[here, :], other[here, :])
            for g in range(WV * WH):
                result[w * WV * WH + g] = rolled[g * PAD : g * PAD + WW]
    for r in range(4):
        cut = slice(r * LANES, (r + 1) * LANES)
        gain_a[:, cut] = gains[r : r + 1, :]
        gain_m[:, cut] = gains[r + 4 : r + 5, :]
    for move in moves:
        move.wait()


VMEM = pl.BlockSpec(memory_space=pltpu.VMEM)
SMEM = pl.BlockSpec(memory_space=pltpu.SMEM)
ANY = pl.BlockSpec(memory_space=pl.ANY)
DMA = pltpu.SemaphoreType.DMA


def call(kernel, outs, in_specs, out_specs, scratch, name, collective_id=None):
    params = {"vmem_limit_bytes": VMEM_BYTES}
    if collective_id is not None:
        params.update(collective_id=collective_id, has_side_effects=True)
    return pl.pallas_call(
        kernel,
        out_shape=[jax.ShapeDtypeStruct(shape, dtype) for shape, dtype in outs],
        in_specs=in_specs,
        out_specs=out_specs,
        scratch_shapes=scratch,
        compiler_params=pltpu.CompilerParams(**params),
        name=name,
    )


def sum_buffers(lanes):
    shapes = [(2, CHUNKS, PART, lanes), (CHUNKS, PART, lanes), (CHUNKS, PART, lanes)]
    for r, count in enumerate(ROUNDS):
        shapes.append((CHUNKS, SIDE - 1, count, lanes))
        if r < 2:
            shapes.append((CHUNKS, count, lanes))
    shapes.append((2, CHUNKS, PART, lanes))
    return [pltpu.VMEM(shape, BF16) for shape in shapes]


def on_device(
    tokens,
    region_ids,
    shift_lat,
    shift_lon,
    gain_attn,
    w_qkv,
    w_out,
    gain_mlp,
    w_up,
    w_down,
    cotangent,
):
    levels, lat_rows, lon_cols, width = tokens.shape
    cells = levels * lat_rows * lon_cols
    ff = w_up.shape[1]
    lines = (levels * lat_rows, lon_cols, width)
    tile = ((cells, width), BF16)
    half, full = pltpu.VMEM((cells, width), BF16), pltpu.VMEM((cells, width), F32)
    total_a, total_b, gains_sum, out_t, out_tx, tok_t, tok_tx = call(
        block_kernel,
        [((2, CHUNKS, PART, 256), BF16), ((2, CHUNKS, PART, LANES), BF16), ((8, LANES), F32)] + [tile] * 4,
        [SMEM] * 2 + [VMEM] * 5 + [ANY] * 4,
        [ANY] * 2 + [VMEM] * 5,
        [pltpu.VMEM(w.shape, BF16) for w in (w_qkv, w_out, w_up, w_down)]
        + [pltpu.VMEM((lines[0] * PAD, width), BF16)]
        + [half] * 8
        + [pltpu.VMEM((16, LANES), jnp.int32)] * 2
        + [
            half,
            full,
            pltpu.VMEM((cells, LANES), BF16),
            full,
            half,
            pltpu.VMEM((cells, 3 * width), BF16),
            pltpu.VMEM((HEADS, 2 * WIN, WIN), F32),
            half,
            full,
            full,
            half,
            full,
            pltpu.VMEM((cells, 3 * width), BF16),
        ]
        + [half] * 4
        + [pltpu.VMEM((4, 8, LANES), F32), pltpu.VMEM((10, 8, LANES), F32)]
        + sum_buffers(256)
        + sum_buffers(LANES)
        + [
            DMA((4,)),
            DMA((14,)),
            DMA((14,)),
            DMA((2 * CHUNKS, SEMS)),
            DMA((2 * CHUNKS, SEMS)),
            DMA((10,)),
            DMA((10,)),
            DMA((4 * CHUNKS,)),
        ],
        "block",
        0,
    )(
        shift_lat, shift_lon, tokens.reshape(lines), cotangent.reshape(lines), region_ids,
        gain_attn.reshape(1, width), gain_mlp.reshape(1, width), w_qkv, w_out, w_up, w_down,
    )
    results = call(
        finish_kernel,
        [
            (lines, BF16),
            (lines, BF16),
            ((1, width), F32),
            ((1, width), F32),
            ((width, 3 * width), F32),
            ((width, width), F32),
            ((width, ff), F32),
            ((ff, width), F32),
        ],
        [SMEM] * 2 + [ANY] * 2 + [VMEM] * 5,
        [VMEM] * 4 + [ANY] * 4,
        [
            pltpu.VMEM((2, CHUNKS, PART, 256), BF16),
            pltpu.VMEM((2, CHUNKS, PART, LANES), BF16),
            pltpu.VMEM((2, CHUNKS, PART, 256), F32),
            pltpu.VMEM((2, CHUNKS, PART, LANES), F32),
            DMA((2, 2, CHUNKS)),
            DMA((8 * CHUNKS,)),
        ],
        "finish",
    )(shift_lat, shift_lon, total_a, total_b, gains_sum, out_t, out_tx, tok_t, tok_tx)
    block_out, grad_tokens, grad_gain_attn, grad_gain_mlp, grad_qkv, grad_out, grad_up, grad_down = results
    return (
        block_out.reshape(tokens.shape),
        grad_tokens.reshape(tokens.shape),
        grad_gain_attn.reshape(width),
        grad_qkv,
        grad_out,
        grad_gain_mlp.reshape(width),
        grad_up,
        grad_down,
    )


def solution(mesh):
    placed = (
        P(None, "lat", "lon", None),
        P("lat", "lon"),
        P(),
        P(),
        P(),
        P(),
        P(),
        P(),
        P(),
        P(),
        P(None, "lat", "lon", None),
    )
    return jax.shard_map(
        on_device,
        mesh=mesh,
        in_specs=placed,
        out_specs=(
            P(None, "lat", "lon", None),
            P(None, "lat", "lon", None),
            P(),
            P(),
            P(),
            P(),
            P(),
            P(),
        ),
        check_vma=False,
    )
```

```python
import functools

import jax
import jax.numpy as jnp
from jax import lax
from jax.experimental import pallas as pl
from jax.experimental.pallas import tpu as pltpu
from jax.sharding import PartitionSpec as P

HEADS = 8
WV = 2
WH = 6
WW = 12
WIN = WV * WH * WW
PLANE = WH * WW
LANES = 128
LEVELS = 4
CELLS = LEVELS * PLANE
SIDE = 4
EPS = 1e-05
MESH = pl.DeviceIdType.MESH
F32 = jnp.float32
BF16 = jnp.bfloat16
CHUNKS = 4
CHAINS = 12
PART = 1024
ROUNDS = (256, 64, 16)
SEMS = 20
VMEM_BYTES = 60 * 1024 * 1024
DIMS_ZERO = (((0,), (0,)), ((), ()))
DIMS_LAST = (((1,), (1,)), ((), ()))


def mm(a, b):
    return jnp.dot(a, b, preferred_element_type=F32)


def mm_tn(a, b):
    return lax.dot_general(a, b, DIMS_ZERO, preferred_element_type=F32)


def mm_nt(a, b):
    return lax.dot_general(a, b, DIMS_LAST, preferred_element_type=F32)


def norm_stats(values):
    center = values - jnp.mean(values, axis=-1, keepdims=True)
    inv_scale = lax.rsqrt(jnp.mean(center * center, axis=-1, keepdims=True) + EPS)
    return (center * inv_scale, inv_scale)


def norm_back(grad, normed, inv_scale, gain):
    gain_grad = jnp.sum(grad * normed, axis=0, keepdims=True)
    graded = grad * gain
    term = inv_scale * (
        graded
        - jnp.mean(graded, axis=-1, keepdims=True)
        - normed * jnp.mean(graded * normed, axis=-1, keepdims=True)
    )
    return (term, gain_grad)


def places():
    lat, lon = lax.axis_index("lat"), lax.axis_index("lon")
    lats, lons = lax.axis_size("lat"), lax.axis_size("lon")
    core, y_hi = lax.rem(lat, 2), lat // 2
    x, y_lo, z = lax.rem(lon, SIDE), lax.rem(lon // SIDE, 2), lon // (2 * SIDE)
    y = y_hi * 2 + y_lo

    def device(x, y, z):
        x, y, z = lax.rem(x, SIDE), lax.rem(y, SIDE), lax.rem(z, SIDE)
        return ((y // 2) * 2 + core, z * 2 * SIDE + lax.rem(y, 2) * SIDE + x)

    steps = range(1, SIDE)
    peers = [
        [device(x + j, y, z) for j in steps],
        [device(x, y + j, z) for j in steps],
        [device(x, y, z + j) for j in steps],
    ]
    grid = {
        "below": (lax.rem(lat + 1, lats), lon),
        "above": (lax.rem(lat + lats - 1, lats), lon),
        "right": (lat, lax.rem(lon + 1, lons)),
        "left": (lat, lax.rem(lon + lons - 1, lons)),
    }
    return grid, core, (y_hi * 2 + 1 - core, lon), peers, (x, y, z)


def remote(src, dst, send, recv, device):
    return pltpu.make_async_remote_copy(
        src_ref=src, dst_ref=dst, send_sem=send, recv_sem=recv, device_id=device, device_id_type=MESH
    )


def div(value, by):
    return jnp.floor((value.astype(F32) + 0.5) * (1.0 / by)).astype(jnp.int32)


def frame_cells(start, count):
    cell = start + lax.broadcasted_iota(jnp.int32, (count, 1), 0)
    level = div(cell, PLANE)
    row = div(cell - level * PLANE, WW)
    return level, row, cell - level * PLANE - row * WW


def data_cells():
    cell = lax.broadcasted_iota(jnp.int32, (CELLS, 1), 0)
    spot = div(cell, LEVELS)
    row = div(spot, WW)
    return cell - spot * LEVELS, row, spot - row * WW


def row_cells():
    cell = lax.broadcasted_iota(jnp.int32, (CELLS, 1), 0)
    row = div(cell, LEVELS * WW)
    level = div(cell - row * LEVELS * WW, WW)
    return level, row, cell - row * LEVELS * WW - level * WW


def per_level(level, ref):
    value = ref[LEVELS - 1]
    for k in reversed(range(LEVELS - 1)):
        value = jnp.where(level == k, ref[k], value)
    return value


def fold(value, limit):
    out = ((value < 0) | (value >= limit)).astype(jnp.int32)
    return jnp.where(value < 0, value + limit, jnp.where(value >= limit, value - limit, value)), out


def one_hot(hit, index, width):
    lanes = lax.broadcasted_iota(jnp.int32, (index.shape[0], width), 1)
    return jnp.where((lanes == index) & hit, 1.0, 0.0).astype(BF16)


def roll_pair(index, out, width):
    return one_hot(out == 0, index, width), one_hot(out == 1, index, width)


def apply_roll(pair, here, there):
    return (mm(pair[0], here) + mm(pair[1], there)).astype(BF16)


def block_kernel(
    rows, cols, tok_in, cot_in, ids_in, gain_a, gain_m, w_qkv_hbm, w_out_hbm, w_up_hbm, w_down_hbm,
    total_hbm, gains_sum, out_t, out_tx, tok_t, tok_tx,
    w_qkv, w_out, w_up, w_down,
    tok_above, cot_above, tok_rows, tok_left, cot_rows, cot_left, ids, ids_x,
    cotf, tokf, labf, norm_a, h_a, qkv, probs, mixed, resid, norm_m, h_m, dh, dqkv,
    out_f, out_right, tok_f, tok_right, gains_acc, gains_in,
    partial, core_in, mine, r1, m1, r2, m2, r3, total,
    load_sem, halo_send, halo_recv, sum_send, sum_recv, gain_send, gain_recv, store_sem,
):
    width = gain_a.shape[1]
    grid, core, core_peer, peers, position = places()
    loads = [
        pltpu.make_async_copy(src, dst, load_sem.at[k])
        for k, (src, dst) in enumerate(
            ((w_qkv_hbm, w_qkv), (w_out_hbm, w_out), (w_up_hbm, w_up), (w_down_hbm, w_down))
        )
    ]
    greeted = [core_peer] + [p for axis in peers for p in axis] + list(grid.values())
    barrier = pltpu.get_barrier_semaphore()
    for device in greeted:
        pl.semaphore_signal(barrier, inc=1, device_id=device, device_id_type=MESH)
    for load in loads:
        load.start()

    started = []
    stores = []

    def go(*args):
        copy = remote(*args)
        copy.start()
        started.append(copy)
        return copy

    halos = []

    def halo_go(src, dst, device):
        k = len(halos)
        halos.append(go(src, dst, halo_send.at[k], halo_recv.at[k], device))
        return halos[-1]

    def window(w):
        return pl.ds(w * WIN, WIN)

    ids[0:8, :] = jnp.zeros((8, LANES), jnp.int32)
    ids[0:WH, 0:WW] = ids_in[...]
    for above in (tok_above, cot_above):
        above[0:WW] = jnp.zeros((WW, LEVELS, width), BF16)
    used_rows = pl.ds(WW, PLANE - WW)
    pl.semaphore_wait(barrier, len(greeted))
    lat_tok = halo_go(tok_in.at[used_rows], tok_above.at[used_rows], grid["below"])
    lat_ids = halo_go(ids.at[pl.ds(0, 8)], ids.at[pl.ds(8, 8)], grid["below"])
    lat_cot = halo_go(cot_in.at[used_rows], cot_above.at[used_rows], grid["below"])
    level, row, col = frame_cells(0, CELLS)
    row, row_out = fold(row - per_level(level, rows), WH)
    row_pair = roll_pair((row * WW + col) * LEVELS + level, row_out, CELLS)
    level, row, col = frame_cells(0, CELLS)
    col, col_out = fold(col - per_level(level, cols), WW)
    col_index = lax.rem(level, WV) * PLANE + row * WW + col
    col_pairs = [
        roll_pair(col_index[w * WIN : (w + 1) * WIN], col_out[w * WIN : (w + 1) * WIN], WIN) for w in range(2)
    ]
    lat_tok.wait_recv()
    tok_rows[...] = apply_roll(
        row_pair, tok_in[...].reshape(CELLS, width), tok_above[...].reshape(CELLS, width)
    )
    lon_tok = [halo_go(tok_rows.at[window(w)], tok_left.at[window(w)], grid["right"]) for w in range(2)]
    lat_ids.wait_recv()
    lon_ids = halo_go(ids, ids_x, grid["right"])
    lat_cot.wait_recv()
    cot_rows[...] = apply_roll(
        row_pair, cot_in[...].reshape(CELLS, width), cot_above[...].reshape(CELLS, width)
    )
    lon_cot = []

    def lon_cot_go(w):
        lon_cot.append(halo_go(cot_rows.at[window(w)], cot_left.at[window(w)], grid["right"]))

    lon_ids.wait_recv()
    ids_all = jnp.concatenate([ids[...], ids_x[...]], axis=0).astype(F32).astype(BF16)
    level, row, col = frame_cells(0, CELLS)
    row, row_out = fold(row - per_level(level, rows), WH)
    col, col_out = fold(col - per_level(level, cols), WW)
    picked = mm(one_hot(level >= 0, (row_out + 2 * col_out) * 8 + row, 32), ids_all)
    lanes = lax.broadcasted_iota(jnp.int32, (CELLS, LANES), 1)
    label = jnp.sum(jnp.where(lanes == col, picked, 0.0), axis=-1, keepdims=True)
    labf[...] = jnp.where(lanes.astype(F32) == label, 1.0, 0.0).astype(BF16)
    scale_a = []

    def forward_in(w):
        here = window(w)
        lon_tok[w].wait_recv()
        lon_cot_go(w)
        values = apply_roll(col_pairs[w], tok_rows[here, :], tok_left[here, :]).astype(F32)
        tokf[here, :] = values
        normed, scale = norm_stats(values)
        scale_a.append(scale)
        norm_a[here, :] = normed
        h_a[here, :] = (normed * gain_a[...]).astype(BF16)
        if w == 0:
            loads[0].wait()
        for c in range(3):
            part = pl.ds(c * width, width)
            qkv[here, part] = mm(h_a[here, :], w_qkv[:, part]).astype(BF16)

    low = lax.broadcasted_iota(jnp.int32, (1, LANES), 1) < LANES // 2

    def pair_stack(block):
        zero = jnp.zeros_like(block)
        return jnp.concatenate([jnp.where(low, block, zero), jnp.where(low, zero, block)], axis=0)

    def pair_join(stack):
        return jnp.where(low, stack[:WIN], stack[WIN:])

    def pair_lanes(p):
        return [pl.ds(part * width + p * LANES, LANES) for part in range(3)]

    for w in range(2):
        here = window(w)
        forward_in(w)
        allowed = mm_nt(labf[here, :], labf[here, :]) > 0.5
        allowed = jnp.concatenate([allowed, allowed], axis=0)
        for p in range(HEADS // 2):
            lanes = pair_lanes(p)
            query = pair_stack(qkv[here, lanes[0]])
            scores = mm_nt(query, qkv[here, lanes[1]]) * 0.125
            scores = jnp.where(allowed, scores, -jnp.inf)
            expo = jnp.exp(scores - jnp.max(scores, axis=-1, keepdims=True))
            prob = expo * (1.0 / jnp.sum(expo, axis=-1, keepdims=True))
            probs[w * 4 + p] = prob
            mixed[here, pl.ds(p * LANES, LANES)] = pair_join(
                mm(prob.astype(BF16), qkv[here, lanes[2]])
            ).astype(BF16)

    for load in loads[1:]:
        load.wait()
    attn = mm(mixed[...], w_out[...]).astype(BF16).astype(F32)
    resid[...] = tokf[...] + attn
    normed, scale_m = norm_stats(resid[...])
    norm_m[...] = normed
    h_m[...] = (normed * gain_m[...]).astype(BF16)
    dh[...] = jnp.zeros_like(dh)
    for w in range(2):
        lon_cot[w].wait_recv()
        cotf[window(w), :] = apply_roll(col_pairs[w], cot_rows[window(w), :], cot_left[window(w), :])

    arrivals, sums = (r1, r2, r3), (mine, m1, m2)

    def block(offset, count):
        return pl.ds(pl.multiple_of(offset, 16), count)

    def store(src, dst):
        copy = pltpu.make_async_copy(src, dst, store_sem.at[len(stores)])
        copy.start()
        stores.append(copy)

    def chain(i):
        order = [(i + r) % 3 for r in range(3)]
        used = [0]

        def send(src, dst, device):
            n = used[0]
            used[0] += 1
            return go(src, dst, sum_send.at[i, n], sum_recv.at[i, n], device)

        first = send(partial.at[1 - core, i], core_in.at[i], core_peer)
        yield
        first.wait_recv()
        mine[i] = (partial[core, i].astype(F32) + core_in[i].astype(F32)).astype(BF16)
        offset, offsets = 0, []
        for r, count in enumerate(ROUNDS):
            at = position[order[r]]
            copies = [
                send(
                    sums[r].at[i, block(lax.rem(at + j, SIDE) * count, count)],
                    arrivals[r].at[i, j - 1],
                    peers[order[r]][j - 1],
                )
                for j in range(1, SIDE)
            ]
            yield
            for copy in copies:
                copy.wait_recv()
            summed = sums[r][i, block(at * count, count), :].astype(F32)
            for j in range(SIDE - 1):
                summed = summed + arrivals[r][i, j].astype(F32)
            offset = offset + at * count
            offsets.append(offset)
            if r < 2:
                sums[r + 1][i] = summed.astype(BF16)
            else:
                total[core, i, block(offset, count), :] = summed.astype(BF16)
        for r in reversed(range(3)):
            place = total.at[core, i, block(offsets[r], ROUNDS[r])]
            copies = [send(place, place, peers[order[r]][j]) for j in range(SIDE - 1)]
            yield
            for copy in copies:
                copy.wait_recv()
        last = send(total.at[core, i], total.at[core, i], core_peer)
        store(total.at[core, i], total_hbm.at[core, i])
        yield
        last.wait_recv()
        store(total.at[1 - core, i], total_hbm.at[1 - core, i])

    def gain_chain():
        used = [0]

        def send(src, device):
            n = used[0]
            used[0] += 1
            return go(src, gains_in.at[n], gain_send.at[n], gain_recv.at[n], device)

        copy = send(gains_acc.at[0], core_peer)
        yield
        copy.wait_recv()
        gains_acc[1] = gains_acc[0] + gains_in[0]
        for axis in range(3):
            copies = [send(gains_acc.at[axis + 1], peer) for peer in peers[axis]]
            yield
            for copy in copies:
                copy.wait_recv()
            base = 1 + 3 * axis
            summed = (gains_acc[axis + 1] + gains_in[base + 1]) + (gains_in[base] + gains_in[base + 2])
            if axis < 2:
                gains_acc[axis + 2] = summed
            else:
                gains_sum[...] = summed

    def advance(*chains):
        for link in chains:
            next(link, None)

    chains = [chain(i) for i in range(CHAINS)]

    def step(*which):
        for i in which:
            next(chains[i], None)

    for c in range(CHUNKS):
        part = pl.ds(c * 512, 512)
        pre = mm(h_m[...], w_up[:, part])
        cdf = 0.5 * (1.0 + lax.erf(pre * 0.7071067811865476))
        act = (pre * cdf).astype(BF16)
        slope = cdf + pre * jnp.exp(-0.5 * pre * pre) * 0.3989422804014327
        resid[...] += mm(act, w_down[part, :])
        grad_pre = (mm_nt(cotf[...], w_down[part, :]) * slope).astype(BF16)
        dh[...] += mm_nt(grad_pre, w_up[:, part])
        down = mm_tn(act, cotf[...]).astype(BF16)
        up = mm_tn(h_m[...], grad_pre).astype(BF16)
        for b in range(4):
            spot = slice((b % 2) * 512, (b % 2 + 1) * 512)
            cut = slice(b * LANES, (b + 1) * LANES)
            partial[0, 2 * c + b // 2, spot, :] = down[:, cut]
            partial[1, 2 * c + b // 2, spot, :] = up[:, cut]
        step(2 * c, 2 * c + 1)
        if c > 0:
            step(2 * c - 2, 2 * c - 1)
    out_f[...] = resid[...].astype(BF16)
    out_lon = halo_go(out_f, out_right, grid["left"])
    term, gain_grad_m = norm_back(dh[...], norm_m[...], scale_m, gain_m[...])
    resid[...] = cotf[...].astype(F32) + term
    grad_attn = resid[...].astype(BF16)

    def put(half, i, b, value):
        for j in range(2):
            partial[half, 8 + i, j * 512 : (j + 1) * 512, :] = value[:, b + j * LANES : b + (j + 1) * LANES]

    grad_out = mm_tn(mixed[...], grad_attn).astype(BF16)
    put(0, 0, 0, grad_out)
    put(1, 0, 256, grad_out)
    step(8, 6, 7)
    mixed[...] = mm_nt(grad_attn, w_out[...]).astype(BF16)
    step(0, 1)

    homes = {(0, 0): (0, 1), (1, 0): (1, 1), (2, 0): (0, 2), (0, 1): (1, 2), (1, 1): (0, 3), (2, 1): (1, 3)}
    pump = [[8, 2, 3], [9, 4, 5, 0, 1], [6, 7, 2, 3, 8], [10, 11, 9, 0, 1, 4, 5]]
    for p in range(HEADS // 2):
        lanes = pair_lanes(p)
        for w in range(2):
            here = window(w)
            prob = probs[w * 4 + p]
            dmix = pair_stack(mixed[here, pl.ds(p * LANES, LANES)])
            query = pair_stack(qkv[here, lanes[0]])
            dprob = mm_nt(dmix, qkv[here, lanes[2]])
            dqkv[here, lanes[2]] = mm_tn(prob.astype(BF16), dmix).astype(BF16)
            dscore = prob * (dprob - jnp.sum(dprob * prob, axis=-1, keepdims=True)) * 0.125
            dscore = dscore.astype(BF16)
            dqkv[here, lanes[0]] = pair_join(mm(dscore, qkv[here, lanes[1]])).astype(BF16)
            dqkv[here, lanes[1]] = mm_tn(dscore, query).astype(BF16)
        if p % 2 == 1:
            for c in range(3):
                half, i = homes[c, p // 2]
                cut = pl.ds(c * width + (p // 2) * 256, 256)
                put(half, i, 0, mm_tn(h_a[...], dqkv[:, cut]).astype(BF16))
        step(*pump[p])

    dframe = None
    for c in range(3):
        part = pl.ds(c * width, width)
        term = mm_nt(dqkv[:, part], w_qkv[:, part])
        dframe = term if dframe is None else dframe + term
    dframe = dframe.astype(BF16).astype(F32)
    step(10, 11, 6, 7, 2, 3)
    term, gain_grad_a = norm_back(dframe, norm_a[...], jnp.concatenate(scale_a, axis=0), gain_a[...])
    for r in range(4):
        cut = slice(r * LANES, (r + 1) * LANES)
        gains_acc[0, r : r + 1, :] = gain_grad_a[:, cut]
        gains_acc[0, r + 4 : r + 5, :] = gain_grad_m[:, cut]
    gains_link = gain_chain()
    advance(gains_link)
    tok_f[...] = (resid[...] + term).astype(BF16)
    tok_lon = halo_go(tok_f, tok_right, grid["left"])
    level, row, col = row_cells()
    col, col_out = fold(col + per_level(level, cols), WW)
    back_pair = roll_pair(level * PLANE + row * WW + col, col_out, CELLS)
    sent_rows = pl.ds(0, CELLS - LEVELS * WW)

    def turn(arrived, own, other, rolled, rolled_x):
        arrived.wait_recv()
        rolled[...] = apply_roll(back_pair, own[...], other[...])
        rolled_x[pl.ds(CELLS - LEVELS * WW, LEVELS * WW), :] = jnp.zeros((LEVELS * WW, width), BF16)
        return halo_go(rolled.at[sent_rows], rolled_x.at[sent_rows], grid["above"])

    chains.append(gains_link)
    out_lat = turn(out_lon, out_f, out_right, out_t, out_tx)
    late = (9, 10, 11)
    step(4, 5, 6, 7, 8, 0, 1, 2, 3)
    step(*late, 12)
    step(4, 5, 6, 7, 0, 1, 2, 3, 8)
    step(*late, 12)
    tok_lat = turn(tok_lon, tok_f, tok_right, tok_t, tok_tx)
    step(*late, 12, 8)
    step(4, 5, 6, 7, *late, 12)
    step(0, 1, 2, 3, 8, *late)
    step(4, 5, 6, 7, 0, 1, 2, 3)
    step(8, *late, 4, 5, 6, 7)
    for again in range(9):
        step(*range(CHAINS + 1))
    for copy in (out_lat, tok_lat):
        copy.wait_recv()
    for copy in started:
        copy.wait_send()
    for copy in stores:
        copy.wait()


def finish_kernel(
    rows, cols, total_hbm, gains, out_t, out_tx, tok_t, tok_tx,
    block_out, grad_tokens, gain_a, gain_m, grad_qkv, grad_out, grad_up, grad_down,
    total, up, down, out, qkv, in_sems, out_sems,
):
    width = gain_a.shape[1]
    loads, moves = {}, []
    for i in range(CHAINS):
        for half in range(2):
            load = pltpu.make_async_copy(total_hbm.at[half, i], total.at[half, i], in_sems.at[half, i])
            load.start()
            loads[half, i] = load

    def put(half, i, j, stage, place):
        stage[place] = total[half, i, j * 512 : (j + 1) * 512, :].astype(F32)

    def move(src, dst):
        copy = pltpu.make_async_copy(src, dst, out_sems.at[len(moves)])
        copy.start()
        moves.append(copy)

    for c in range(CHUNKS):
        here = slice(c * 512, (c + 1) * 512)
        for half in range(2):
            for s in range(2):
                loads[half, 2 * c + s].wait()
                for j in range(2):
                    cut = slice((2 * s + j) * LANES, (2 * s + j + 1) * LANES)
                    if half == 0:
                        put(half, 2 * c + s, j, down, (here, cut))
                    else:
                        first = c * 512 + (2 * s + j) * LANES
                        put(half, 2 * c + s, j, up, (slice(None), slice(first, first + LANES)))
        move(down.at[pl.ds(c * 512, 512)], grad_down.at[pl.ds(c * 512, 512)])
        move(up.at[:, pl.ds(c * 512, 512)], grad_up.at[:, pl.ds(c * 512, 512)])
    homes = {(0, 1): (0, 0), (1, 1): (1, 0), (0, 2): (2, 0), (1, 2): (0, 1), (0, 3): (1, 1), (1, 3): (2, 1)}
    for i in range(4):
        for half in range(2):
            loads[half, 8 + i].wait()
            for j in range(2):
                if i == 0:
                    first = half * 256 + j * LANES
                    put(half, 8, j, out, (slice(None), slice(first, first + LANES)))
                else:
                    c, second = homes[half, i]
                    first = c * width + second * 256 + j * LANES
                    put(half, 8 + i, j, qkv, (slice(None), slice(first, first + LANES)))
        if i == 0:
            move(out, grad_out)
    move(qkv, grad_qkv)
    level, row, col = data_cells()
    row, row_out = fold(row + per_level(level, rows), WH)
    pair = roll_pair(row * LEVELS * WW + level * WW + col, row_out, CELLS)
    for own, other, result in ((out_t, out_tx, block_out), (tok_t, tok_tx, grad_tokens)):
        result[...] = apply_roll(pair, own[...], other[...]).reshape(result.shape)
    for r in range(4):
        cut = slice(r * LANES, (r + 1) * LANES)
        gain_a[:, cut] = gains[r : r + 1, :]
        gain_m[:, cut] = gains[r + 4 : r + 5, :]
    for copy in moves:
        copy.wait()


VMEM = pl.BlockSpec(memory_space=pltpu.VMEM)
SMEM = pl.BlockSpec(memory_space=pltpu.SMEM)
ANY = pl.BlockSpec(memory_space=pl.ANY)
DMA = pltpu.SemaphoreType.DMA


def call(kernel, outs, in_specs, out_specs, scratch, name, collective_id=None):
    params = {"vmem_limit_bytes": VMEM_BYTES}
    if collective_id is not None:
        params.update(collective_id=collective_id, has_side_effects=True)
    return pl.pallas_call(
        kernel,
        out_shape=[jax.ShapeDtypeStruct(shape, dtype) for shape, dtype in outs],
        in_specs=in_specs,
        out_specs=out_specs,
        scratch_shapes=scratch,
        compiler_params=pltpu.CompilerParams(**params),
        name=name,
    )


def sum_buffers():
    shapes = [(2, CHAINS, PART, LANES), (CHAINS, PART, LANES), (CHAINS, PART, LANES)]
    for r, count in enumerate(ROUNDS):
        shapes.append((CHAINS, SIDE - 1, count, LANES))
        if r < 2:
            shapes.append((CHAINS, count, LANES))
    shapes.append((2, CHAINS, PART, LANES))
    return [pltpu.VMEM(shape, BF16) for shape in shapes]


def native(field):
    return field.transpose(1, 2, 0, 3).reshape(-1, field.shape[0], field.shape[3])


def on_device(
    tokens,
    region_ids,
    shift_lat,
    shift_lon,
    gain_attn,
    w_qkv,
    w_out,
    gain_mlp,
    w_up,
    w_down,
    cotangent,
):
    levels, lat_rows, lon_cols, width = tokens.shape
    cells = levels * lat_rows * lon_cols
    ff = w_up.shape[1]
    lines = (lat_rows * lon_cols, levels, width)
    tile = ((cells, width), BF16)
    half, full = pltpu.VMEM((cells, width), BF16), pltpu.VMEM((cells, width), F32)
    total, gains_sum, out_t, out_tx, tok_t, tok_tx = call(
        block_kernel,
        [((2, CHAINS, PART, LANES), BF16), ((8, LANES), F32)] + [tile] * 4,
        [SMEM] * 2 + [VMEM] * 5 + [ANY] * 4,
        [ANY] + [VMEM] * 5,
        [pltpu.VMEM(w.shape, BF16) for w in (w_qkv, w_out, w_up, w_down)]
        + [pltpu.VMEM(lines, BF16)] * 2
        + [half] * 4
        + [pltpu.VMEM((16, LANES), jnp.int32)] * 2
        + [
            half,
            full,
            pltpu.VMEM((cells, LANES), BF16),
            full,
            half,
            pltpu.VMEM((cells, 3 * width), BF16),
            pltpu.VMEM((HEADS, 2 * WIN, WIN), F32),
            half,
            full,
            full,
            half,
            full,
            pltpu.VMEM((cells, 3 * width), BF16),
        ]
        + [half] * 4
        + [pltpu.VMEM((4, 8, LANES), F32), pltpu.VMEM((10, 8, LANES), F32)]
        + sum_buffers()
        + [
            DMA((4,)),
            DMA((12,)),
            DMA((12,)),
            DMA((CHAINS, SEMS)),
            DMA((CHAINS, SEMS)),
            DMA((10,)),
            DMA((10,)),
            DMA((2 * CHAINS,)),
        ],
        "block",
        0,
    )(
        shift_lat, shift_lon, native(tokens), native(cotangent), region_ids,
        gain_attn.reshape(1, width), gain_mlp.reshape(1, width), w_qkv, w_out, w_up, w_down,
    )
    results = call(
        finish_kernel,
        [
            (lines, BF16),
            (lines, BF16),
            ((1, width), F32),
            ((1, width), F32),
            ((width, 3 * width), F32),
            ((width, width), F32),
            ((width, ff), F32),
            ((ff, width), F32),
        ],
        [SMEM] * 2 + [ANY] + [VMEM] * 5,
        [VMEM] * 4 + [ANY] * 4,
        [
            pltpu.VMEM((2, CHAINS, PART, LANES), BF16),
            pltpu.VMEM(w_up.shape, F32),
            pltpu.VMEM(w_down.shape, F32),
            pltpu.VMEM(w_out.shape, F32),
            pltpu.VMEM(w_qkv.shape, F32),
            DMA((2, CHAINS)),
            DMA((2 * CHUNKS + 2,)),
        ],
        "finish",
    )(shift_lat, shift_lon, total, gains_sum, out_t, out_tx, tok_t, tok_tx)
    block_out, grad_tokens, grad_gain_attn, grad_gain_mlp, grad_qkv, grad_out, grad_up, grad_down = results

    def whole(field):
        return field.reshape(lat_rows, lon_cols, levels, width).transpose(2, 0, 1, 3)

    return (
        whole(block_out),
        whole(grad_tokens),
        grad_gain_attn.reshape(width),
        grad_qkv,
        grad_out,
        grad_gain_mlp.reshape(width),
        grad_up,
        grad_down,
    )


def solution(mesh):
    placed = (
        P(None, "lat", "lon", None),
        P("lat", "lon"),
        P(),
        P(),
        P(),
        P(),
        P(),
        P(),
        P(),
        P(),
        P(None, "lat", "lon", None),
    )
    return jax.shard_map(
        on_device,
        mesh=mesh,
        in_specs=placed,
        out_specs=(
            P(None, "lat", "lon", None),
            P(None, "lat", "lon", None),
            P(),
            P(),
            P(),
            P(),
            P(),
            P(),
        ),
        check_vma=False,
    )
```

```python
import functools

import jax
import jax.numpy as jnp
from jax import lax
from jax.experimental import pallas as pl
from jax.experimental.pallas import tpu as pltpu
from jax.sharding import PartitionSpec as P

HEADS = 8
WV = 2
WH = 6
WW = 12
WIN = WV * WH * WW
PLANE = WH * WW
LANES = 128
LEVELS = 4
CELLS = LEVELS * PLANE
SIDE = 4
EPS = 1e-05
MESH = pl.DeviceIdType.MESH
F32 = jnp.float32
BF16 = jnp.bfloat16
CHUNKS = 4
FIRST_AXIS = (0, 1, 2, 1, 0, 2, 0, 1)
GAINS, OUT, TOK = 8, 9, 10
PUMP_MLP = ((), (), (0,), (1, 2))
PUMP_PAIRS = ((3, 4), (5,), (), (6, 7, 5))
PUMP_FRAME = (0, 6, 7, 1, 2)
PUMP_TAIL = (
    (5, OUT, 3, 1, 4, GAINS, 0, 7, 6, 3, 1, 2, 4, 7, GAINS, 0, 6, TOK, 3, 5, 7, 2, 1, 4, GAINS, 1, 6, 0)
    + (GAINS, 5, 0, 4, 2, 3, 4, 2, 6, 5, 3, 7, 6, 5, 7)
)
PART = 1024
QUARTER = 256
SHARE = 16
ROUNDS = 6
VMEM_BYTES = 60 * 1024 * 1024
DIMS_ZERO = (((0,), (0,)), ((), ()))
DIMS_LAST = (((1,), (1,)), ((), ()))


def mm(a, b):
    return jnp.dot(a, b, preferred_element_type=F32)


def mm_tn(a, b):
    return lax.dot_general(a, b, DIMS_ZERO, preferred_element_type=F32)


def mm_nt(a, b):
    return lax.dot_general(a, b, DIMS_LAST, preferred_element_type=F32)


def norm_stats(values):
    center = values - jnp.mean(values, axis=-1, keepdims=True)
    inv_scale = lax.rsqrt(jnp.mean(center * center, axis=-1, keepdims=True) + EPS)
    return (center * inv_scale, inv_scale)


def norm_back(grad, normed, inv_scale, gain):
    gain_grad = jnp.sum(grad * normed, axis=0, keepdims=True)
    graded = grad * gain
    term = inv_scale * (
        graded
        - jnp.mean(graded, axis=-1, keepdims=True)
        - normed * jnp.mean(graded * normed, axis=-1, keepdims=True)
    )
    return (term, gain_grad)


def places():
    lat, lon = lax.axis_index("lat"), lax.axis_index("lon")
    lats, lons = lax.axis_size("lat"), lax.axis_size("lon")
    core, y_hi = lax.rem(lat, 2), lat // 2
    x, y_lo, z = lax.rem(lon, SIDE), lax.rem(lon // SIDE, 2), lon // (2 * SIDE)
    y = y_hi * 2 + y_lo

    def device(x, y, z):
        x, y, z = lax.rem(x, SIDE), lax.rem(y, SIDE), lax.rem(z, SIDE)
        return ((y // 2) * 2 + core, z * 2 * SIDE + lax.rem(y, 2) * SIDE + x)

    spot = (x, y, z)

    def away(offset):
        return device(*[p + o for p, o in zip(spot, offset)])

    offsets = [(i, j, k) for i in range(SIDE) for j in range(SIDE) for k in range(SIDE)]
    peers = [[away([j * (a == b) for b in range(3)]) for j in range(1, SIDE)] for a in range(3)]
    planes = [[(o, away(o)) for o in offsets if o[a] == 0 and any(o)] for a in range(3)]
    known = [away(o) for o in offsets if 0 in o and any(o)]
    grid = {
        "below": (lax.rem(lat + 1, lats), lon),
        "above": (lax.rem(lat + lats - 1, lats), lon),
        "right": (lat, lax.rem(lon + 1, lons)),
        "left": (lat, lax.rem(lon + lons - 1, lons)),
    }
    return grid, core, (y_hi * 2 + 1 - core, lon), peers, planes, known, spot


def remote(src, dst, send, recv, device):
    return pltpu.make_async_remote_copy(
        src_ref=src, dst_ref=dst, send_sem=send, recv_sem=recv, device_id=device, device_id_type=MESH
    )


def div(value, by):
    return jnp.floor((value.astype(F32) + 0.5) * (1.0 / by)).astype(jnp.int32)


def frame_cells(start, count):
    cell = start + lax.broadcasted_iota(jnp.int32, (count, 1), 0)
    level = div(cell, PLANE)
    row = div(cell - level * PLANE, WW)
    return level, row, cell - level * PLANE - row * WW


def data_cells():
    cell = lax.broadcasted_iota(jnp.int32, (CELLS, 1), 0)
    spot = div(cell, LEVELS)
    row = div(spot, WW)
    return cell - spot * LEVELS, row, spot - row * WW


def row_cells():
    cell = lax.broadcasted_iota(jnp.int32, (CELLS, 1), 0)
    row = div(cell, LEVELS * WW)
    level = div(cell - row * LEVELS * WW, WW)
    return level, row, cell - row * LEVELS * WW - level * WW


def per_level(level, ref):
    value = ref[LEVELS - 1]
    for k in reversed(range(LEVELS - 1)):
        value = jnp.where(level == k, ref[k], value)
    return value


def fold(value, limit):
    out = ((value < 0) | (value >= limit)).astype(jnp.int32)
    return jnp.where(value < 0, value + limit, jnp.where(value >= limit, value - limit, value)), out


def one_hot(hit, index, width):
    lanes = lax.broadcasted_iota(jnp.int32, (index.shape[0], width), 1)
    return jnp.where((lanes == index) & hit, 1.0, 0.0).astype(BF16)


def roll_pair(index, out, width):
    return one_hot(out == 0, index, width), one_hot(out == 1, index, width)


def apply_roll(pair, here, there):
    return (mm(pair[0], here) + mm(pair[1], there)).astype(BF16)


def block_kernel(
    rows, cols, tok_in, cot_in, ids_in, gain_a, gain_m, w_qkv_hbm, w_out_hbm, w_up_hbm, w_down_hbm,
    total_a_hbm, total_b_hbm, gains_sum, out_t_hbm, out_tx_hbm, tok_t_hbm, tok_tx_hbm,
    w_qkv, w_out, w_up, w_down,
    tok_above, cot_left, tok_rows, tok_left, cot_cols, cot_above, ids, ids_x,
    cotf, tokf, labf, norm_a, h_a, qkv, probs, mixed, resid, norm_m, h_m, dh, dqkv,
    out_f, out_right, tok_f, tok_right, out_t, out_tx, tok_t, tok_tx, gains_acc, gains_in,
    part_a, core_a, mine_a, r1_a, m1_a, r2_a, total_a,
    part_b, core_b, mine_b, r1_b, m1_b, r2_b, total_b,
    load_sem, halo_send, halo_recv, sum_send, sum_recv, gain_send, gain_recv, store_sem,
):
    width = gain_a.shape[1]
    grid, core, core_peer, peers, planes, known, position = places()
    loads = [
        pltpu.make_async_copy(src, dst, load_sem.at[k])
        for k, (src, dst) in enumerate(
            ((w_qkv_hbm, w_qkv), (w_out_hbm, w_out), (w_up_hbm, w_up), (w_down_hbm, w_down))
        )
    ]
    greeted = [core_peer] + known + list(grid.values())
    barrier = pltpu.get_barrier_semaphore()
    for device in greeted:
        pl.semaphore_signal(barrier, inc=1, device_id=device, device_id_type=MESH)
    for load in loads:
        load.start()

    started = []
    stores = []

    def go(*args):
        copy = remote(*args)
        copy.start()
        started.append(copy)
        return copy

    halos = []

    def halo_go(src, dst, device):
        k = len(halos)
        halos.append(go(src, dst, halo_send.at[k], halo_recv.at[k], device))
        return halos[-1]

    def window(w):
        return pl.ds(w * WIN, WIN)

    ids[0:8, :] = jnp.zeros((8, LANES), jnp.int32)
    ids[0:WH, 0:WW] = ids_in[...]
    tok_above[0:WW] = jnp.zeros((WW, LEVELS, width), BF16)
    cot_left[:, 0:1] = jnp.zeros((WH, 1, LEVELS, width), BF16)
    line = LEVELS * WW
    cot_above[0:line, :] = jnp.zeros((line, width), BF16)
    used_rows, used_cols, used_lines = pl.ds(WW, PLANE - WW), pl.ds(1, WW - 1), pl.ds(line, CELLS - line)
    pl.semaphore_wait(barrier, len(greeted))
    lat_tok = halo_go(tok_in.at[used_rows], tok_above.at[used_rows], grid["below"])
    lat_ids = halo_go(ids.at[pl.ds(0, 8)], ids.at[pl.ds(8, 8)], grid["below"])
    lon_cot = halo_go(cot_in.at[:, used_cols], cot_left.at[:, used_cols], grid["right"])
    level, row, col = row_cells()
    col, col_out = fold(col - per_level(level, cols), WW)
    first_pair = roll_pair((row * WW + col) * LEVELS + level, col_out, CELLS)
    level, row, col = frame_cells(0, CELLS)
    row, row_out = fold(row - per_level(level, rows), WH)
    second_pair = roll_pair(row * line + level * WW + col, row_out, CELLS)
    level, row, col = frame_cells(0, CELLS)
    row, row_out = fold(row - per_level(level, rows), WH)
    row_pair = roll_pair((row * WW + col) * LEVELS + level, row_out, CELLS)
    level, row, col = frame_cells(0, CELLS)
    col, col_out = fold(col - per_level(level, cols), WW)
    col_index = lax.rem(level, WV) * PLANE + row * WW + col
    col_pairs = [
        roll_pair(col_index[w * WIN : (w + 1) * WIN], col_out[w * WIN : (w + 1) * WIN], WIN) for w in range(2)
    ]
    lat_tok.wait_recv()
    tok_rows[...] = apply_roll(
        row_pair, tok_in[...].reshape(CELLS, width), tok_above[...].reshape(CELLS, width)
    )
    lon_tok = [halo_go(tok_rows.at[window(w)], tok_left.at[window(w)], grid["right"]) for w in range(2)]
    lat_ids.wait_recv()
    lon_ids = halo_go(ids, ids_x, grid["right"])
    lon_cot.wait_recv()
    cot_cols[...] = apply_roll(
        first_pair, cot_in[...].reshape(CELLS, width), cot_left[...].reshape(CELLS, width)
    )
    lat_cot = halo_go(cot_cols.at[used_lines], cot_above.at[used_lines], grid["below"])

    lon_ids.wait_recv()
    ids_all = jnp.concatenate([ids[...], ids_x[...]], axis=0).astype(F32).astype(BF16)
    level, row, col = frame_cells(0, CELLS)
    row, row_out = fold(row - per_level(level, rows), WH)
    col, col_out = fold(col - per_level(level, cols), WW)
    picked = mm(one_hot(level >= 0, (row_out + 2 * col_out) * 8 + row, 32), ids_all)
    lanes = lax.broadcasted_iota(jnp.int32, (CELLS, LANES), 1)
    label = jnp.sum(jnp.where(lanes == col, picked, 0.0), axis=-1, keepdims=True)
    labf[...] = jnp.where(lanes.astype(F32) == label, 1.0, 0.0).astype(BF16)
    scale_a = []

    def forward_in(w):
        here = window(w)
        lon_tok[w].wait_recv()
        values = apply_roll(col_pairs[w], tok_rows[here, :], tok_left[here, :]).astype(F32)
        tokf[here, :] = values
        normed, scale = norm_stats(values)
        scale_a.append(scale)
        norm_a[here, :] = normed
        h_a[here, :] = (normed * gain_a[...]).astype(BF16)
        if w == 0:
            loads[0].wait()
        for c in range(3):
            part = pl.ds(c * width, width)
            qkv[here, part] = mm(h_a[here, :], w_qkv[:, part]).astype(BF16)

    low = lax.broadcasted_iota(jnp.int32, (1, LANES), 1) < LANES // 2

    def pair_stack(block):
        zero = jnp.zeros_like(block)
        return jnp.concatenate([jnp.where(low, block, zero), jnp.where(low, zero, block)], axis=0)

    def pair_join(stack):
        return jnp.where(low, stack[:WIN], stack[WIN:])

    def pair_lanes(p):
        return [pl.ds(part * width + p * LANES, LANES) for part in range(3)]

    for w in range(2):
        here = window(w)
        forward_in(w)
        allowed = mm_nt(labf[here, :], labf[here, :]) > 0.5
        allowed = jnp.concatenate([allowed, allowed], axis=0)
        for p in range(HEADS // 2):
            lanes = pair_lanes(p)
            query = pair_stack(qkv[here, lanes[0]])
            scores = mm_nt(query, qkv[here, lanes[1]]) * 0.125
            scores = jnp.where(allowed, scores, -jnp.inf)
            expo = jnp.exp(scores - jnp.max(scores, axis=-1, keepdims=True))
            prob = expo * (1.0 / jnp.sum(expo, axis=-1, keepdims=True))
            probs[w * 4 + p] = prob
            mixed[here, pl.ds(p * LANES, LANES)] = pair_join(
                mm(prob.astype(BF16), qkv[here, lanes[2]])
            ).astype(BF16)

    for load in loads[1:]:
        load.wait()
    attn = mm(mixed[...], w_out[...]).astype(BF16).astype(F32)
    resid[...] = tokf[...] + attn
    normed, scale_m = norm_stats(resid[...])
    norm_m[...] = normed
    h_m[...] = (normed * gain_m[...]).astype(BF16)
    dh[...] = jnp.zeros_like(dh)
    lat_cot.wait_recv()
    cotf[...] = apply_roll(second_pair, cot_cols[...], cot_above[...])

    set_a = (part_a, core_a, mine_a, r1_a, m1_a, r2_a, total_a, total_a_hbm)
    set_b = (part_b, core_b, mine_b, r1_b, m1_b, r2_b, total_b, total_b_hbm)
    sent = []

    def block(offset, count):
        return pl.ds(pl.multiple_of(offset, 16), count)

    def store(src, dst):
        copy = pltpu.make_async_copy(src, dst, store_sem.at[len(stores)])
        copy.start()
        stores.append(copy)

    def chain(refs, i, k):
        partial, core_in, mine, r1, m1, r2, total, total_hbm = refs
        axis = FIRST_AXIS[k]
        plane = planes[axis]
        at = position[axis]
        rest = [a for a in range(3) if a != axis]

        def share(offset):
            first, second = [lax.rem(position[a] + offset[a], SIDE) for a in rest]
            return (first * SIDE + second) * SHARE

        def send(n, src, dst, device):
            remote(src, dst, sum_send.at[k, n], sum_recv.at[k, n], device).start()

        def arrive(n, like):
            whole = remote(like, like, sum_send.at[k, n], sum_recv.at[k, n], core_peer)
            sent.append(whole)
            whole.wait_recv()

        send(0, partial.at[1 - core, i], core_in.at[i], core_peer)
        yield
        arrive(0, core_in.at[i])
        mine[i] = (partial[core, i].astype(F32) + core_in[i].astype(F32)).astype(BF16)
        for j in range(1, SIDE):
            quarter = block(lax.rem(at + j, SIDE) * QUARTER, QUARTER)
            send(1, mine.at[i, quarter], r1.at[i, j - 1], peers[axis][j - 1])
        yield
        arrive(1, r1.at[i])
        summed = mine[i, block(at * QUARTER, QUARTER), :].astype(F32)
        for j in range(SIDE - 1):
            summed = summed + r1[i, j].astype(F32)
        m1[i] = summed.astype(BF16)
        for n, (offset, device) in enumerate(plane):
            send(2, m1.at[i, block(share(offset), SHARE)], r2.at[i, n], device)
        yield
        arrive(2, r2.at[i])
        own = share((0, 0, 0))
        summed = m1[i, block(own, SHARE), :].astype(F32) + jnp.sum(r2[i].astype(F32), axis=0)
        place = (core, i, block(at * QUARTER + own, SHARE))
        total[place] = summed.astype(BF16)
        for offset, device in plane:
            send(3, total.at[place], total.at[place], device)
        yield
        arrive(3, r2.at[i])
        place = (core, i, block(at * QUARTER, QUARTER))
        for device in peers[axis]:
            send(4, total.at[place], total.at[place], device)
        yield
        arrive(4, r1.at[i])
        send(5, total.at[core, i], total.at[core, i], core_peer)
        store(total.at[core, i], total_hbm.at[core, i])
        yield
        arrive(5, core_in.at[i])
        store(total.at[1 - core, i], total_hbm.at[1 - core, i])

    def gain_chain():
        used = [0]

        def send(src, device):
            n = used[0]
            used[0] += 1
            return go(src, gains_in.at[n], gain_send.at[n], gain_recv.at[n], device)

        copy = send(gains_acc.at[0], core_peer)
        yield
        copy.wait_recv()
        gains_acc[1] = gains_acc[0] + gains_in[0]
        for axis in range(3):
            copies = [send(gains_acc.at[axis + 1], peer) for peer in peers[axis]]
            yield
            for copy in copies:
                copy.wait_recv()
            base = 1 + 3 * axis
            summed = (gains_acc[axis + 1] + gains_in[base + 1]) + (gains_in[base] + gains_in[base + 2])
            if axis < 2:
                gains_acc[axis + 2] = summed
            else:
                gains_sum[...] = summed

    def advance(*chains):
        for link in chains:
            next(link, None)

    chains = [chain(set_a, i, i) for i in range(CHUNKS)]
    chains += [chain(set_b, i, CHUNKS + i) for i in range(CHUNKS)]

    def step(*which):
        for i in which:
            next(chains[i], None)

    for c in range(CHUNKS):
        part = pl.ds(c * 512, 512)
        pre = mm(h_m[...], w_up[:, part])
        cdf = 0.5 * (1.0 + lax.erf(pre * 0.7071067811865476))
        act = (pre * cdf).astype(BF16)
        slope = cdf + pre * jnp.exp(-0.5 * pre * pre) * 0.3989422804014327
        resid[...] += mm(act, w_down[part, :])
        grad_pre = (mm_nt(cotf[...], w_down[part, :]) * slope).astype(BF16)
        dh[...] += mm_nt(grad_pre, w_up[:, part])
        down = mm_tn(act, cotf[...]).astype(BF16)
        up = mm_tn(h_m[...], grad_pre).astype(BF16)
        for b in range(2):
            spot = slice(b * 512, (b + 1) * 512)
            cut = slice(b * 256, (b + 1) * 256)
            part_a[0, c, spot, :] = down[:, cut]
            part_a[1, c, spot, :] = up[:, cut]
        step(c, *PUMP_MLP[c])
    out_f[...] = resid[...].astype(BF16)
    out_lon = halo_go(out_f, out_right, grid["left"])
    term, gain_grad_m = norm_back(dh[...], norm_m[...], scale_m, gain_m[...])
    resid[...] = cotf[...].astype(F32) + term
    grad_attn = resid[...].astype(BF16)

    def put(half, i, b, value):
        for j in range(2):
            part_b[half, i, j * 512 : (j + 1) * 512, :] = value[:, b + j * LANES : b + (j + 1) * LANES]

    grad_out = mm_tn(mixed[...], grad_attn).astype(BF16)
    put(0, 0, 0, grad_out)
    put(1, 0, 256, grad_out)
    step(4)
    mixed[...] = mm_nt(grad_attn, w_out[...]).astype(BF16)

    homes = {(0, 0): (0, 1), (1, 0): (1, 1), (2, 0): (0, 2), (0, 1): (1, 2), (1, 1): (0, 3), (2, 1): (1, 3)}
    for p in range(HEADS // 2):
        lanes = pair_lanes(p)
        for w in range(2):
            here = window(w)
            prob = probs[w * 4 + p]
            dmix = pair_stack(mixed[here, pl.ds(p * LANES, LANES)])
            query = pair_stack(qkv[here, lanes[0]])
            dprob = mm_nt(dmix, qkv[here, lanes[2]])
            dqkv[here, lanes[2]] = mm_tn(prob.astype(BF16), dmix).astype(BF16)
            dscore = prob * (dprob - jnp.sum(dprob * prob, axis=-1, keepdims=True)) * 0.125
            dscore = dscore.astype(BF16)
            dqkv[here, lanes[0]] = pair_join(mm(dscore, qkv[here, lanes[1]])).astype(BF16)
            dqkv[here, lanes[1]] = mm_tn(dscore, query).astype(BF16)
        if p % 2 == 1:
            for c in range(3):
                half, i = homes[c, p // 2]
                cut = pl.ds(c * width + (p // 2) * 256, 256)
                put(half, i, 0, mm_tn(h_a[...], dqkv[:, cut]).astype(BF16))
        step(*PUMP_PAIRS[p])

    dframe = None
    for c in range(3):
        part = pl.ds(c * width, width)
        term = mm_nt(dqkv[:, part], w_qkv[:, part])
        dframe = term if dframe is None else dframe + term
    dframe = dframe.astype(BF16).astype(F32)
    step(*PUMP_FRAME)
    term, gain_grad_a = norm_back(dframe, norm_a[...], jnp.concatenate(scale_a, axis=0), gain_a[...])
    for r in range(4):
        cut = slice(r * LANES, (r + 1) * LANES)
        gains_acc[0, r : r + 1, :] = gain_grad_a[:, cut]
        gains_acc[0, r + 4 : r + 5, :] = gain_grad_m[:, cut]
    gains_link = gain_chain()
    advance(gains_link)
    tok_f[...] = (resid[...] + term).astype(BF16)
    tok_lon = halo_go(tok_f, tok_right, grid["left"])
    level, row, col = row_cells()
    col, col_out = fold(col + per_level(level, cols), WW)
    back_pair = roll_pair(level * PLANE + row * WW + col, col_out, CELLS)
    sent_rows = pl.ds(0, CELLS - LEVELS * WW)

    def turn(arrived, own, other, rolled, rolled_x, rolled_hbm):
        arrived.wait_recv()
        rolled[...] = apply_roll(back_pair, own[...], other[...])
        rolled_x[pl.ds(CELLS - LEVELS * WW, LEVELS * WW), :] = jnp.zeros((LEVELS * WW, width), BF16)
        store(rolled, rolled_hbm)
        return halo_go(rolled.at[sent_rows], rolled_x.at[sent_rows], grid["above"])

    chains.append(gains_link)
    lat_back = []

    def out_back():
        lat_back.append(turn(out_lon, out_f, out_right, out_t, out_tx, out_t_hbm))
        yield

    def tok_back():
        lat_back.append(turn(tok_lon, tok_f, tok_right, tok_t, tok_tx, tok_t_hbm))
        yield

    chains.extend((out_back(), tok_back()))
    step(*PUMP_TAIL)
    for again in range(ROUNDS):
        step(*range(CHUNKS * 2 + 1))
    for copy, rolled_x, rolled_hbm in zip(lat_back, (out_tx, tok_tx), (out_tx_hbm, tok_tx_hbm)):
        copy.wait_recv()
        store(rolled_x, rolled_hbm)
    for copy in sent:
        copy.wait_send()
    for copy in started:
        copy.wait_send()
    for copy in stores:
        copy.wait()


def finish_kernel(
    rows, cols, total_a_hbm, total_b_hbm, gains, out_t_hbm, out_tx_hbm, tok_t_hbm, tok_tx_hbm,
    block_out, grad_tokens, gain_a, gain_m, grad_qkv, grad_out, grad_up, grad_down,
    total_a, total_b, up, down, out, qkv, tiles, results, in_sems, tile_sems, out_sems,
):
    width = gain_a.shape[1]
    loads, moves = {}, []
    for i in range(CHUNKS):
        for kind, (src, dst) in enumerate(((total_a_hbm, total_a), (total_b_hbm, total_b))):
            for half in range(2):
                load = pltpu.make_async_copy(src.at[half, i], dst.at[half, i], in_sems.at[kind, half, i])
                load.start()
                loads[kind, half, i] = load
    tile_loads = [
        pltpu.make_async_copy(src, tiles.at[n], tile_sems.at[n])
        for n, src in enumerate((out_t_hbm, out_tx_hbm, tok_t_hbm, tok_tx_hbm))
    ]
    for load in tile_loads:
        load.start()

    def move(src, dst):
        copy = pltpu.make_async_copy(src, dst, out_sems.at[len(moves)])
        copy.start()
        moves.append(copy)

    homes = {(0, 1): (0, 0), (1, 1): (1, 0), (0, 2): (2, 0), (1, 2): (0, 1), (0, 3): (1, 1), (1, 3): (2, 1)}
    for i in range(CHUNKS):
        here = slice(i * 512, (i + 1) * 512)
        for half in range(2):
            loads[0, half, i].wait()
            for b in range(2):
                value = total_a[half, i, b * 512 : (b + 1) * 512, :].astype(F32)
                if half == 0:
                    down[here, b * 256 : (b + 1) * 256] = value
                else:
                    up[:, i * 512 + b * 256 : i * 512 + (b + 1) * 256] = value
        move(down.at[pl.ds(i * 512, 512)], grad_down.at[pl.ds(i * 512, 512)])
        move(up.at[:, pl.ds(i * 512, 512)], grad_up.at[:, pl.ds(i * 512, 512)])
        for half in range(2):
            loads[1, half, i].wait()
            for j in range(2):
                value = total_b[half, i, j * 512 : (j + 1) * 512, :].astype(F32)
                if i == 0:
                    first = half * 256 + j * LANES
                    out[:, first : first + LANES] = value
                else:
                    c, second = homes[half, i]
                    first = c * width + second * 256 + j * LANES
                    qkv[:, first : first + LANES] = value
        if i == 0:
            move(out, grad_out)
    move(qkv, grad_qkv)
    level, row, col = data_cells()
    row, row_out = fold(row + per_level(level, rows), WH)
    pair = roll_pair(row * LEVELS * WW + level * WW + col, row_out, CELLS)
    for load in tile_loads:
        load.wait()
    for n, result in enumerate((block_out, grad_tokens)):
        results[n] = apply_roll(pair, tiles[2 * n], tiles[2 * n + 1]).reshape(result.shape)
        move(results.at[n], result)
    for r in range(4):
        cut = slice(r * LANES, (r + 1) * LANES)
        gain_a[:, cut] = gains[r : r + 1, :]
        gain_m[:, cut] = gains[r + 4 : r + 5, :]
    for copy in moves:
        copy.wait()


VMEM = pl.BlockSpec(memory_space=pltpu.VMEM)
SMEM = pl.BlockSpec(memory_space=pltpu.SMEM)
ANY = pl.BlockSpec(memory_space=pl.ANY)
DMA = pltpu.SemaphoreType.DMA


def call(kernel, outs, in_specs, out_specs, scratch, name, collective_id=None):
    params = {"vmem_limit_bytes": VMEM_BYTES}
    if collective_id is not None:
        params.update(collective_id=collective_id, has_side_effects=True)
    return pl.pallas_call(
        kernel,
        out_shape=[jax.ShapeDtypeStruct(shape, dtype) for shape, dtype in outs],
        in_specs=in_specs,
        out_specs=out_specs,
        scratch_shapes=scratch,
        compiler_params=pltpu.CompilerParams(**params),
        name=name,
    )


def sum_buffers(lanes):
    shapes = [
        (2, CHUNKS, PART, lanes),
        (CHUNKS, PART, lanes),
        (CHUNKS, PART, lanes),
        (CHUNKS, SIDE - 1, QUARTER, lanes),
        (CHUNKS, QUARTER, lanes),
        (CHUNKS, SIDE * SIDE - 1, SHARE, lanes),
        (2, CHUNKS, PART, lanes),
    ]
    return [pltpu.VMEM(shape, BF16) for shape in shapes]


def native(field):
    return field.transpose(1, 2, 0, 3).reshape(-1, field.shape[0], field.shape[3])


def on_device(
    tokens,
    region_ids,
    shift_lat,
    shift_lon,
    gain_attn,
    w_qkv,
    w_out,
    gain_mlp,
    w_up,
    w_down,
    cotangent,
):
    levels, lat_rows, lon_cols, width = tokens.shape
    cells = levels * lat_rows * lon_cols
    ff = w_up.shape[1]
    lines = (lat_rows * lon_cols, levels, width)
    tile = ((cells, width), BF16)
    half, full = pltpu.VMEM((cells, width), BF16), pltpu.VMEM((cells, width), F32)
    total_a, total_b, gains_sum, *rolled = call(
        block_kernel,
        [((2, CHUNKS, PART, 256), BF16), ((2, CHUNKS, PART, LANES), BF16), ((8, LANES), F32)] + [tile] * 4,
        [SMEM] * 2 + [VMEM] * 5 + [ANY] * 4,
        [ANY] * 2 + [VMEM] + [ANY] * 4,
        [pltpu.VMEM(w.shape, BF16) for w in (w_qkv, w_out, w_up, w_down)]
        + [pltpu.VMEM(lines, BF16), pltpu.VMEM((lat_rows, lon_cols, levels, width), BF16)]
        + [half] * 4
        + [pltpu.VMEM((16, LANES), jnp.int32)] * 2
        + [
            half,
            full,
            pltpu.VMEM((cells, LANES), BF16),
            full,
            half,
            pltpu.VMEM((cells, 3 * width), BF16),
            pltpu.VMEM((HEADS, 2 * WIN, WIN), F32),
            half,
            full,
            full,
            half,
            full,
            pltpu.VMEM((cells, 3 * width), BF16),
        ]
        + [half] * 8
        + [pltpu.VMEM((4, 8, LANES), F32), pltpu.VMEM((10, 8, LANES), F32)]
        + sum_buffers(256)
        + sum_buffers(LANES)
        + [
            DMA((4,)),
            DMA((11,)),
            DMA((11,)),
            DMA((2 * CHUNKS, ROUNDS)),
            DMA((2 * CHUNKS, ROUNDS)),
            DMA((10,)),
            DMA((10,)),
            DMA((4 * CHUNKS + 4,)),
        ],
        "block",
        0,
    )(
        shift_lat, shift_lon, native(tokens), cotangent.transpose(1, 2, 0, 3), region_ids,
        gain_attn.reshape(1, width), gain_mlp.reshape(1, width), w_qkv, w_out, w_up, w_down,
    )
    results = call(
        finish_kernel,
        [
            (lines, BF16),
            (lines, BF16),
            ((1, width), F32),
            ((1, width), F32),
            ((width, 3 * width), F32),
            ((width, width), F32),
            ((width, ff), F32),
            ((ff, width), F32),
        ],
        [SMEM] * 2 + [ANY] * 2 + [VMEM] + [ANY] * 4,
        [ANY] * 2 + [VMEM] * 2 + [ANY] * 4,
        [
            pltpu.VMEM((2, CHUNKS, PART, 256), BF16),
            pltpu.VMEM((2, CHUNKS, PART, LANES), BF16),
            pltpu.VMEM(w_up.shape, F32),
            pltpu.VMEM(w_down.shape, F32),
            pltpu.VMEM(w_out.shape, F32),
            pltpu.VMEM(w_qkv.shape, F32),
            pltpu.VMEM((4, cells, width), BF16),
            pltpu.VMEM((2,) + lines, BF16),
            DMA((2, 2, CHUNKS)),
            DMA((4,)),
            DMA((2 * CHUNKS + 4,)),
        ],
        "finish",
    )(shift_lat, shift_lon, total_a, total_b, gains_sum, *rolled)
    block_out, grad_tokens, grad_gain_attn, grad_gain_mlp, grad_qkv, grad_out, grad_up, grad_down = results

    def whole(field):
        return field.reshape(lat_rows, lon_cols, levels, width).transpose(2, 0, 1, 3)

    return (
        whole(block_out),
        whole(grad_tokens),
        grad_gain_attn.reshape(width),
        grad_qkv,
        grad_out,
        grad_gain_mlp.reshape(width),
        grad_up,
        grad_down,
    )


def solution(mesh):
    placed = (
        P(None, "lat", "lon", None),
        P("lat", "lon"),
        P(),
        P(),
        P(),
        P(),
        P(),
        P(),
        P(),
        P(),
        P(None, "lat", "lon", None),
    )
    return jax.shard_map(
        on_device,
        mesh=mesh,
        in_specs=placed,
        out_specs=(
            P(None, "lat", "lon", None),
            P(None, "lat", "lon", None),
            P(),
            P(),
            P(),
            P(),
            P(),
            P(),
        ),
        check_vma=False,
    )
```

```python
import functools

import jax
import jax.numpy as jnp
from jax import lax
from jax.experimental import pallas as pl
from jax.experimental.pallas import tpu as pltpu
from jax.sharding import PartitionSpec as P

HEADS = 8
WV = 2
WH = 6
WW = 12
WIN = WV * WH * WW
PLANE = WH * WW
LANES = 128
LEVELS = 4
CELLS = LEVELS * PLANE
SIDE = 4
EPS = 1e-05
MESH = pl.DeviceIdType.MESH
F32 = jnp.float32
BF16 = jnp.bfloat16
CHUNKS = 4
FIRST_AXIS = (1, 2, 1, 0, 2, 1, 2, 2)
GAINS, OUT, TOK = 8, 9, 10
PUMP_MLP = ((0,), (1,), (2, 0), (3, 1, 2))
PUMP_OUT, PUMP_MIX = (4, 3), ()
PUMP_PAIRS = ((4,), (5,), (), (6, 7, 5, 0, 9, 6, 7, 1))
PUMP_FRAME = ()
PUMP_TAIL = (4, 8, 2, 3, 0, 5, 6, 1, 7, 10, 8, 3, 2, 4, 0, 6, 5, 1, 8, 7, 2, 4, 3, 6, 5, 7, 0, 8, 1, 0, 1, 4, 3, 2, 4, 6, 3, 5, 2, 6, 7, 5, 7)
PART = 1024
QUARTER = 256
SHARE = 16
ROUNDS = 6
VMEM_BYTES = 60 * 1024 * 1024
DIMS_ZERO = (((0,), (0,)), ((), ()))
DIMS_LAST = (((1,), (1,)), ((), ()))


def mm(a, b):
    return jnp.dot(a, b, preferred_element_type=F32)


def mm_tn(a, b):
    return lax.dot_general(a, b, DIMS_ZERO, preferred_element_type=F32)


def mm_nt(a, b):
    return lax.dot_general(a, b, DIMS_LAST, preferred_element_type=F32)


def norm_stats(values):
    center = values - jnp.mean(values, axis=-1, keepdims=True)
    inv_scale = lax.rsqrt(jnp.mean(center * center, axis=-1, keepdims=True) + EPS)
    return (center * inv_scale, inv_scale)


def norm_back(grad, normed, inv_scale, gain):
    gain_grad = jnp.sum(grad * normed, axis=0, keepdims=True)
    graded = grad * gain
    term = inv_scale * (
        graded
        - jnp.mean(graded, axis=-1, keepdims=True)
        - normed * jnp.mean(graded * normed, axis=-1, keepdims=True)
    )
    return (term, gain_grad)


def places():
    lat, lon = lax.axis_index("lat"), lax.axis_index("lon")
    lats, lons = lax.axis_size("lat"), lax.axis_size("lon")
    core, y_hi = lax.rem(lat, 2), lat // 2
    x, y_lo, z = lax.rem(lon, SIDE), lax.rem(lon // SIDE, 2), lon // (2 * SIDE)
    y = y_hi * 2 + y_lo

    def device(x, y, z):
        x, y, z = lax.rem(x, SIDE), lax.rem(y, SIDE), lax.rem(z, SIDE)
        return ((y // 2) * 2 + core, z * 2 * SIDE + lax.rem(y, 2) * SIDE + x)

    spot = (x, y, z)

    def away(offset):
        return device(*[p + o for p, o in zip(spot, offset)])

    offsets = [(i, j, k) for i in range(SIDE) for j in range(SIDE) for k in range(SIDE)]
    peers = [[away([j * (a == b) for b in range(3)]) for j in range(1, SIDE)] for a in range(3)]
    planes = [[(o, away(o)) for o in offsets if o[a] == 0 and any(o)] for a in range(3)]
    known = [away(o) for o in offsets if 0 in o and any(o)]
    grid = {
        "below": (lax.rem(lat + 1, lats), lon),
        "above": (lax.rem(lat + lats - 1, lats), lon),
        "right": (lat, lax.rem(lon + 1, lons)),
        "left": (lat, lax.rem(lon + lons - 1, lons)),
    }
    return grid, core, (y_hi * 2 + 1 - core, lon), peers, planes, known, spot


def remote(src, dst, send, recv, device):
    return pltpu.make_async_remote_copy(
        src_ref=src, dst_ref=dst, send_sem=send, recv_sem=recv, device_id=device, device_id_type=MESH
    )


def div(value, by):
    return jnp.floor((value.astype(F32) + 0.5) * (1.0 / by)).astype(jnp.int32)


def frame_cells(start, count):
    cell = start + lax.broadcasted_iota(jnp.int32, (count, 1), 0)
    level = div(cell, PLANE)
    row = div(cell - level * PLANE, WW)
    return level, row, cell - level * PLANE - row * WW


def data_cells():
    cell = lax.broadcasted_iota(jnp.int32, (CELLS, 1), 0)
    spot = div(cell, LEVELS)
    row = div(spot, WW)
    return cell - spot * LEVELS, row, spot - row * WW


def row_cells():
    cell = lax.broadcasted_iota(jnp.int32, (CELLS, 1), 0)
    row = div(cell, LEVELS * WW)
    level = div(cell - row * LEVELS * WW, WW)
    return level, row, cell - row * LEVELS * WW - level * WW


def per_level(level, ref):
    value = ref[LEVELS - 1]
    for k in reversed(range(LEVELS - 1)):
        value = jnp.where(level == k, ref[k], value)
    return value


def fold(value, limit):
    out = ((value < 0) | (value >= limit)).astype(jnp.int32)
    return jnp.where(value < 0, value + limit, jnp.where(value >= limit, value - limit, value)), out


def one_hot(hit, index, width):
    lanes = lax.broadcasted_iota(jnp.int32, (index.shape[0], width), 1)
    return jnp.where((lanes == index) & hit, 1.0, 0.0).astype(BF16)


def roll_pair(index, out, width):
    return one_hot(out == 0, index, width), one_hot(out == 1, index, width)


def apply_roll(pair, here, there):
    return (mm(pair[0], here) + mm(pair[1], there)).astype(BF16)


def block_kernel(
    rows, cols, tok_in, cot_in, ids_in, gain_a, gain_m, w_qkv_hbm, w_out_hbm, w_up_hbm, w_down_hbm,
    total_a_hbm, total_b_hbm, gains_sum, out_t_hbm, out_tx_hbm, tok_t_hbm, tok_tx_hbm,
    w_qkv, w_out, w_up, w_down,
    tok_above, cot_left, tok_rows, tok_left, cot_cols, cot_above, ids, ids_x,
    cotf, tokf, labf, norm_a, h_a, qkv, probs, mixed, resid, norm_m, h_m, dh, dqkv,
    out_f, out_right, tok_f, tok_right, out_t, out_tx, tok_t, tok_tx, gains_acc, gains_in,
    part_a, core_a, mine_a, r1_a, m1_a, r2_a, total_a,
    part_b, core_b, mine_b, r1_b, m1_b, r2_b, total_b,
    load_sem, halo_send, halo_recv, sum_send, sum_recv, gain_send, gain_recv, store_sem,
):
    width = gain_a.shape[1]
    grid, core, core_peer, peers, planes, known, position = places()
    loads = [
        pltpu.make_async_copy(src, dst, load_sem.at[k])
        for k, (src, dst) in enumerate(
            ((w_qkv_hbm, w_qkv), (w_out_hbm, w_out), (w_up_hbm, w_up), (w_down_hbm, w_down))
        )
    ]
    greeted = [core_peer] + known + list(grid.values())
    barrier = pltpu.get_barrier_semaphore()
    for device in greeted:
        pl.semaphore_signal(barrier, inc=1, device_id=device, device_id_type=MESH)
    for load in loads:
        load.start()

    started = []
    stores = []

    def go(*args):
        copy = remote(*args)
        copy.start()
        started.append(copy)
        return copy

    halos = []

    def halo_go(src, dst, device):
        k = len(halos)
        halos.append(go(src, dst, halo_send.at[k], halo_recv.at[k], device))
        return halos[-1]

    def halo_split(src, dst, device, start, count, pieces):
        size = count // pieces
        cuts = [pl.ds(start + n * size, size) for n in range(pieces)]
        return [halo_go(src.at[cut], dst.at[cut], device) for cut in cuts]

    def arrived(copies):
        for copy in copies:
            copy.wait_recv()

    def window(w):
        return pl.ds(w * WIN, WIN)

    ids[0:8, :] = jnp.zeros((8, LANES), jnp.int32)
    ids[0:WH, 0:WW] = ids_in[...]
    tok_above[0:WW] = jnp.zeros((WW, LEVELS, width), BF16)
    cot_left[:, 0:1] = jnp.zeros((WH, 1, LEVELS, width), BF16)
    line = LEVELS * WW
    cot_above[0:line, :] = jnp.zeros((line, width), BF16)
    used_cols = pl.ds(1, WW - 1)
    pl.semaphore_wait(barrier, len(greeted))
    lat_tok = halo_split(tok_in, tok_above, grid["below"], WW, PLANE - WW, 4)
    lat_ids = halo_go(ids.at[pl.ds(0, 8)], ids.at[pl.ds(8, 8)], grid["below"])
    lon_cot = halo_go(cot_in.at[:, used_cols], cot_left.at[:, used_cols], grid["right"])
    level, row, col = row_cells()
    col, col_out = fold(col - per_level(level, cols), WW)
    first_pair = roll_pair((row * WW + col) * LEVELS + level, col_out, CELLS)
    level, row, col = frame_cells(0, CELLS)
    row, row_out = fold(row - per_level(level, rows), WH)
    second_pair = roll_pair(row * line + level * WW + col, row_out, CELLS)
    level, row, col = frame_cells(0, CELLS)
    row, row_out = fold(row - per_level(level, rows), WH)
    row_pair = roll_pair((row * WW + col) * LEVELS + level, row_out, CELLS)
    level, row, col = frame_cells(0, CELLS)
    col, col_out = fold(col - per_level(level, cols), WW)
    col_index = lax.rem(level, WV) * PLANE + row * WW + col
    col_pairs = [
        roll_pair(col_index[w * WIN : (w + 1) * WIN], col_out[w * WIN : (w + 1) * WIN], WIN) for w in range(2)
    ]
    arrived(lat_tok)
    tok_rows[...] = apply_roll(
        row_pair, tok_in[...].reshape(CELLS, width), tok_above[...].reshape(CELLS, width)
    )
    lon_tok = [halo_go(tok_rows.at[window(w)], tok_left.at[window(w)], grid["right"]) for w in range(2)]
    lat_ids.wait_recv()
    lon_ids = halo_go(ids, ids_x, grid["right"])
    lon_cot.wait_recv()
    cot_cols[...] = apply_roll(
        first_pair, cot_in[...].reshape(CELLS, width), cot_left[...].reshape(CELLS, width)
    )
    lat_cot = halo_split(cot_cols, cot_above, grid["below"], line, CELLS - line, 3)

    lon_ids.wait_recv()
    ids_all = jnp.concatenate([ids[...], ids_x[...]], axis=0).astype(F32).astype(BF16)
    level, row, col = frame_cells(0, CELLS)
    row, row_out = fold(row - per_level(level, rows), WH)
    col, col_out = fold(col - per_level(level, cols), WW)
    picked = mm(one_hot(level >= 0, (row_out + 2 * col_out) * 8 + row, 32), ids_all)
    lanes = lax.broadcasted_iota(jnp.int32, (CELLS, LANES), 1)
    label = jnp.sum(jnp.where(lanes == col, picked, 0.0), axis=-1, keepdims=True)
    labf[...] = jnp.where(lanes.astype(F32) == label, 1.0, 0.0).astype(BF16)
    scale_a = []

    def forward_in(w):
        here = window(w)
        lon_tok[w].wait_recv()
        values = apply_roll(col_pairs[w], tok_rows[here, :], tok_left[here, :]).astype(F32)
        tokf[here, :] = values
        normed, scale = norm_stats(values)
        scale_a.append(scale)
        norm_a[here, :] = normed
        h_a[here, :] = (normed * gain_a[...]).astype(BF16)
        if w == 0:
            loads[0].wait()
        for c in range(3):
            part = pl.ds(c * width, width)
            qkv[here, part] = mm(h_a[here, :], w_qkv[:, part]).astype(BF16)

    low = lax.broadcasted_iota(jnp.int32, (1, LANES), 1) < LANES // 2

    def pair_stack(block):
        zero = jnp.zeros_like(block)
        return jnp.concatenate([jnp.where(low, block, zero), jnp.where(low, zero, block)], axis=0)

    def pair_join(stack):
        return jnp.where(low, stack[:WIN], stack[WIN:])

    def pair_lanes(p):
        return [pl.ds(part * width + p * LANES, LANES) for part in range(3)]

    for w in range(2):
        here = window(w)
        forward_in(w)
        allowed = mm_nt(labf[here, :], labf[here, :]) > 0.5
        allowed = jnp.concatenate([allowed, allowed], axis=0)
        for p in range(HEADS // 2):
            lanes = pair_lanes(p)
            query = pair_stack(qkv[here, lanes[0]])
            scores = mm_nt(query, qkv[here, lanes[1]]) * 0.125
            scores = jnp.where(allowed, scores, -jnp.inf)
            expo = jnp.exp(scores - jnp.max(scores, axis=-1, keepdims=True))
            prob = expo * (1.0 / jnp.sum(expo, axis=-1, keepdims=True))
            probs[w * 4 + p] = prob
            mixed[here, pl.ds(p * LANES, LANES)] = pair_join(
                mm(prob.astype(BF16), qkv[here, lanes[2]])
            ).astype(BF16)

    for load in loads[1:]:
        load.wait()
    attn = mm(mixed[...], w_out[...]).astype(BF16).astype(F32)
    resid[...] = tokf[...] + attn
    normed, scale_m = norm_stats(resid[...])
    norm_m[...] = normed
    h_m[...] = (normed * gain_m[...]).astype(BF16)
    dh[...] = jnp.zeros_like(dh)
    arrived(lat_cot)
    cotf[...] = apply_roll(second_pair, cot_cols[...], cot_above[...])

    set_a = (part_a, core_a, mine_a, r1_a, m1_a, r2_a, total_a, total_a_hbm)
    set_b = (part_b, core_b, mine_b, r1_b, m1_b, r2_b, total_b, total_b_hbm)
    sent = []

    def block(offset, count):
        return pl.ds(pl.multiple_of(offset, 16), count)

    def store(src, dst):
        copy = pltpu.make_async_copy(src, dst, store_sem.at[len(stores)])
        copy.start()
        stores.append(copy)

    def chain(refs, i, k):
        partial, core_in, mine, r1, m1, r2, total, total_hbm = refs
        axis = FIRST_AXIS[k]
        plane = planes[axis]
        at = position[axis]
        rest = [a for a in range(3) if a != axis]

        def share(offset):
            first, second = [lax.rem(position[a] + offset[a], SIDE) for a in rest]
            return (first * SIDE + second) * SHARE

        def send(n, src, dst, device):
            remote(src, dst, sum_send.at[k, n], sum_recv.at[k, n], device).start()

        def arrive(n, like):
            whole = remote(like, like, sum_send.at[k, n], sum_recv.at[k, n], core_peer)
            sent.append(whole)
            whole.wait_recv()

        send(0, partial.at[1 - core, i], core_in.at[i], core_peer)
        yield
        arrive(0, core_in.at[i])
        mine[i] = (partial[core, i].astype(F32) + core_in[i].astype(F32)).astype(BF16)
        for j in range(1, SIDE):
            quarter = block(lax.rem(at + j, SIDE) * QUARTER, QUARTER)
            send(1, mine.at[i, quarter], r1.at[i, j - 1], peers[axis][j - 1])
        yield
        arrive(1, r1.at[i])
        summed = mine[i, block(at * QUARTER, QUARTER), :].astype(F32)
        for j in range(SIDE - 1):
            summed = summed + r1[i, j].astype(F32)
        m1[i] = summed.astype(BF16)
        for n, (offset, device) in enumerate(plane):
            send(2, m1.at[i, block(share(offset), SHARE)], r2.at[i, n], device)
        yield
        arrive(2, r2.at[i])
        own = share((0, 0, 0))
        summed = m1[i, block(own, SHARE), :].astype(F32) + jnp.sum(r2[i].astype(F32), axis=0)
        place = (core, i, block(at * QUARTER + own, SHARE))
        total[place] = summed.astype(BF16)
        for offset, device in plane:
            send(3, total.at[place], total.at[place], device)
        yield
        arrive(3, r2.at[i])
        place = (core, i, block(at * QUARTER, QUARTER))
        for device in peers[axis]:
            send(4, total.at[place], total.at[place], device)
        yield
        arrive(4, r1.at[i])
        send(5, total.at[core, i], total.at[core, i], core_peer)
        store(total.at[core, i], total_hbm.at[core, i])
        yield
        arrive(5, core_in.at[i])
        store(total.at[1 - core, i], total_hbm.at[1 - core, i])

    def gain_chain():
        used = [0]

        def send(src, device):
            n = used[0]
            used[0] += 1
            return go(src, gains_in.at[n], gain_send.at[n], gain_recv.at[n], device)

        copy = send(gains_acc.at[0], core_peer)
        yield
        copy.wait_recv()
        gains_acc[1] = gains_acc[0] + gains_in[0]
        for axis in range(3):
            copies = [send(gains_acc.at[axis + 1], peer) for peer in peers[axis]]
            yield
            for copy in copies:
                copy.wait_recv()
            base = 1 + 3 * axis
            summed = (gains_acc[axis + 1] + gains_in[base + 1]) + (gains_in[base] + gains_in[base + 2])
            if axis < 2:
                gains_acc[axis + 2] = summed
            else:
                gains_sum[...] = summed

    def advance(*chains):
        for link in chains:
            next(link, None)

    chains = [chain(set_a, i, i) for i in range(CHUNKS)]
    chains += [chain(set_b, i, CHUNKS + i) for i in range(CHUNKS)]

    def step(*which):
        for i in which:
            next(chains[i], None)

    level, row, col = row_cells()
    col, col_out = fold(col + per_level(level, cols), WW)
    back_pair = roll_pair(level * PLANE + row * WW + col, col_out, CELLS)

    def turn(arrived, own, other, rolled, rolled_x, rolled_hbm):
        arrived.wait_recv()
        rolled[...] = apply_roll(back_pair, own[...], other[...])
        rolled_x[pl.ds(CELLS - LEVELS * WW, LEVELS * WW), :] = jnp.zeros((LEVELS * WW, width), BF16)
        store(rolled, rolled_hbm)
        return halo_split(rolled, rolled_x, grid["above"], 0, CELLS - line, 3)

    gains_link = gain_chain()
    chains.append(gains_link)
    lat_back, halo_lon = [], []

    def out_back():
        lat_back.append(turn(halo_lon[0], out_f, out_right, out_t, out_tx, out_t_hbm))
        yield

    def tok_back():
        lat_back.append(turn(halo_lon[1], tok_f, tok_right, tok_t, tok_tx, tok_t_hbm))
        yield

    chains.extend((out_back(), tok_back()))
    for c in range(CHUNKS):
        part = pl.ds(c * 512, 512)
        pre = mm(h_m[...], w_up[:, part])
        cdf = 0.5 * (1.0 + lax.erf(pre * 0.7071067811865476))
        act = (pre * cdf).astype(BF16)
        slope = cdf + pre * jnp.exp(-0.5 * pre * pre) * 0.3989422804014327
        resid[...] += mm(act, w_down[part, :])
        grad_pre = (mm_nt(cotf[...], w_down[part, :]) * slope).astype(BF16)
        dh[...] += mm_nt(grad_pre, w_up[:, part])
        down = mm_tn(act, cotf[...]).astype(BF16)
        up = mm_tn(h_m[...], grad_pre).astype(BF16)
        for b in range(2):
            spot = slice(b * 512, (b + 1) * 512)
            cut = slice(b * 256, (b + 1) * 256)
            part_a[0, c, spot, :] = down[:, cut]
            part_a[1, c, spot, :] = up[:, cut]
        step(*PUMP_MLP[c])
    out_f[...] = resid[...].astype(BF16)
    halo_lon.append(halo_go(out_f, out_right, grid["left"]))
    term, gain_grad_m = norm_back(dh[...], norm_m[...], scale_m, gain_m[...])
    resid[...] = cotf[...].astype(F32) + term
    grad_attn = resid[...].astype(BF16)

    def put(half, i, b, value):
        for j in range(2):
            part_b[half, i, j * 512 : (j + 1) * 512, :] = value[:, b + j * LANES : b + (j + 1) * LANES]

    grad_out = mm_tn(mixed[...], grad_attn).astype(BF16)
    put(0, 0, 0, grad_out)
    put(1, 0, 256, grad_out)
    step(*PUMP_OUT)
    mixed[...] = mm_nt(grad_attn, w_out[...]).astype(BF16)
    step(*PUMP_MIX)

    homes = {(0, 0): (0, 1), (1, 0): (1, 1), (2, 0): (0, 2), (0, 1): (1, 2), (1, 1): (0, 3), (2, 1): (1, 3)}
    for p in range(HEADS // 2):
        lanes = pair_lanes(p)
        for w in range(2):
            here = window(w)
            prob = probs[w * 4 + p]
            dmix = pair_stack(mixed[here, pl.ds(p * LANES, LANES)])
            query = pair_stack(qkv[here, lanes[0]])
            dprob = mm_nt(dmix, qkv[here, lanes[2]])
            dqkv[here, lanes[2]] = mm_tn(prob.astype(BF16), dmix).astype(BF16)
            dscore = prob * (dprob - jnp.sum(dprob * prob, axis=-1, keepdims=True)) * 0.125
            dscore = dscore.astype(BF16)
            dqkv[here, lanes[0]] = pair_join(mm(dscore, qkv[here, lanes[1]])).astype(BF16)
            dqkv[here, lanes[1]] = mm_tn(dscore, query).astype(BF16)
        if p % 2 == 1:
            for c in range(3):
                half, i = homes[c, p // 2]
                cut = pl.ds(c * width + (p // 2) * 256, 256)
                put(half, i, 0, mm_tn(h_a[...], dqkv[:, cut]).astype(BF16))
        step(*PUMP_PAIRS[p])

    dframe = None
    for c in range(3):
        part = pl.ds(c * width, width)
        term = mm_nt(dqkv[:, part], w_qkv[:, part])
        dframe = term if dframe is None else dframe + term
    dframe = dframe.astype(BF16).astype(F32)
    step(*PUMP_FRAME)
    term, gain_grad_a = norm_back(dframe, norm_a[...], jnp.concatenate(scale_a, axis=0), gain_a[...])
    for r in range(4):
        cut = slice(r * LANES, (r + 1) * LANES)
        gains_acc[0, r : r + 1, :] = gain_grad_a[:, cut]
        gains_acc[0, r + 4 : r + 5, :] = gain_grad_m[:, cut]
    advance(gains_link)
    tok_f[...] = (resid[...] + term).astype(BF16)
    halo_lon.append(halo_go(tok_f, tok_right, grid["left"]))
    step(*PUMP_TAIL)
    for again in range(ROUNDS):
        step(*range(CHUNKS * 2 + 1))
    for copy, rolled_x, rolled_hbm in zip(lat_back, (out_tx, tok_tx), (out_tx_hbm, tok_tx_hbm)):
        arrived(copy)
        store(rolled_x, rolled_hbm)
    for copy in sent:
        copy.wait_send()
    for copy in started:
        copy.wait_send()
    for copy in stores:
        copy.wait()


def finish_kernel(
    rows, cols, total_a_hbm, total_b_hbm, gains, out_t_hbm, out_tx_hbm, tok_t_hbm, tok_tx_hbm,
    block_out, grad_tokens, gain_a, gain_m, grad_qkv, grad_out, grad_up, grad_down,
    total_a, total_b, up, down, out, qkv, tiles, results, in_sems, tile_sems, out_sems,
):
    width = gain_a.shape[1]
    loads, moves = {}, []
    for i in range(CHUNKS):
        for kind, (src, dst) in enumerate(((total_a_hbm, total_a), (total_b_hbm, total_b))):
            for half in range(2):
                load = pltpu.make_async_copy(src.at[half, i], dst.at[half, i], in_sems.at[kind, half, i])
                load.start()
                loads[kind, half, i] = load
    tile_loads = [
        pltpu.make_async_copy(src, tiles.at[n], tile_sems.at[n])
        for n, src in enumerate((out_t_hbm, out_tx_hbm, tok_t_hbm, tok_tx_hbm))
    ]
    for load in tile_loads:
        load.start()

    def move(src, dst):
        copy = pltpu.make_async_copy(src, dst, out_sems.at[len(moves)])
        copy.start()
        moves.append(copy)

    homes = {(0, 1): (0, 0), (1, 1): (1, 0), (0, 2): (2, 0), (1, 2): (0, 1), (0, 3): (1, 1), (1, 3): (2, 1)}
    for i in range(CHUNKS):
        here = slice(i * 512, (i + 1) * 512)
        for half in range(2):
            loads[0, half, i].wait()
            for b in range(2):
                value = total_a[half, i, b * 512 : (b + 1) * 512, :].astype(F32)
                if half == 0:
                    down[here, b * 256 : (b + 1) * 256] = value
                else:
                    up[:, i * 512 + b * 256 : i * 512 + (b + 1) * 256] = value
        move(down.at[pl.ds(i * 512, 512)], grad_down.at[pl.ds(i * 512, 512)])
        move(up.at[:, pl.ds(i * 512, 512)], grad_up.at[:, pl.ds(i * 512, 512)])
        for half in range(2):
            loads[1, half, i].wait()
            for j in range(2):
                value = total_b[half, i, j * 512 : (j + 1) * 512, :].astype(F32)
                if i == 0:
                    first = half * 256 + j * LANES
                    out[:, first : first + LANES] = value
                else:
                    c, second = homes[half, i]
                    first = c * width + second * 256 + j * LANES
                    qkv[:, first : first + LANES] = value
        if i == 0:
            move(out, grad_out)
    move(qkv, grad_qkv)
    level, row, col = data_cells()
    row, row_out = fold(row + per_level(level, rows), WH)
    pair = roll_pair(row * LEVELS * WW + level * WW + col, row_out, CELLS)
    for load in tile_loads:
        load.wait()
    for n, result in enumerate((block_out, grad_tokens)):
        results[n] = apply_roll(pair, tiles[2 * n], tiles[2 * n + 1]).reshape(result.shape)
        move(results.at[n], result)
    for r in range(4):
        cut = slice(r * LANES, (r + 1) * LANES)
        gain_a[:, cut] = gains[r : r + 1, :]
        gain_m[:, cut] = gains[r + 4 : r + 5, :]
    for copy in moves:
        copy.wait()


VMEM = pl.BlockSpec(memory_space=pltpu.VMEM)
SMEM = pl.BlockSpec(memory_space=pltpu.SMEM)
ANY = pl.BlockSpec(memory_space=pl.ANY)
DMA = pltpu.SemaphoreType.DMA


def call(kernel, outs, in_specs, out_specs, scratch, name, collective_id=None):
    params = {"vmem_limit_bytes": VMEM_BYTES}
    if collective_id is not None:
        params.update(collective_id=collective_id, has_side_effects=True)
    return pl.pallas_call(
        kernel,
        out_shape=[jax.ShapeDtypeStruct(shape, dtype) for shape, dtype in outs],
        in_specs=in_specs,
        out_specs=out_specs,
        scratch_shapes=scratch,
        compiler_params=pltpu.CompilerParams(**params),
        name=name,
    )


def sum_buffers(lanes):
    shapes = [
        (2, CHUNKS, PART, lanes),
        (CHUNKS, PART, lanes),
        (CHUNKS, PART, lanes),
        (CHUNKS, SIDE - 1, QUARTER, lanes),
        (CHUNKS, QUARTER, lanes),
        (CHUNKS, SIDE * SIDE - 1, SHARE, lanes),
        (2, CHUNKS, PART, lanes),
    ]
    return [pltpu.VMEM(shape, BF16) for shape in shapes]


def native(field):
    return field.transpose(1, 2, 0, 3).reshape(-1, field.shape[0], field.shape[3])


def on_device(
    tokens,
    region_ids,
    shift_lat,
    shift_lon,
    gain_attn,
    w_qkv,
    w_out,
    gain_mlp,
    w_up,
    w_down,
    cotangent,
):
    levels, lat_rows, lon_cols, width = tokens.shape
    cells = levels * lat_rows * lon_cols
    ff = w_up.shape[1]
    lines = (lat_rows * lon_cols, levels, width)
    tile = ((cells, width), BF16)
    half, full = pltpu.VMEM((cells, width), BF16), pltpu.VMEM((cells, width), F32)
    total_a, total_b, gains_sum, *rolled = call(
        block_kernel,
        [((2, CHUNKS, PART, 256), BF16), ((2, CHUNKS, PART, LANES), BF16), ((8, LANES), F32)] + [tile] * 4,
        [SMEM] * 2 + [VMEM] * 5 + [ANY] * 4,
        [ANY] * 2 + [VMEM] + [ANY] * 4,
        [pltpu.VMEM(w.shape, BF16) for w in (w_qkv, w_out, w_up, w_down)]
        + [pltpu.VMEM(lines, BF16), pltpu.VMEM((lat_rows, lon_cols, levels, width), BF16)]
        + [half] * 4
        + [pltpu.VMEM((16, LANES), jnp.int32)] * 2
        + [
            half,
            full,
            pltpu.VMEM((cells, LANES), BF16),
            full,
            half,
            pltpu.VMEM((cells, 3 * width), BF16),
            pltpu.VMEM((HEADS, 2 * WIN, WIN), F32),
            half,
            full,
            full,
            half,
            full,
            pltpu.VMEM((cells, 3 * width), BF16),
        ]
        + [half] * 8
        + [pltpu.VMEM((4, 8, LANES), F32), pltpu.VMEM((10, 8, LANES), F32)]
        + sum_buffers(256)
        + sum_buffers(LANES)
        + [
            DMA((4,)),
            DMA((20,)),
            DMA((20,)),
            DMA((2 * CHUNKS, ROUNDS)),
            DMA((2 * CHUNKS, ROUNDS)),
            DMA((10,)),
            DMA((10,)),
            DMA((4 * CHUNKS + 4,)),
        ],
        "block",
        0,
    )(
        shift_lat, shift_lon, native(tokens), cotangent.transpose(1, 2, 0, 3), region_ids,
        gain_attn.reshape(1, width), gain_mlp.reshape(1, width), w_qkv, w_out, w_up, w_down,
    )
    results = call(
        finish_kernel,
        [
            (lines, BF16),
            (lines, BF16),
            ((1, width), F32),
            ((1, width), F32),
            ((width, 3 * width), F32),
            ((width, width), F32),
            ((width, ff), F32),
            ((ff, width), F32),
        ],
        [SMEM] * 2 + [ANY] * 2 + [VMEM] + [ANY] * 4,
        [ANY] * 2 + [VMEM] * 2 + [ANY] * 4,
        [
            pltpu.VMEM((2, CHUNKS, PART, 256), BF16),
            pltpu.VMEM((2, CHUNKS, PART, LANES), BF16),
            pltpu.VMEM(w_up.shape, F32),
            pltpu.VMEM(w_down.shape, F32),
            pltpu.VMEM(w_out.shape, F32),
            pltpu.VMEM(w_qkv.shape, F32),
            pltpu.VMEM((4, cells, width), BF16),
            pltpu.VMEM((2,) + lines, BF16),
            DMA((2, 2, CHUNKS)),
            DMA((4,)),
            DMA((2 * CHUNKS + 4,)),
        ],
        "finish",
    )(shift_lat, shift_lon, total_a, total_b, gains_sum, *rolled)
    block_out, grad_tokens, grad_gain_attn, grad_gain_mlp, grad_qkv, grad_out, grad_up, grad_down = results

    def whole(field):
        return field.reshape(lat_rows, lon_cols, levels, width).transpose(2, 0, 1, 3)

    return (
        whole(block_out),
        whole(grad_tokens),
        grad_gain_attn.reshape(width),
        grad_qkv,
        grad_out,
        grad_gain_mlp.reshape(width),
        grad_up,
        grad_down,
    )


def solution(mesh):
    placed = (
        P(None, "lat", "lon", None),
        P("lat", "lon"),
        P(),
        P(),
        P(),
        P(),
        P(),
        P(),
        P(),
        P(),
        P(None, "lat", "lon", None),
    )
    return jax.shard_map(
        on_device,
        mesh=mesh,
        in_specs=placed,
        out_specs=(
            P(None, "lat", "lon", None),
            P(None, "lat", "lon", None),
            P(),
            P(),
            P(),
            P(),
            P(),
            P(),
        ),
        check_vma=False,
    )
```

```python
import functools

import jax
import jax.numpy as jnp
from jax import lax
from jax.experimental import pallas as pl
from jax.experimental.pallas import tpu as pltpu
from jax.sharding import PartitionSpec as P

HEADS = 8
WV = 2
WH = 6
WW = 12
WIN = WV * WH * WW
PLANE = WH * WW
LANES = 128
LEVELS = 4
CELLS = LEVELS * PLANE
SIDE = 4
EPS = 1e-05
MESH = pl.DeviceIdType.MESH
F32 = jnp.float32
BF16 = jnp.bfloat16
CHUNKS = 4
ORDER = ((0, 1, 2), (1, 2, 0), (2, 0, 1), (2, 1, 0), (1, 0, 2), (1, 2, 0), (0, 1, 2), (2, 1, 0))
GAINS, OUT, TOK = 8, 9, 10
PUMP_MLP = ((0,), (1,), (2, 0), (3, 1, 2))
PUMP_OUT, PUMP_MIX = (4,), ()
PUMP_PAIRS = ((3, 4), (5,), (), (6, 7, 5))
PUMP_FRAME = (0, 6, 7, 1, 2)
PUMP_TAIL = (8, 4, 9, 5, 3, 0, 6, 2, 7, 1, 5, 3, 6, 0, 2, 7, 8, 10, 4, 6, 0, 8, 1, 5, 3, 4, 8, 2, 7, 6, 1, 5, 3, 7, 0, 4, 0, 2, 6, 1, 2, 6, 1, 5, 3, 5, 4, 3, 7, 4, 7)
PART = 1024
QUARTER = 256
SHARE = 64
ROUNDS = 7
VMEM_BYTES = 60 * 1024 * 1024
DIMS_ZERO = (((0,), (0,)), ((), ()))
DIMS_LAST = (((1,), (1,)), ((), ()))


def mm(a, b):
    return jnp.dot(a, b, preferred_element_type=F32)


def mm_tn(a, b):
    return lax.dot_general(a, b, DIMS_ZERO, preferred_element_type=F32)


def mm_nt(a, b):
    return lax.dot_general(a, b, DIMS_LAST, preferred_element_type=F32)


def norm_stats(values):
    center = values - jnp.mean(values, axis=-1, keepdims=True)
    inv_scale = lax.rsqrt(jnp.mean(center * center, axis=-1, keepdims=True) + EPS)
    return (center * inv_scale, inv_scale)


def norm_back(grad, normed, inv_scale, gain):
    gain_grad = jnp.sum(grad * normed, axis=0, keepdims=True)
    graded = grad * gain
    term = inv_scale * (
        graded
        - jnp.mean(graded, axis=-1, keepdims=True)
        - normed * jnp.mean(graded * normed, axis=-1, keepdims=True)
    )
    return (term, gain_grad)


def places():
    lat, lon = lax.axis_index("lat"), lax.axis_index("lon")
    lats, lons = lax.axis_size("lat"), lax.axis_size("lon")
    core, y_hi = lax.rem(lat, 2), lat // 2
    x, y_lo, z = lax.rem(lon, SIDE), lax.rem(lon // SIDE, 2), lon // (2 * SIDE)
    y = y_hi * 2 + y_lo

    def device(x, y, z):
        x, y, z = lax.rem(x, SIDE), lax.rem(y, SIDE), lax.rem(z, SIDE)
        return ((y // 2) * 2 + core, z * 2 * SIDE + lax.rem(y, 2) * SIDE + x)

    spot = (x, y, z)

    def away(offset):
        return device(*[p + o for p, o in zip(spot, offset)])

    peers = [[away([j * (a == b) for b in range(3)]) for j in range(1, SIDE)] for a in range(3)]
    grid = {
        "below": (lax.rem(lat + 1, lats), lon),
        "above": (lax.rem(lat + lats - 1, lats), lon),
        "right": (lat, lax.rem(lon + 1, lons)),
        "left": (lat, lax.rem(lon + lons - 1, lons)),
    }
    return grid, core, (y_hi * 2 + 1 - core, lon), peers, spot


def remote(src, dst, send, recv, device):
    return pltpu.make_async_remote_copy(
        src_ref=src, dst_ref=dst, send_sem=send, recv_sem=recv, device_id=device, device_id_type=MESH
    )


def div(value, by):
    return jnp.floor((value.astype(F32) + 0.5) * (1.0 / by)).astype(jnp.int32)


def frame_cells(start, count):
    cell = start + lax.broadcasted_iota(jnp.int32, (count, 1), 0)
    level = div(cell, PLANE)
    row = div(cell - level * PLANE, WW)
    return level, row, cell - level * PLANE - row * WW


def data_cells():
    cell = lax.broadcasted_iota(jnp.int32, (CELLS, 1), 0)
    spot = div(cell, LEVELS)
    row = div(spot, WW)
    return cell - spot * LEVELS, row, spot - row * WW


def row_cells():
    cell = lax.broadcasted_iota(jnp.int32, (CELLS, 1), 0)
    row = div(cell, LEVELS * WW)
    level = div(cell - row * LEVELS * WW, WW)
    return level, row, cell - row * LEVELS * WW - level * WW


def per_level(level, ref):
    value = ref[LEVELS - 1]
    for k in reversed(range(LEVELS - 1)):
        value = jnp.where(level == k, ref[k], value)
    return value


def fold(value, limit):
    out = ((value < 0) | (value >= limit)).astype(jnp.int32)
    return jnp.where(value < 0, value + limit, jnp.where(value >= limit, value - limit, value)), out


def one_hot(hit, index, width):
    lanes = lax.broadcasted_iota(jnp.int32, (index.shape[0], width), 1)
    return jnp.where((lanes == index) & hit, 1.0, 0.0).astype(BF16)


def roll_pair(index, out, width):
    return one_hot(out == 0, index, width), one_hot(out == 1, index, width)


def apply_roll(pair, here, there):
    return (mm(pair[0], here) + mm(pair[1], there)).astype(BF16)


def block_kernel(
    rows, cols, tok_in, cot_in, ids_in, gain_a, gain_m, w_qkv_hbm, w_out_hbm, w_up_hbm, w_down_hbm,
    total_a_hbm, total_b_hbm, gains_sum, out_t_hbm, out_tx_hbm, tok_t_hbm, tok_tx_hbm,
    w_qkv, w_out, w_up, w_down,
    tok_above, cot_left, tok_rows, tok_left, cot_cols, cot_above, ids, ids_x,
    cotf, tokf, labf, norm_a, h_a, qkv, probs, mixed, resid, norm_m, h_m, dh, dqkv,
    out_f, out_right, tok_f, tok_right, out_t, out_tx, tok_t, tok_tx, gains_acc, gains_in,
    part_a, core_a, mine_a, r1_a, m1_a, r2_a, m2_a, r3_a, total_a,
    part_b, core_b, mine_b, r1_b, m1_b, r2_b, m2_b, r3_b, total_b,
    load_sem, halo_send, halo_recv, sum_send, sum_recv, gain_send, gain_recv, store_sem,
):
    width = gain_a.shape[1]
    grid, core, core_peer, peers, position = places()
    loads = [
        pltpu.make_async_copy(src, dst, load_sem.at[k])
        for k, (src, dst) in enumerate(
            ((w_qkv_hbm, w_qkv), (w_out_hbm, w_out), (w_up_hbm, w_up), (w_down_hbm, w_down))
        )
    ]
    greeted = [core_peer] + [p for axis in peers for p in axis] + list(grid.values())
    barrier = pltpu.get_barrier_semaphore()
    for device in greeted:
        pl.semaphore_signal(barrier, inc=1, device_id=device, device_id_type=MESH)
    for load in loads:
        load.start()

    started = []
    stores = []

    def go(*args):
        copy = remote(*args)
        copy.start()
        started.append(copy)
        return copy

    halos = []

    def halo_go(src, dst, device):
        k = len(halos)
        halos.append(go(src, dst, halo_send.at[k], halo_recv.at[k], device))
        return halos[-1]

    def halo_split(src, dst, device, start, count, pieces):
        size = count // pieces
        cuts = [pl.ds(start + n * size, size) for n in range(pieces)]
        return [halo_go(src.at[cut], dst.at[cut], device) for cut in cuts]

    def arrived(copies):
        for copy in copies:
            copy.wait_recv()

    def window(w):
        return pl.ds(w * WIN, WIN)

    ids[0:8, :] = jnp.zeros((8, LANES), jnp.int32)
    ids[0:WH, 0:WW] = ids_in[...]
    tok_above[0:WW] = jnp.zeros((WW, LEVELS, width), BF16)
    cot_left[:, 0:1] = jnp.zeros((WH, 1, LEVELS, width), BF16)
    line = LEVELS * WW
    cot_above[0:line, :] = jnp.zeros((line, width), BF16)
    used_cols = pl.ds(1, WW - 1)
    pl.semaphore_wait(barrier, len(greeted))
    lat_tok = halo_split(tok_in, tok_above, grid["below"], WW, PLANE - WW, 4)
    lat_ids = halo_go(ids.at[pl.ds(0, 8)], ids.at[pl.ds(8, 8)], grid["below"])
    lon_cot = halo_go(cot_in.at[:, used_cols], cot_left.at[:, used_cols], grid["right"])
    level, row, col = row_cells()
    col, col_out = fold(col - per_level(level, cols), WW)
    first_pair = roll_pair((row * WW + col) * LEVELS + level, col_out, CELLS)
    level, row, col = frame_cells(0, CELLS)
    row, row_out = fold(row - per_level(level, rows), WH)
    second_pair = roll_pair(row * line + level * WW + col, row_out, CELLS)
    level, row, col = frame_cells(0, CELLS)
    row, row_out = fold(row - per_level(level, rows), WH)
    row_pair = roll_pair((row * WW + col) * LEVELS + level, row_out, CELLS)
    level, row, col = frame_cells(0, CELLS)
    col, col_out = fold(col - per_level(level, cols), WW)
    col_index = lax.rem(level, WV) * PLANE + row * WW + col
    col_pairs = [
        roll_pair(col_index[w * WIN : (w + 1) * WIN], col_out[w * WIN : (w + 1) * WIN], WIN) for w in range(2)
    ]
    arrived(lat_tok)
    tok_rows[...] = apply_roll(
        row_pair, tok_in[...].reshape(CELLS, width), tok_above[...].reshape(CELLS, width)
    )
    lon_tok = [halo_go(tok_rows.at[window(w)], tok_left.at[window(w)], grid["right"]) for w in range(2)]
    lat_ids.wait_recv()
    lon_ids = halo_go(ids, ids_x, grid["right"])
    lon_cot.wait_recv()
    cot_cols[...] = apply_roll(
        first_pair, cot_in[...].reshape(CELLS, width), cot_left[...].reshape(CELLS, width)
    )
    lat_cot = halo_split(cot_cols, cot_above, grid["below"], line, CELLS - line, 3)

    lon_ids.wait_recv()
    ids_all = jnp.concatenate([ids[...], ids_x[...]], axis=0).astype(F32).astype(BF16)
    level, row, col = frame_cells(0, CELLS)
    row, row_out = fold(row - per_level(level, rows), WH)
    col, col_out = fold(col - per_level(level, cols), WW)
    picked = mm(one_hot(level >= 0, (row_out + 2 * col_out) * 8 + row, 32), ids_all)
    lanes = lax.broadcasted_iota(jnp.int32, (CELLS, LANES), 1)
    label = jnp.sum(jnp.where(lanes == col, picked, 0.0), axis=-1, keepdims=True)
    labf[...] = jnp.where(lanes.astype(F32) == label, 1.0, 0.0).astype(BF16)
    scale_a = []

    def forward_in(w):
        here = window(w)
        lon_tok[w].wait_recv()
        values = apply_roll(col_pairs[w], tok_rows[here, :], tok_left[here, :]).astype(F32)
        tokf[here, :] = values
        normed, scale = norm_stats(values)
        scale_a.append(scale)
        norm_a[here, :] = normed
        h_a[here, :] = (normed * gain_a[...]).astype(BF16)
        if w == 0:
            loads[0].wait()
        for c in range(3):
            part = pl.ds(c * width, width)
            qkv[here, part] = mm(h_a[here, :], w_qkv[:, part]).astype(BF16)

    low = lax.broadcasted_iota(jnp.int32, (1, LANES), 1) < LANES // 2

    def pair_stack(block):
        zero = jnp.zeros_like(block)
        return jnp.concatenate([jnp.where(low, block, zero), jnp.where(low, zero, block)], axis=0)

    def pair_join(stack):
        return jnp.where(low, stack[:WIN], stack[WIN:])

    def pair_lanes(p):
        return [pl.ds(part * width + p * LANES, LANES) for part in range(3)]

    for w in range(2):
        here = window(w)
        forward_in(w)
        allowed = mm_nt(labf[here, :], labf[here, :]) > 0.5
        allowed = jnp.concatenate([allowed, allowed], axis=0)
        for p in range(HEADS // 2):
            lanes = pair_lanes(p)
            query = pair_stack(qkv[here, lanes[0]])
            scores = mm_nt(query, qkv[here, lanes[1]]) * 0.125
            scores = jnp.where(allowed, scores, -jnp.inf)
            expo = jnp.exp(scores - jnp.max(scores, axis=-1, keepdims=True))
            prob = expo * (1.0 / jnp.sum(expo, axis=-1, keepdims=True))
            probs[w * 4 + p] = prob
            mixed[here, pl.ds(p * LANES, LANES)] = pair_join(
                mm(prob.astype(BF16), qkv[here, lanes[2]])
            ).astype(BF16)

    for load in loads[1:]:
        load.wait()
    attn = mm(mixed[...], w_out[...]).astype(BF16).astype(F32)
    resid[...] = tokf[...] + attn
    normed, scale_m = norm_stats(resid[...])
    norm_m[...] = normed
    h_m[...] = (normed * gain_m[...]).astype(BF16)
    dh[...] = jnp.zeros_like(dh)
    arrived(lat_cot)
    cotf[...] = apply_roll(second_pair, cot_cols[...], cot_above[...])

    set_a = (part_a, core_a, mine_a, r1_a, m1_a, r2_a, m2_a, r3_a, total_a, total_a_hbm)
    set_b = (part_b, core_b, mine_b, r1_b, m1_b, r2_b, m2_b, r3_b, total_b, total_b_hbm)
    sent = []

    def block(offset, count):
        return pl.ds(pl.multiple_of(offset, 16), count)

    def store(src, dst):
        copy = pltpu.make_async_copy(src, dst, store_sem.at[len(stores)])
        copy.start()
        stores.append(copy)

    def chain(refs, i, k):
        partial, core_in, mine, r1, m1, r2, m2, r3, total, total_hbm = refs
        first, second, third = ORDER[k]
        at, then = position[first], position[second]

        def send(n, src, dst, device):
            remote(src, dst, sum_send.at[k, n], sum_recv.at[k, n], device).start()

        def arrive(n, like):
            whole = remote(like, like, sum_send.at[k, n], sum_recv.at[k, n], core_peer)
            sent.append(whole)
            whole.wait_recv()

        send(0, partial.at[1 - core, i], core_in.at[i], core_peer)
        yield
        arrive(0, core_in.at[i])
        mine[i] = (partial[core, i].astype(F32) + core_in[i].astype(F32)).astype(BF16)
        for j in range(1, SIDE):
            quarter = block(lax.rem(at + j, SIDE) * QUARTER, QUARTER)
            send(1, mine.at[i, quarter], r1.at[i, j - 1], peers[first][j - 1])
        yield
        arrive(1, r1.at[i])
        summed = mine[i, block(at * QUARTER, QUARTER), :].astype(F32)
        for j in range(SIDE - 1):
            summed = summed + r1[i, j].astype(F32)
        m1[i] = summed.astype(BF16)
        for j in range(1, SIDE):
            share = block(lax.rem(then + j, SIDE) * SHARE, SHARE)
            send(2, m1.at[i, share], r2.at[i, j - 1], peers[second][j - 1])
        yield
        arrive(2, r2.at[i])
        summed = m1[i, block(then * SHARE, SHARE), :].astype(F32)
        for j in range(SIDE - 1):
            summed = summed + r2[i, j].astype(F32)
        m2[i] = summed.astype(BF16)
        for j in range(SIDE - 1):
            send(3, m2.at[i], r3.at[i, j], peers[third][j])
        yield
        arrive(3, r3.at[i])
        near, far = r3[i, 0].astype(F32) + r3[i, 2].astype(F32), m2[i].astype(F32) + r3[i, 1].astype(F32)
        place = (core, i, block(at * QUARTER + then * SHARE, SHARE))
        total[place] = (near + far).astype(BF16)
        for device in peers[second]:
            send(4, total.at[place], total.at[place], device)
        yield
        arrive(4, r2.at[i])
        place = (core, i, block(at * QUARTER, QUARTER))
        for device in peers[first]:
            send(5, total.at[place], total.at[place], device)
        yield
        arrive(5, r1.at[i])
        send(6, total.at[core, i], total.at[core, i], core_peer)
        store(total.at[core, i], total_hbm.at[core, i])
        yield
        arrive(6, core_in.at[i])
        store(total.at[1 - core, i], total_hbm.at[1 - core, i])

    def gain_chain():
        used = [0]

        def send(src, device):
            n = used[0]
            used[0] += 1
            return go(src, gains_in.at[n], gain_send.at[n], gain_recv.at[n], device)

        copy = send(gains_acc.at[0], core_peer)
        yield
        copy.wait_recv()
        gains_acc[1] = gains_acc[0] + gains_in[0]
        for axis in range(3):
            copies = [send(gains_acc.at[axis + 1], peer) for peer in peers[axis]]
            yield
            for copy in copies:
                copy.wait_recv()
            base = 1 + 3 * axis
            summed = (gains_acc[axis + 1] + gains_in[base + 1]) + (gains_in[base] + gains_in[base + 2])
            if axis < 2:
                gains_acc[axis + 2] = summed
            else:
                gains_sum[...] = summed

    def advance(*chains):
        for link in chains:
            next(link, None)

    chains = [chain(set_a, i, i) for i in range(CHUNKS)]
    chains += [chain(set_b, i, CHUNKS + i) for i in range(CHUNKS)]

    def step(*which):
        for i in which:
            next(chains[i], None)

    level, row, col = row_cells()
    col, col_out = fold(col + per_level(level, cols), WW)
    back_pair = roll_pair(level * PLANE + row * WW + col, col_out, CELLS)

    def turn(arrived, own, other, rolled, rolled_x, rolled_hbm):
        arrived.wait_recv()
        rolled[...] = apply_roll(back_pair, own[...], other[...])
        rolled_x[pl.ds(CELLS - LEVELS * WW, LEVELS * WW), :] = jnp.zeros((LEVELS * WW, width), BF16)
        store(rolled, rolled_hbm)
        return halo_split(rolled, rolled_x, grid["above"], 0, CELLS - line, 3)

    gains_link = gain_chain()
    chains.append(gains_link)
    lat_back, halo_lon = [], []

    def out_back():
        lat_back.append(turn(halo_lon[0], out_f, out_right, out_t, out_tx, out_t_hbm))
        yield

    def tok_back():
        lat_back.append(turn(halo_lon[1], tok_f, tok_right, tok_t, tok_tx, tok_t_hbm))
        yield

    chains.extend((out_back(), tok_back()))
    for c in range(CHUNKS):
        part = pl.ds(c * 512, 512)
        pre = mm(h_m[...], w_up[:, part])
        cdf = 0.5 * (1.0 + lax.erf(pre * 0.7071067811865476))
        act = (pre * cdf).astype(BF16)
        slope = cdf + pre * jnp.exp(-0.5 * pre * pre) * 0.3989422804014327
        resid[...] += mm(act, w_down[part, :])
        grad_pre = (mm_nt(cotf[...], w_down[part, :]) * slope).astype(BF16)
        dh[...] += mm_nt(grad_pre, w_up[:, part])
        down = mm_tn(act, cotf[...]).astype(BF16)
        up = mm_tn(h_m[...], grad_pre).astype(BF16)
        for b in range(2):
            spot = slice(b * 512, (b + 1) * 512)
            cut = slice(b * 256, (b + 1) * 256)
            part_a[0, c, spot, :] = down[:, cut]
            part_a[1, c, spot, :] = up[:, cut]
        step(*PUMP_MLP[c])
    out_f[...] = resid[...].astype(BF16)
    halo_lon.append(halo_go(out_f, out_right, grid["left"]))
    term, gain_grad_m = norm_back(dh[...], norm_m[...], scale_m, gain_m[...])
    resid[...] = cotf[...].astype(F32) + term
    grad_attn = resid[...].astype(BF16)

    def put(half, i, b, value):
        for j in range(2):
            part_b[half, i, j * 512 : (j + 1) * 512, :] = value[:, b + j * LANES : b + (j + 1) * LANES]

    grad_out = mm_tn(mixed[...], grad_attn).astype(BF16)
    put(0, 0, 0, grad_out)
    put(1, 0, 256, grad_out)
    step(*PUMP_OUT)
    mixed[...] = mm_nt(grad_attn, w_out[...]).astype(BF16)
    step(*PUMP_MIX)

    homes = {(0, 0): (0, 1), (1, 0): (1, 1), (2, 0): (0, 2), (0, 1): (1, 2), (1, 1): (0, 3), (2, 1): (1, 3)}
    for p in range(HEADS // 2):
        lanes = pair_lanes(p)
        for w in range(2):
            here = window(w)
            prob = probs[w * 4 + p]
            dmix = pair_stack(mixed[here, pl.ds(p * LANES, LANES)])
            query = pair_stack(qkv[here, lanes[0]])
            dprob = mm_nt(dmix, qkv[here, lanes[2]])
            dqkv[here, lanes[2]] = mm_tn(prob.astype(BF16), dmix).astype(BF16)
            dscore = prob * (dprob - jnp.sum(dprob * prob, axis=-1, keepdims=True)) * 0.125
            dscore = dscore.astype(BF16)
            dqkv[here, lanes[0]] = pair_join(mm(dscore, qkv[here, lanes[1]])).astype(BF16)
            dqkv[here, lanes[1]] = mm_tn(dscore, query).astype(BF16)
        if p % 2 == 1:
            for c in range(3):
                half, i = homes[c, p // 2]
                cut = pl.ds(c * width + (p // 2) * 256, 256)
                put(half, i, 0, mm_tn(h_a[...], dqkv[:, cut]).astype(BF16))
        step(*PUMP_PAIRS[p])

    dframe = None
    for c in range(3):
        part = pl.ds(c * width, width)
        term = mm_nt(dqkv[:, part], w_qkv[:, part])
        dframe = term if dframe is None else dframe + term
    dframe = dframe.astype(BF16).astype(F32)
    step(*PUMP_FRAME)
    term, gain_grad_a = norm_back(dframe, norm_a[...], jnp.concatenate(scale_a, axis=0), gain_a[...])
    for r in range(4):
        cut = slice(r * LANES, (r + 1) * LANES)
        gains_acc[0, r : r + 1, :] = gain_grad_a[:, cut]
        gains_acc[0, r + 4 : r + 5, :] = gain_grad_m[:, cut]
    advance(gains_link)
    tok_f[...] = (resid[...] + term).astype(BF16)
    halo_lon.append(halo_go(tok_f, tok_right, grid["left"]))
    step(*PUMP_TAIL)
    for again in range(ROUNDS):
        step(*range(CHUNKS * 2 + 1))
    for copy, rolled_x, rolled_hbm in zip(lat_back, (out_tx, tok_tx), (out_tx_hbm, tok_tx_hbm)):
        arrived(copy)
        store(rolled_x, rolled_hbm)
    for copy in sent:
        copy.wait_send()
    for copy in started:
        copy.wait_send()
    for copy in stores:
        copy.wait()


def finish_kernel(
    rows, cols, total_a_hbm, total_b_hbm, gains, out_t_hbm, out_tx_hbm, tok_t_hbm, tok_tx_hbm,
    block_out, grad_tokens, gain_a, gain_m, grad_qkv, grad_out, grad_up, grad_down,
    total_a, total_b, up, down, out, qkv, tiles, results, in_sems, tile_sems, out_sems,
):
    width = gain_a.shape[1]
    loads, moves = {}, []

    def load_group(i):
        for kind, (src, dst) in enumerate(((total_a_hbm, total_a), (total_b_hbm, total_b))):
            for half in range(2):
                load = pltpu.make_async_copy(src.at[half, i], dst.at[half, i], in_sems.at[kind, half, i])
                load.start()
                loads[kind, half, i] = load

    load_group(0)
    load_group(1)
    tile_loads = [
        pltpu.make_async_copy(src, tiles.at[n], tile_sems.at[n])
        for n, src in enumerate((out_t_hbm, out_tx_hbm, tok_t_hbm, tok_tx_hbm))
    ]
    def move(src, dst):
        copy = pltpu.make_async_copy(src, dst, out_sems.at[len(moves)])
        copy.start()
        moves.append(copy)

    homes = {(0, 1): (0, 0), (1, 1): (1, 0), (0, 2): (2, 0), (1, 2): (0, 1), (0, 3): (1, 1), (1, 3): (2, 1)}
    for i in range(CHUNKS):
        if i == 2:
            for load in tile_loads:
                load.start()
        here = slice(i * 512, (i + 1) * 512)
        for half in range(2):
            loads[0, half, i].wait()
            if half == 0 and i + 2 < CHUNKS:
                load_group(i + 2)
            for b in range(2):
                value = total_a[half, i, b * 512 : (b + 1) * 512, :].astype(F32)
                if half == 0:
                    down[here, b * 256 : (b + 1) * 256] = value
                else:
                    up[:, i * 512 + b * 256 : i * 512 + (b + 1) * 256] = value
        move(down.at[pl.ds(i * 512, 512)], grad_down.at[pl.ds(i * 512, 512)])
        move(up.at[:, pl.ds(i * 512, 512)], grad_up.at[:, pl.ds(i * 512, 512)])
        for half in range(2):
            loads[1, half, i].wait()
            for j in range(2):
                value = total_b[half, i, j * 512 : (j + 1) * 512, :].astype(F32)
                if i == 0:
                    first = half * 256 + j * LANES
                    out[:, first : first + LANES] = value
                else:
                    c, second = homes[half, i]
                    first = c * width + second * 256 + j * LANES
                    qkv[:, first : first + LANES] = value
        if i == 0:
            move(out, grad_out)
    move(qkv, grad_qkv)
    level, row, col = data_cells()
    row, row_out = fold(row + per_level(level, rows), WH)
    pair = roll_pair(row * LEVELS * WW + level * WW + col, row_out, CELLS)
    for load in tile_loads:
        load.wait()
    for n, result in enumerate((block_out, grad_tokens)):
        results[n] = apply_roll(pair, tiles[2 * n], tiles[2 * n + 1]).reshape(result.shape)
        move(results.at[n], result)
    for r in range(4):
        cut = slice(r * LANES, (r + 1) * LANES)
        gain_a[:, cut] = gains[r : r + 1, :]
        gain_m[:, cut] = gains[r + 4 : r + 5, :]
    for copy in moves:
        copy.wait()


VMEM = pl.BlockSpec(memory_space=pltpu.VMEM)
SMEM = pl.BlockSpec(memory_space=pltpu.SMEM)
ANY = pl.BlockSpec(memory_space=pl.ANY)
DMA = pltpu.SemaphoreType.DMA


def call(kernel, outs, in_specs, out_specs, scratch, name, collective_id=None):
    params = {"vmem_limit_bytes": VMEM_BYTES}
    if collective_id is not None:
        params.update(collective_id=collective_id, has_side_effects=True)
    return pl.pallas_call(
        kernel,
        out_shape=[jax.ShapeDtypeStruct(shape, dtype) for shape, dtype in outs],
        in_specs=in_specs,
        out_specs=out_specs,
        scratch_shapes=scratch,
        compiler_params=pltpu.CompilerParams(**params),
        name=name,
    )


def sum_buffers(lanes):
    shapes = [
        (2, CHUNKS, PART, lanes),
        (CHUNKS, PART, lanes),
        (CHUNKS, PART, lanes),
        (CHUNKS, SIDE - 1, QUARTER, lanes),
        (CHUNKS, QUARTER, lanes),
        (CHUNKS, SIDE - 1, SHARE, lanes),
        (CHUNKS, SHARE, lanes),
        (CHUNKS, SIDE - 1, SHARE, lanes),
        (2, CHUNKS, PART, lanes),
    ]
    return [pltpu.VMEM(shape, BF16) for shape in shapes]


def native(field):
    return field.transpose(1, 2, 0, 3).reshape(-1, field.shape[0], field.shape[3])


def on_device(
    tokens,
    region_ids,
    shift_lat,
    shift_lon,
    gain_attn,
    w_qkv,
    w_out,
    gain_mlp,
    w_up,
    w_down,
    cotangent,
):
    levels, lat_rows, lon_cols, width = tokens.shape
    cells = levels * lat_rows * lon_cols
    ff = w_up.shape[1]
    lines = (lat_rows * lon_cols, levels, width)
    tile = ((cells, width), BF16)
    half, full = pltpu.VMEM((cells, width), BF16), pltpu.VMEM((cells, width), F32)
    total_a, total_b, gains_sum, *rolled = call(
        block_kernel,
        [((2, CHUNKS, PART, 256), BF16), ((2, CHUNKS, PART, LANES), BF16), ((8, LANES), F32)] + [tile] * 4,
        [SMEM] * 2 + [VMEM] * 5 + [ANY] * 4,
        [ANY] * 2 + [VMEM] + [ANY] * 4,
        [pltpu.VMEM(w.shape, BF16) for w in (w_qkv, w_out, w_up, w_down)]
        + [pltpu.VMEM(lines, BF16), pltpu.VMEM((lat_rows, lon_cols, levels, width), BF16)]
        + [half] * 4
        + [pltpu.VMEM((16, LANES), jnp.int32)] * 2
        + [
            half,
            full,
            pltpu.VMEM((cells, LANES), BF16),
            full,
            half,
            pltpu.VMEM((cells, 3 * width), BF16),
            pltpu.VMEM((HEADS, 2 * WIN, WIN), F32),
            half,
            full,
            full,
            half,
            full,
            pltpu.VMEM((cells, 3 * width), BF16),
        ]
        + [half] * 8
        + [pltpu.VMEM((4, 8, LANES), F32), pltpu.VMEM((10, 8, LANES), F32)]
        + sum_buffers(256)
        + sum_buffers(LANES)
        + [
            DMA((4,)),
            DMA((20,)),
            DMA((20,)),
            DMA((2 * CHUNKS, ROUNDS)),
            DMA((2 * CHUNKS, ROUNDS)),
            DMA((10,)),
            DMA((10,)),
            DMA((4 * CHUNKS + 4,)),
        ],
        "block",
        0,
    )(
        shift_lat, shift_lon, native(tokens), cotangent.transpose(1, 2, 0, 3), region_ids,
        gain_attn.reshape(1, width), gain_mlp.reshape(1, width), w_qkv, w_out, w_up, w_down,
    )
    results = call(
        finish_kernel,
        [
            (lines, BF16),
            (lines, BF16),
            ((1, width), F32),
            ((1, width), F32),
            ((width, 3 * width), F32),
            ((width, width), F32),
            ((width, ff), F32),
            ((ff, width), F32),
        ],
        [SMEM] * 2 + [ANY] * 2 + [VMEM] + [ANY] * 4,
        [ANY] * 2 + [VMEM] * 2 + [ANY] * 4,
        [
            pltpu.VMEM((2, CHUNKS, PART, 256), BF16),
            pltpu.VMEM((2, CHUNKS, PART, LANES), BF16),
            pltpu.VMEM(w_up.shape, F32),
            pltpu.VMEM(w_down.shape, F32),
            pltpu.VMEM(w_out.shape, F32),
            pltpu.VMEM(w_qkv.shape, F32),
            pltpu.VMEM((4, cells, width), BF16),
            pltpu.VMEM((2,) + lines, BF16),
            DMA((2, 2, CHUNKS)),
            DMA((4,)),
            DMA((2 * CHUNKS + 4,)),
        ],
        "finish",
    )(shift_lat, shift_lon, total_a, total_b, gains_sum, *rolled)
    block_out, grad_tokens, grad_gain_attn, grad_gain_mlp, grad_qkv, grad_out, grad_up, grad_down = results

    def whole(field):
        return field.reshape(lat_rows, lon_cols, levels, width).transpose(2, 0, 1, 3)

    return (
        whole(block_out),
        whole(grad_tokens),
        grad_gain_attn.reshape(width),
        grad_qkv,
        grad_out,
        grad_gain_mlp.reshape(width),
        grad_up,
        grad_down,
    )


def solution(mesh):
    placed = (
        P(None, "lat", "lon", None),
        P("lat", "lon"),
        P(),
        P(),
        P(),
        P(),
        P(),
        P(),
        P(),
        P(),
        P(None, "lat", "lon", None),
    )
    return jax.shard_map(
        on_device,
        mesh=mesh,
        in_specs=placed,
        out_specs=(
            P(None, "lat", "lon", None),
            P(None, "lat", "lon", None),
            P(),
            P(),
            P(),
            P(),
            P(),
            P(),
        ),
        check_vma=False,
    )
```

```python
import functools

import jax
import jax.numpy as jnp
from jax import lax
from jax.experimental import pallas as pl
from jax.experimental.pallas import tpu as pltpu
from jax.sharding import PartitionSpec as P

HEADS = 8
WV = 2
WH = 6
WW = 12
WIN = WV * WH * WW
PLANE = WH * WW
LANES = 128
LEVELS = 4
CELLS = LEVELS * PLANE
SIDE = 4
EPS = 1e-05
MESH = pl.DeviceIdType.MESH
F32 = jnp.float32
BF16 = jnp.bfloat16
CHUNKS = 4
ORDER = ((0, 1, 2), (1, 2, 0), (2, 0, 1), (2, 1, 0), (1, 0, 2), (1, 2, 0), (0, 1, 2), (2, 1, 0))
GAINS, OUT, TOK = 8, 9, 10
PUMP_MLP = ((0,), (1,), (2, 0), (3, 1, 2))
PUMP_OUT, PUMP_MIX = (4,), ()
PUMP_PAIRS = ((3, 4), (5,), (), (6, 7))
PUMP_FRAME = (5, 0, 6, 7, 1, 2)
PUMP_TAIL = (8, 4, 9, 5, 3, 0, 6, 2, 7, 1, 5, 3, 6, 0, 2, 7, 8, 10, 4, 6, 0, 8, 1, 5, 3, 4, 8, 2, 7, 6, 1, 5, 3, 7, 0, 4, 0, 2, 6, 1, 2, 6, 1, 5, 3, 5, 4, 3, 7, 4, 7)
PART = 1024
QUARTER = 256
SHARE = 64
ROUNDS = 7
VMEM_BYTES = 60 * 1024 * 1024
DIMS_ZERO = (((0,), (0,)), ((), ()))
DIMS_LAST = (((1,), (1,)), ((), ()))


def mm(a, b):
    return jnp.dot(a, b, preferred_element_type=F32)


def mm_tn(a, b):
    return lax.dot_general(a, b, DIMS_ZERO, preferred_element_type=F32)


def mm_nt(a, b):
    return lax.dot_general(a, b, DIMS_LAST, preferred_element_type=F32)


def norm_stats(values):
    center = values - jnp.mean(values, axis=-1, keepdims=True)
    inv_scale = lax.rsqrt(jnp.mean(center * center, axis=-1, keepdims=True) + EPS)
    return (center * inv_scale, inv_scale)


def norm_back(grad, normed, inv_scale, gain):
    gain_grad = jnp.sum(grad * normed, axis=0, keepdims=True)
    graded = grad * gain
    term = inv_scale * (
        graded
        - jnp.mean(graded, axis=-1, keepdims=True)
        - normed * jnp.mean(graded * normed, axis=-1, keepdims=True)
    )
    return (term, gain_grad)


def places():
    lat, lon = lax.axis_index("lat"), lax.axis_index("lon")
    lats, lons = lax.axis_size("lat"), lax.axis_size("lon")
    core, y_hi = lax.rem(lat, 2), lat // 2
    x, y_lo, z = lax.rem(lon, SIDE), lax.rem(lon // SIDE, 2), lon // (2 * SIDE)
    y = y_hi * 2 + y_lo

    def device(x, y, z):
        x, y, z = lax.rem(x, SIDE), lax.rem(y, SIDE), lax.rem(z, SIDE)
        return ((y // 2) * 2 + core, z * 2 * SIDE + lax.rem(y, 2) * SIDE + x)

    spot = (x, y, z)

    def away(offset):
        return device(*[p + o for p, o in zip(spot, offset)])

    peers = [[away([j * (a == b) for b in range(3)]) for j in range(1, SIDE)] for a in range(3)]
    grid = {
        "below": (lax.rem(lat + 1, lats), lon),
        "above": (lax.rem(lat + lats - 1, lats), lon),
        "right": (lat, lax.rem(lon + 1, lons)),
        "left": (lat, lax.rem(lon + lons - 1, lons)),
    }
    return grid, core, (y_hi * 2 + 1 - core, lon), peers, spot


def remote(src, dst, send, recv, device):
    return pltpu.make_async_remote_copy(
        src_ref=src, dst_ref=dst, send_sem=send, recv_sem=recv, device_id=device, device_id_type=MESH
    )


def div(value, by):
    return jnp.floor((value.astype(F32) + 0.5) * (1.0 / by)).astype(jnp.int32)


def frame_cells(start, count):
    cell = start + lax.broadcasted_iota(jnp.int32, (count, 1), 0)
    level = div(cell, PLANE)
    row = div(cell - level * PLANE, WW)
    return level, row, cell - level * PLANE - row * WW


def data_cells():
    cell = lax.broadcasted_iota(jnp.int32, (CELLS, 1), 0)
    spot = div(cell, LEVELS)
    row = div(spot, WW)
    return cell - spot * LEVELS, row, spot - row * WW


def row_cells():
    cell = lax.broadcasted_iota(jnp.int32, (CELLS, 1), 0)
    row = div(cell, LEVELS * WW)
    level = div(cell - row * LEVELS * WW, WW)
    return level, row, cell - row * LEVELS * WW - level * WW


def per_level(level, ref):
    value = ref[LEVELS - 1]
    for k in reversed(range(LEVELS - 1)):
        value = jnp.where(level == k, ref[k], value)
    return value


def fold(value, limit):
    out = ((value < 0) | (value >= limit)).astype(jnp.int32)
    return jnp.where(value < 0, value + limit, jnp.where(value >= limit, value - limit, value)), out


def one_hot(hit, index, width):
    lanes = lax.broadcasted_iota(jnp.int32, (index.shape[0], width), 1)
    return jnp.where((lanes == index) & hit, 1.0, 0.0).astype(BF16)


def roll_pair(index, out, width):
    return one_hot(out == 0, index, width), one_hot(out == 1, index, width)


def apply_roll(pair, here, there):
    return (mm(pair[0], here) + mm(pair[1], there)).astype(BF16)


def block_kernel(
    rows, cols, tok_in, cot_in, ids_in, gain_a, gain_m, w_qkv_hbm, w_out_hbm, w_up_hbm, w_down_hbm,
    total_a_hbm, total_b_hbm, gains_sum, out_t_hbm, out_tx_hbm, tok_t_hbm, tok_tx_hbm,
    w_qkv, w_out, w_up, w_down,
    tok_above, cot_left, tok_rows, tok_left, cot_cols, cot_above, ids, ids_x,
    cotf, tokf, labf, norm_a, h_a, qkv, probs, mixed, resid, norm_m, h_m, dh, dqkv,
    out_f, out_right, tok_f, tok_right, out_t, out_tx, tok_t, tok_tx, gains_acc, gains_in,
    part_a, core_a, mine_a, r1_a, m1_a, r2_a, m2_a, r3_a, total_a,
    part_b, core_b, mine_b, r1_b, m1_b, r2_b, m2_b, r3_b, total_b,
    load_sem, halo_send, halo_recv, sum_send, sum_recv, gain_send, gain_recv, store_sem,
):
    width = gain_a.shape[1]
    grid, core, core_peer, peers, position = places()
    loads = [
        pltpu.make_async_copy(src, dst, load_sem.at[k])
        for k, (src, dst) in enumerate(
            ((w_qkv_hbm, w_qkv), (w_out_hbm, w_out), (w_up_hbm, w_up), (w_down_hbm, w_down))
        )
    ]
    greeted = [core_peer] + [p for axis in peers for p in axis] + list(grid.values())
    barrier = pltpu.get_barrier_semaphore()
    for device in greeted:
        pl.semaphore_signal(barrier, inc=1, device_id=device, device_id_type=MESH)
    for load in loads:
        load.start()

    started = []
    stores = []

    def go(*args):
        copy = remote(*args)
        copy.start()
        started.append(copy)
        return copy

    halos = []

    def halo_go(src, dst, device):
        k = len(halos)
        halos.append(go(src, dst, halo_send.at[k], halo_recv.at[k], device))
        return halos[-1]

    def halo_split(src, dst, device, start, count, pieces):
        size = count // pieces
        cuts = [pl.ds(start + n * size, size) for n in range(pieces)]
        return [halo_go(src.at[cut], dst.at[cut], device) for cut in cuts]

    def arrived(copies):
        for copy in copies:
            copy.wait_recv()

    def window(w):
        return pl.ds(w * WIN, WIN)

    ids[0:8, :] = jnp.zeros((8, LANES), jnp.int32)
    ids[0:WH, 0:WW] = ids_in[...]
    tok_above[0:WW] = jnp.zeros((WW, LEVELS, width), BF16)
    cot_left[:, 0:1] = jnp.zeros((WH, 1, LEVELS, width), BF16)
    line = LEVELS * WW
    cot_above[0:line, :] = jnp.zeros((line, width), BF16)
    used_cols = pl.ds(1, WW - 1)
    pl.semaphore_wait(barrier, len(greeted))
    lat_tok = halo_split(tok_in, tok_above, grid["below"], WW, PLANE - WW, 4)
    lat_ids = halo_go(ids.at[pl.ds(0, 8)], ids.at[pl.ds(8, 8)], grid["below"])
    lon_cot = halo_go(cot_in.at[:, used_cols], cot_left.at[:, used_cols], grid["right"])
    level, row, col = row_cells()
    col, col_out = fold(col - per_level(level, cols), WW)
    first_pair = roll_pair((row * WW + col) * LEVELS + level, col_out, CELLS)
    level, row, col = frame_cells(0, CELLS)
    row, row_out = fold(row - per_level(level, rows), WH)
    second_pair = roll_pair(row * line + level * WW + col, row_out, CELLS)
    level, row, col = frame_cells(0, CELLS)
    row, row_out = fold(row - per_level(level, rows), WH)
    row_pair = roll_pair((row * WW + col) * LEVELS + level, row_out, CELLS)
    level, row, col = frame_cells(0, CELLS)
    col, col_out = fold(col - per_level(level, cols), WW)
    col_index = lax.rem(level, WV) * PLANE + row * WW + col
    col_pairs = [
        roll_pair(col_index[w * WIN : (w + 1) * WIN], col_out[w * WIN : (w + 1) * WIN], WIN) for w in range(2)
    ]
    arrived(lat_tok)
    tok_rows[...] = apply_roll(
        row_pair, tok_in[...].reshape(CELLS, width), tok_above[...].reshape(CELLS, width)
    )
    lon_tok = [halo_go(tok_rows.at[window(w)], tok_left.at[window(w)], grid["right"]) for w in range(2)]
    lat_ids.wait_recv()
    lon_ids = halo_go(ids, ids_x, grid["right"])
    lon_cot.wait_recv()
    cot_cols[...] = apply_roll(
        first_pair, cot_in[...].reshape(CELLS, width), cot_left[...].reshape(CELLS, width)
    )
    lat_cot = halo_split(cot_cols, cot_above, grid["below"], line, CELLS - line, 3)

    lon_ids.wait_recv()
    ids_all = jnp.concatenate([ids[...], ids_x[...]], axis=0).astype(F32).astype(BF16)
    level, row, col = frame_cells(0, CELLS)
    row, row_out = fold(row - per_level(level, rows), WH)
    col, col_out = fold(col - per_level(level, cols), WW)
    picked = mm(one_hot(level >= 0, (row_out + 2 * col_out) * 8 + row, 32), ids_all)
    lanes = lax.broadcasted_iota(jnp.int32, (CELLS, LANES), 1)
    label = jnp.sum(jnp.where(lanes == col, picked, 0.0), axis=-1, keepdims=True)
    labf[...] = jnp.where(lanes.astype(F32) == label, 1.0, 0.0).astype(BF16)
    scale_a = []

    def forward_in(w):
        here = window(w)
        lon_tok[w].wait_recv()
        values = apply_roll(col_pairs[w], tok_rows[here, :], tok_left[here, :]).astype(F32)
        tokf[here, :] = values
        normed, scale = norm_stats(values)
        scale_a.append(scale)
        norm_a[here, :] = normed
        h_a[here, :] = (normed * gain_a[...]).astype(BF16)
        if w == 0:
            loads[0].wait()
        for c in range(3):
            part = pl.ds(c * width, width)
            qkv[here, part] = mm(h_a[here, :], w_qkv[:, part]).astype(BF16)

    low = lax.broadcasted_iota(jnp.int32, (1, LANES), 1) < LANES // 2

    def pair_stack(block):
        zero = jnp.zeros_like(block)
        return jnp.concatenate([jnp.where(low, block, zero), jnp.where(low, zero, block)], axis=0)

    def pair_join(stack):
        return jnp.where(low, stack[:WIN], stack[WIN:])

    def pair_lanes(p):
        return [pl.ds(part * width + p * LANES, LANES) for part in range(3)]

    for w in range(2):
        here = window(w)
        forward_in(w)
        allowed = mm_nt(labf[here, :], labf[here, :]) > 0.5
        allowed = jnp.concatenate([allowed, allowed], axis=0)
        for p in range(HEADS // 2):
            lanes = pair_lanes(p)
            query = pair_stack(qkv[here, lanes[0]])
            scores = mm_nt(query, qkv[here, lanes[1]]) * 0.125
            scores = jnp.where(allowed, scores, -jnp.inf)
            expo = jnp.exp(scores - jnp.max(scores, axis=-1, keepdims=True))
            prob = expo * (1.0 / jnp.sum(expo, axis=-1, keepdims=True))
            probs[w * 4 + p] = prob
            mixed[here, pl.ds(p * LANES, LANES)] = pair_join(
                mm(prob.astype(BF16), qkv[here, lanes[2]])
            ).astype(BF16)

    for load in loads[1:]:
        load.wait()
    attn = mm(mixed[...], w_out[...]).astype(BF16).astype(F32)
    resid[...] = tokf[...] + attn
    normed, scale_m = norm_stats(resid[...])
    norm_m[...] = normed
    h_m[...] = (normed * gain_m[...]).astype(BF16)
    dh[...] = jnp.zeros_like(dh)
    arrived(lat_cot)
    cotf[...] = apply_roll(second_pair, cot_cols[...], cot_above[...])

    set_a = (part_a, core_a, mine_a, r1_a, m1_a, r2_a, m2_a, r3_a, total_a, total_a_hbm)
    set_b = (part_b, core_b, mine_b, r1_b, m1_b, r2_b, m2_b, r3_b, total_b, total_b_hbm)
    sent = []

    def block(offset, count):
        return pl.ds(pl.multiple_of(offset, 16), count)

    def store(src, dst):
        copy = pltpu.make_async_copy(src, dst, store_sem.at[len(stores)])
        copy.start()
        stores.append(copy)

    def chain(refs, i, k):
        partial, core_in, mine, r1, m1, r2, m2, r3, total, total_hbm = refs
        first, second, third = ORDER[k]
        at, then = position[first], position[second]

        def send(n, src, dst, device):
            remote(src, dst, sum_send.at[k, n], sum_recv.at[k, n], device).start()

        def arrive(n, like):
            whole = remote(like, like, sum_send.at[k, n], sum_recv.at[k, n], core_peer)
            sent.append(whole)
            whole.wait_recv()

        send(0, partial.at[1 - core, i], core_in.at[i], core_peer)
        yield
        arrive(0, core_in.at[i])
        mine[i] = (partial[core, i].astype(F32) + core_in[i].astype(F32)).astype(BF16)
        for j in range(1, SIDE):
            quarter = block(lax.rem(at + j, SIDE) * QUARTER, QUARTER)
            send(1, mine.at[i, quarter], r1.at[i, j - 1], peers[first][j - 1])
        yield
        arrive(1, r1.at[i])
        summed = mine[i, block(at * QUARTER, QUARTER), :].astype(F32)
        for j in range(SIDE - 1):
            summed = summed + r1[i, j].astype(F32)
        m1[i] = summed.astype(BF16)
        for j in range(1, SIDE):
            share = block(lax.rem(then + j, SIDE) * SHARE, SHARE)
            send(2, m1.at[i, share], r2.at[i, j - 1], peers[second][j - 1])
        yield
        arrive(2, r2.at[i])
        summed = m1[i, block(then * SHARE, SHARE), :].astype(F32)
        for j in range(SIDE - 1):
            summed = summed + r2[i, j].astype(F32)
        m2[i] = summed.astype(BF16)
        for j in range(SIDE - 1):
            send(3, m2.at[i], r3.at[i, j], peers[third][j])
        yield
        arrive(3, r3.at[i])
        near, far = r3[i, 0].astype(F32) + r3[i, 2].astype(F32), m2[i].astype(F32) + r3[i, 1].astype(F32)
        place = (core, i, block(at * QUARTER + then * SHARE, SHARE))
        total[place] = (near + far).astype(BF16)
        for device in peers[second]:
            send(4, total.at[place], total.at[place], device)
        yield
        arrive(4, r2.at[i])
        place = (core, i, block(at * QUARTER, QUARTER))
        for device in peers[first]:
            send(5, total.at[place], total.at[place], device)
        yield
        arrive(5, r1.at[i])
        send(6, total.at[core, i], total.at[core, i], core_peer)
        store(total.at[core, i], total_hbm.at[core, i])
        yield
        arrive(6, core_in.at[i])
        store(total.at[1 - core, i], total_hbm.at[1 - core, i])

    def gain_chain():
        used = [0]

        def send(src, device):
            n = used[0]
            used[0] += 1
            return go(src, gains_in.at[n], gain_send.at[n], gain_recv.at[n], device)

        copy = send(gains_acc.at[0], core_peer)
        yield
        copy.wait_recv()
        gains_acc[1] = gains_acc[0] + gains_in[0]
        for axis in range(3):
            copies = [send(gains_acc.at[axis + 1], peer) for peer in peers[axis]]
            yield
            for copy in copies:
                copy.wait_recv()
            base = 1 + 3 * axis
            summed = (gains_acc[axis + 1] + gains_in[base + 1]) + (gains_in[base] + gains_in[base + 2])
            if axis < 2:
                gains_acc[axis + 2] = summed
            else:
                gains_sum[...] = summed

    def advance(*chains):
        for link in chains:
            next(link, None)

    chains = [chain(set_a, i, i) for i in range(CHUNKS)]
    chains += [chain(set_b, i, CHUNKS + i) for i in range(CHUNKS)]

    def step(*which):
        for i in which:
            next(chains[i], None)

    level, row, col = row_cells()
    col, col_out = fold(col + per_level(level, cols), WW)
    back_pair = roll_pair(level * PLANE + row * WW + col, col_out, CELLS)

    def turn(arrived, own, other, rolled, rolled_x, rolled_hbm):
        arrived.wait_recv()
        rolled[...] = apply_roll(back_pair, own[...], other[...])
        rolled_x[pl.ds(CELLS - LEVELS * WW, LEVELS * WW), :] = jnp.zeros((LEVELS * WW, width), BF16)
        store(rolled, rolled_hbm)
        return halo_split(rolled, rolled_x, grid["above"], 0, CELLS - line, 3)

    gains_link = gain_chain()
    chains.append(gains_link)
    lat_back, halo_lon = [], []

    def out_back():
        lat_back.append(turn(halo_lon[0], out_f, out_right, out_t, out_tx, out_t_hbm))
        yield

    def tok_back():
        lat_back.append(turn(halo_lon[1], tok_f, tok_right, tok_t, tok_tx, tok_t_hbm))
        yield

    chains.extend((out_back(), tok_back()))
    for c in range(CHUNKS):
        part = pl.ds(c * 512, 512)
        pre = mm(h_m[...], w_up[:, part])
        cdf = 0.5 * (1.0 + lax.erf(pre * 0.7071067811865476))
        act = (pre * cdf).astype(BF16)
        slope = cdf + pre * jnp.exp(-0.5 * pre * pre) * 0.3989422804014327
        resid[...] += mm(act, w_down[part, :])
        grad_pre = (mm_nt(cotf[...], w_down[part, :]) * slope).astype(BF16)
        dh[...] += mm_nt(grad_pre, w_up[:, part])
        down = mm_tn(act, cotf[...]).astype(BF16)
        up = mm_tn(h_m[...], grad_pre).astype(BF16)
        for b in range(2):
            spot = slice(b * 512, (b + 1) * 512)
            cut = slice(b * 256, (b + 1) * 256)
            part_a[0, c, spot, :] = down[:, cut]
            part_a[1, c, spot, :] = up[:, cut]
        step(*PUMP_MLP[c])
    out_f[...] = resid[...].astype(BF16)
    halo_lon.append(halo_go(out_f, out_right, grid["left"]))
    term, gain_grad_m = norm_back(dh[...], norm_m[...], scale_m, gain_m[...])
    resid[...] = cotf[...].astype(F32) + term
    grad_attn = resid[...].astype(BF16)

    def put(half, i, b, value):
        for j in range(2):
            part_b[half, i, j * 512 : (j + 1) * 512, :] = value[:, b + j * LANES : b + (j + 1) * LANES]

    grad_out = mm_tn(mixed[...], grad_attn).astype(BF16)
    put(0, 0, 0, grad_out)
    put(1, 0, 256, grad_out)
    step(*PUMP_OUT)
    mixed[...] = mm_nt(grad_attn, w_out[...]).astype(BF16)
    step(*PUMP_MIX)

    homes = {(0, 0): (0, 1), (1, 0): (1, 1), (2, 0): (0, 2), (0, 1): (1, 2), (1, 1): (0, 3), (2, 1): (1, 3)}
    for p in range(HEADS // 2):
        lanes = pair_lanes(p)
        for w in range(2):
            here = window(w)
            prob = probs[w * 4 + p]
            dmix = pair_stack(mixed[here, pl.ds(p * LANES, LANES)])
            query = pair_stack(qkv[here, lanes[0]])
            dprob = mm_nt(dmix, qkv[here, lanes[2]])
            dqkv[here, lanes[2]] = mm_tn(prob.astype(BF16), dmix).astype(BF16)
            dscore = prob * (dprob - jnp.sum(dprob * prob, axis=-1, keepdims=True)) * 0.125
            dscore = dscore.astype(BF16)
            dqkv[here, lanes[0]] = pair_join(mm(dscore, qkv[here, lanes[1]])).astype(BF16)
            dqkv[here, lanes[1]] = mm_tn(dscore, query).astype(BF16)
        if p % 2 == 1:
            for c in range(3):
                half, i = homes[c, p // 2]
                cut = pl.ds(c * width + (p // 2) * 256, 256)
                put(half, i, 0, mm_tn(h_a[...], dqkv[:, cut]).astype(BF16))
        step(*PUMP_PAIRS[p])

    dframe = None
    for c in range(3):
        part = pl.ds(c * width, width)
        term = mm_nt(dqkv[:, part], w_qkv[:, part])
        dframe = term if dframe is None else dframe + term
    dframe = dframe.astype(BF16).astype(F32)
    step(*PUMP_FRAME)
    term, gain_grad_a = norm_back(dframe, norm_a[...], jnp.concatenate(scale_a, axis=0), gain_a[...])
    for r in range(4):
        cut = slice(r * LANES, (r + 1) * LANES)
        gains_acc[0, r : r + 1, :] = gain_grad_a[:, cut]
        gains_acc[0, r + 4 : r + 5, :] = gain_grad_m[:, cut]
    advance(gains_link)
    tok_f[...] = (resid[...] + term).astype(BF16)
    halo_lon.append(halo_go(tok_f, tok_right, grid["left"]))
    step(*PUMP_TAIL)
    for again in range(ROUNDS):
        step(*range(CHUNKS * 2 + 1))
    for copy, rolled_x, rolled_hbm in zip(lat_back, (out_tx, tok_tx), (out_tx_hbm, tok_tx_hbm)):
        arrived(copy)
        store(rolled_x, rolled_hbm)
    for copy in sent:
        copy.wait_send()
    for copy in started:
        copy.wait_send()
    for copy in stores:
        copy.wait()


def finish_kernel(
    rows, cols, total_a_hbm, total_b_hbm, gains, out_t_hbm, out_tx_hbm, tok_t_hbm, tok_tx_hbm,
    block_out, grad_tokens, gain_a, gain_m, grad_qkv, grad_out, grad_up, grad_down,
    total_a, total_b, up, down, out, qkv, tiles, results, in_sems, tile_sems, out_sems,
):
    width = gain_a.shape[1]
    loads, moves = {}, []

    def load_group(i):
        for kind, (src, dst) in enumerate(((total_a_hbm, total_a), (total_b_hbm, total_b))):
            for half in range(2):
                load = pltpu.make_async_copy(src.at[half, i], dst.at[half, i], in_sems.at[kind, half, i])
                load.start()
                loads[kind, half, i] = load

    load_group(0)
    load_group(1)
    tile_loads = [
        pltpu.make_async_copy(src, tiles.at[n], tile_sems.at[n])
        for n, src in enumerate((out_t_hbm, out_tx_hbm, tok_t_hbm, tok_tx_hbm))
    ]
    def move(src, dst):
        copy = pltpu.make_async_copy(src, dst, out_sems.at[len(moves)])
        copy.start()
        moves.append(copy)

    homes = {(0, 1): (0, 0), (1, 1): (1, 0), (0, 2): (2, 0), (1, 2): (0, 1), (0, 3): (1, 1), (1, 3): (2, 1)}
    for i in range(CHUNKS):
        if i == 2:
            for load in tile_loads:
                load.start()
        here = slice(i * 512, (i + 1) * 512)
        for half in range(2):
            loads[0, half, i].wait()
            if half == 0 and i + 2 < CHUNKS:
                load_group(i + 2)
            for b in range(2):
                value = total_a[half, i, b * 512 : (b + 1) * 512, :].astype(F32)
                if half == 0:
                    down[here, b * 256 : (b + 1) * 256] = value
                else:
                    up[:, i * 512 + b * 256 : i * 512 + (b + 1) * 256] = value
        move(down.at[pl.ds(i * 512, 512)], grad_down.at[pl.ds(i * 512, 512)])
        move(up.at[:, pl.ds(i * 512, 512)], grad_up.at[:, pl.ds(i * 512, 512)])
        for half in range(2):
            loads[1, half, i].wait()
            for j in range(2):
                value = total_b[half, i, j * 512 : (j + 1) * 512, :].astype(F32)
                if i == 0:
                    first = half * 256 + j * LANES
                    out[:, first : first + LANES] = value
                else:
                    c, second = homes[half, i]
                    first = c * width + second * 256 + j * LANES
                    qkv[:, first : first + LANES] = value
        if i == 0:
            move(out, grad_out)
    move(qkv, grad_qkv)
    level, row, col = data_cells()
    row, row_out = fold(row + per_level(level, rows), WH)
    pair = roll_pair(row * LEVELS * WW + level * WW + col, row_out, CELLS)
    for load in tile_loads:
        load.wait()
    for n, result in enumerate((block_out, grad_tokens)):
        results[n] = apply_roll(pair, tiles[2 * n], tiles[2 * n + 1]).reshape(result.shape)
        move(results.at[n], result)
    for r in range(4):
        cut = slice(r * LANES, (r + 1) * LANES)
        gain_a[:, cut] = gains[r : r + 1, :]
        gain_m[:, cut] = gains[r + 4 : r + 5, :]
    for copy in moves:
        copy.wait()


VMEM = pl.BlockSpec(memory_space=pltpu.VMEM)
SMEM = pl.BlockSpec(memory_space=pltpu.SMEM)
ANY = pl.BlockSpec(memory_space=pl.ANY)
DMA = pltpu.SemaphoreType.DMA


def call(kernel, outs, in_specs, out_specs, scratch, name, collective_id=None):
    params = {"vmem_limit_bytes": VMEM_BYTES}
    if collective_id is not None:
        params.update(collective_id=collective_id, has_side_effects=True)
    return pl.pallas_call(
        kernel,
        out_shape=[jax.ShapeDtypeStruct(shape, dtype) for shape, dtype in outs],
        in_specs=in_specs,
        out_specs=out_specs,
        scratch_shapes=scratch,
        compiler_params=pltpu.CompilerParams(**params),
        name=name,
    )


def sum_buffers(lanes):
    shapes = [
        (2, CHUNKS, PART, lanes),
        (CHUNKS, PART, lanes),
        (CHUNKS, PART, lanes),
        (CHUNKS, SIDE - 1, QUARTER, lanes),
        (CHUNKS, QUARTER, lanes),
        (CHUNKS, SIDE - 1, SHARE, lanes),
        (CHUNKS, SHARE, lanes),
        (CHUNKS, SIDE - 1, SHARE, lanes),
        (2, CHUNKS, PART, lanes),
    ]
    return [pltpu.VMEM(shape, BF16) for shape in shapes]


def native(field):
    return field.transpose(1, 2, 0, 3).reshape(-1, field.shape[0], field.shape[3])


def on_device(
    tokens,
    region_ids,
    shift_lat,
    shift_lon,
    gain_attn,
    w_qkv,
    w_out,
    gain_mlp,
    w_up,
    w_down,
    cotangent,
):
    levels, lat_rows, lon_cols, width = tokens.shape
    cells = levels * lat_rows * lon_cols
    ff = w_up.shape[1]
    lines = (lat_rows * lon_cols, levels, width)
    tile = ((cells, width), BF16)
    half, full = pltpu.VMEM((cells, width), BF16), pltpu.VMEM((cells, width), F32)
    total_a, total_b, gains_sum, *rolled = call(
        block_kernel,
        [((2, CHUNKS, PART, 256), BF16), ((2, CHUNKS, PART, LANES), BF16), ((8, LANES), F32)] + [tile] * 4,
        [SMEM] * 2 + [VMEM] * 5 + [ANY] * 4,
        [ANY] * 2 + [VMEM] + [ANY] * 4,
        [pltpu.VMEM(w.shape, BF16) for w in (w_qkv, w_out, w_up, w_down)]
        + [pltpu.VMEM(lines, BF16), pltpu.VMEM((lat_rows, lon_cols, levels, width), BF16)]
        + [half] * 4
        + [pltpu.VMEM((16, LANES), jnp.int32)] * 2
        + [
            half,
            full,
            pltpu.VMEM((cells, LANES), BF16),
            full,
            half,
            pltpu.VMEM((cells, 3 * width), BF16),
            pltpu.VMEM((HEADS, 2 * WIN, WIN), F32),
            half,
            full,
            full,
            half,
            full,
            pltpu.VMEM((cells, 3 * width), BF16),
        ]
        + [half] * 8
        + [pltpu.VMEM((4, 8, LANES), F32), pltpu.VMEM((10, 8, LANES), F32)]
        + sum_buffers(256)
        + sum_buffers(LANES)
        + [
            DMA((4,)),
            DMA((20,)),
            DMA((20,)),
            DMA((2 * CHUNKS, ROUNDS)),
            DMA((2 * CHUNKS, ROUNDS)),
            DMA((10,)),
            DMA((10,)),
            DMA((4 * CHUNKS + 4,)),
        ],
        "block",
        0,
    )(
        shift_lat, shift_lon, native(tokens), cotangent.transpose(1, 2, 0, 3), region_ids,
        gain_attn.reshape(1, width), gain_mlp.reshape(1, width), w_qkv, w_out, w_up, w_down,
    )
    results = call(
        finish_kernel,
        [
            (lines, BF16),
            (lines, BF16),
            ((1, width), F32),
            ((1, width), F32),
            ((width, 3 * width), F32),
            ((width, width), F32),
            ((width, ff), F32),
            ((ff, width), F32),
        ],
        [SMEM] * 2 + [ANY] * 2 + [VMEM] + [ANY] * 4,
        [ANY] * 2 + [VMEM] * 2 + [ANY] * 4,
        [
            pltpu.VMEM((2, CHUNKS, PART, 256), BF16),
            pltpu.VMEM((2, CHUNKS, PART, LANES), BF16),
            pltpu.VMEM(w_up.shape, F32),
            pltpu.VMEM(w_down.shape, F32),
            pltpu.VMEM(w_out.shape, F32),
            pltpu.VMEM(w_qkv.shape, F32),
            pltpu.VMEM((4, cells, width), BF16),
            pltpu.VMEM((2,) + lines, BF16),
            DMA((2, 2, CHUNKS)),
            DMA((4,)),
            DMA((2 * CHUNKS + 4,)),
        ],
        "finish",
    )(shift_lat, shift_lon, total_a, total_b, gains_sum, *rolled)
    block_out, grad_tokens, grad_gain_attn, grad_gain_mlp, grad_qkv, grad_out, grad_up, grad_down = results

    def whole(field):
        return field.reshape(lat_rows, lon_cols, levels, width).transpose(2, 0, 1, 3)

    return (
        whole(block_out),
        whole(grad_tokens),
        grad_gain_attn.reshape(width),
        grad_qkv,
        grad_out,
        grad_gain_mlp.reshape(width),
        grad_up,
        grad_down,
    )


def solution(mesh):
    placed = (
        P(None, "lat", "lon", None),
        P("lat", "lon"),
        P(),
        P(),
        P(),
        P(),
        P(),
        P(),
        P(),
        P(),
        P(None, "lat", "lon", None),
    )
    return jax.shard_map(
        on_device,
        mesh=mesh,
        in_specs=placed,
        out_specs=(
            P(None, "lat", "lon", None),
            P(None, "lat", "lon", None),
            P(),
            P(),
            P(),
            P(),
            P(),
            P(),
        ),
        check_vma=False,
    )
```
